32 devices in a mesh: tok: 8 (over z, y), mp: 4 (over x, core).
Axes of the slice: x: 2, y: 2, z: 4, core: 2. Of those that a mesh axis runs over, the one named last changes fastest.
Arguments:
- inputs: bfloat16 [8192, 2560], P(('tok', 'mp')), may hold values from -40 to 40
- grad_output: bfloat16 [8192, 2560], P(('tok', 'mp')), may hold values from -6 to 6
- segments: int32 [8192], replicated, may hold values from 0 to 4, as said below
- attention_gain: bfloat16 [2560], P('tok'), may hold values from 0.25 to 1.75
- query_weight: bfloat16 [2560, 2560], P('tok', 'mp'), may hold values from -0.125 to 0.125
- key_matrix: bfloat16 [2560, 640], P('tok', 'mp'), may hold values from -0.15625 to 0.15625
- value_matrix: bfloat16 [2560, 640], P('tok', 'mp'), may hold values from -0.125 to 0.125
- output_weight: bfloat16 [2560, 2560], P('mp', 'tok'), may hold values from -1 to 1
- feedforward_gain: bfloat16 [2560], P('tok'), may hold values from 0.25 to 1.75
- gate_weight: bfloat16 [2560, 7168], P('tok', 'mp'), may hold values from -0.125 to 0.125
- up_weight: bfloat16 [2560, 7168], P('tok', 'mp'), may hold values from -0.125 to 0.125
- down_weight: bfloat16 [7168, 2560], P('mp', 'tok'), may hold values from -0.09375 to 0.09375
Outputs:
- layer_output: bfloat16 [8192, 2560], P(('tok', 'mp'))
- input_gradient: float32 [8192, 2560], P(('tok', 'mp'))
- attention_gain_gradient: float32 [2560], P('tok')
- query_weight_gradient: float32 [2560, 2560], P('tok', 'mp')
- key_weight_gradient: float32 [2560, 640], P('tok', 'mp')
- value_weight_gradient: float32 [2560, 640], P('tok', 'mp')
- output_weight_gradient: float32 [2560, 2560], P('mp', 'tok')
- feedforward_gain_gradient: float32 [2560], P('tok')
- gate_weight_gradient: float32 [2560, 7168], P('tok', 'mp')
- up_weight_gradient: float32 [2560, 7168], P('tok', 'mp')
- down_weight_gradient: float32 [7168, 2560], P('mp', 'tok')
The draws below stay inside these ranges and needn't reach their ends.
Inputs may be any that keep to these rules, and one draw needn't show every extreme that they name: `segments`: document numbers never fall along the tokens and start at 0; document 2 begins within the first 512 tokens and ends within the last 512 tokens; the other documents lie in those ends.
All inputs are finite; a program needn't handle non-finite values.
Results may differ from the reference program's by a relative error of at most 0.025.
Values may be sent and summed in bfloat16 or wider, within the bound.
A program may use at most 256 MiB of HBM per device.

```python
import jax
import jax.numpy as jnp
from jax import lax

MODEL_WIDTH = 2560
QUERY_HEADS = 32
KEY_VALUE_HEADS = 8
HEAD_SIZE = 80
FF = 7168
WINDOW_LENGTH = 512
TOK_DEV = 1024
TOKENS = 8192


def draw_inputs(key, part):
    key = jax.random.fold_in(key, 11)
    key_states = jax.random.split(key, 3)
    row_scale = jnp.exp(jax.random.uniform(key_states[1], (TOKENS, 1), jnp.float32, -1.15, 1.15))
    column_scale = jnp.exp(jax.random.uniform(key_states[2], (1, MODEL_WIDTH), jnp.float32, -1.15, 1.15))
    base = jax.random.truncated_normal(key_states[0], -4.0, 4.0, (TOKENS, MODEL_WIDTH), jnp.float32)
    value_states = base * row_scale * column_scale
    return value_states.astype(jnp.bfloat16)


def draw_segments(key, part):
    key = jax.random.fold_in(key, 5)
    key_states = jax.random.split(key, 4)
    begin = jax.random.randint(key_states[0], (), 2, TOK_DEV // 2)
    first = jax.random.randint(key_states[1], (), 1, begin)
    finish = TOKENS - jax.random.randint(key_states[2], (), 2, TOK_DEV // 2)
    last = finish + jax.random.randint(key_states[3], (), 1, TOKENS - finish)
    places = jnp.arange(TOKENS, dtype=jnp.int32)
    ids = (places >= first).astype(jnp.int32) + (places >= begin).astype(jnp.int32)
    ids = ids + (places >= finish).astype(jnp.int32) + (places >= last).astype(jnp.int32)
    return ids


def block_scale(key, shape, shards, least, high):
    level = 1.0
    for axis_at, parts in shards:
        draws = jax.random.uniform(jax.random.fold_in(jax.random.fold_in(key, 6), axis_at), (parts,), jnp.float32, least / len(shards), high / len(shards))
        level = level * jnp.repeat(jnp.exp(draws), shape[axis_at] // parts).reshape((-1,) + (1,) * (len(shape) - 1 - axis_at))
    return level


def normal_values(own_key, extent, scale, limit, cuts=(), kind=jnp.bfloat16):
    level = block_scale(own_key, extent, cuts, -0.22, 0.18) if cuts else 1.0
    drawn = jax.random.normal(own_key, extent, jnp.float32) * scale * level
    return jnp.minimum(jnp.maximum(drawn, -limit), limit).astype(kind)


def setup_inputs(seed: int = 0) -> dict:
    keys = jax.random.split(jax.random.key(seed), 13)
    inputs = draw_inputs(jax.random.fold_in(keys[12], 71), 0)
    grad_output = normal_values(keys[1], (TOKENS, MODEL_WIDTH), 1.0, 6.0, ((0, 32),))
    segments = draw_segments(jax.random.fold_in(keys[12], 71), 0)
    attention_gain = jnp.clip(1.0 + 0.15 * jax.random.normal(keys[3], (MODEL_WIDTH,), jnp.float32), 0.25, 1.75).astype(jnp.bfloat16)
    query_weight = normal_values(keys[4], (MODEL_WIDTH, QUERY_HEADS * HEAD_SIZE), MODEL_WIDTH ** -0.5, 0.125, ((0, 8), (1, 4)))
    key_matrix = normal_values(keys[5], (MODEL_WIDTH, KEY_VALUE_HEADS * HEAD_SIZE), (MODEL_WIDTH // 2) ** -0.5, 0.15625, ((0, 8), (1, 4)))
    value_matrix = normal_values(keys[6], (MODEL_WIDTH, KEY_VALUE_HEADS * HEAD_SIZE), MODEL_WIDTH ** -0.5, 0.125, ((0, 8), (1, 4)))
    output_weight = normal_values(keys[7], (QUERY_HEADS * HEAD_SIZE, MODEL_WIDTH), (QUERY_HEADS * HEAD_SIZE * 8 // WINDOW_LENGTH) ** -0.5, 1.0, ((0, 4), (1, 8)))
    feedforward_gain = jnp.clip(1.0 + 0.15 * jax.random.normal(keys[8], (MODEL_WIDTH,), jnp.float32), 0.25, 1.75).astype(jnp.bfloat16)
    gate_weight = normal_values(keys[9], (MODEL_WIDTH, FF), MODEL_WIDTH ** -0.5, 0.125, ((0, 8), (1, 4)))
    up_weight = normal_values(keys[10], (MODEL_WIDTH, FF), MODEL_WIDTH ** -0.5, 0.125, ((0, 8), (1, 4)))
    down_weight = normal_values(keys[11], (FF, MODEL_WIDTH), (FF // 2) ** -0.5, 0.09375, ((0, 4), (1, 8)))
    return {"inputs": inputs, "grad_output": grad_output, "segments": segments, "attention_gain": attention_gain, "query_weight": query_weight, "key_matrix": key_matrix, "value_matrix": value_matrix, "output_weight": output_weight, "feedforward_gain": feedforward_gain, "gate_weight": gate_weight, "up_weight": up_weight, "down_weight": down_weight}


EPS = 1e-05
THETA = 1000000.0
FLOOR = -1e+30
HIGH_PRECISION = lax.Precision.HIGHEST

@jax.custom_vjp
def lower_bound(v):
    return lax.optimization_barrier(v.astype(jnp.bfloat16)).astype(jnp.float32)

@jax.custom_vjp
def lower_bound_backward(v):
    return v

def low_keep(v):
    return (lower_bound(v), None)

def low_pass(kept, grad):
    return (grad,)

def back_keep(v):
    return (v, None)

def back_low(kept, grad):
    return (lower_bound(grad),)
lower_bound.defvjp(low_keep, low_pass)
lower_bound_backward.defvjp(back_keep, back_low)

def rope_tables(count, first, width):
    places = (first + jnp.arange(count, dtype=jnp.int32)).astype(jnp.float32)
    freqs = THETA ** (-(jnp.arange(width // 2, dtype=jnp.int32).astype(jnp.float32) * 2.0 / width))
    angles = places[:, None] * freqs[None, :]
    angles = jnp.concatenate([angles, angles], axis=1)
    return (jnp.cos(angles), jnp.sin(angles))

def turn(value_states, cosine, sine):
    half = value_states.shape[-1] // 2
    swapped = jnp.concatenate([-value_states[..., half:], value_states[..., :half]], axis=-1)
    return value_states * cosine[:, None, :] + swapped * sine[:, None, :]

def normalize(value_states, gain):
    inverse = lax.rsqrt(lax.optimization_barrier(jnp.mean(value_states * value_states, axis=-1, keepdims=True)) + EPS)
    return value_states * inverse * gain

def attention(query_states, key_states, value_states, segments):
    total_length = query_states.shape[0]
    block_rows = min(TOK_DEV, 512)
    head_group = QUERY_HEADS // KEY_VALUE_HEADS
    scale = HEAD_SIZE ** (-0.5)
    padded_keys = jnp.concatenate([jnp.zeros((WINDOW_LENGTH, KEY_VALUE_HEADS, HEAD_SIZE), jnp.float32), key_states], 0)
    padded_values = jnp.concatenate([jnp.zeros((WINDOW_LENGTH, KEY_VALUE_HEADS, HEAD_SIZE), jnp.float32), value_states], 0)
    ids_pad = jnp.concatenate([jnp.full((WINDOW_LENGTH,), -1, jnp.int32), segments.astype(jnp.int32)])

    def one_block(start_index):
        query_tile_rows = lax.dynamic_slice_in_dim(query_states, start_index, block_rows, 0).reshape(block_rows, KEY_VALUE_HEADS, head_group, HEAD_SIZE)
        key_block = lax.dynamic_slice_in_dim(padded_keys, start_index, block_rows + WINDOW_LENGTH, 0)
        value_block = lax.dynamic_slice_in_dim(padded_values, start_index, block_rows + WINDOW_LENGTH, 0)
        key_ids = lax.dynamic_slice_in_dim(ids_pad, start_index, block_rows + WINDOW_LENGTH, 0)
        query_ids = lax.dynamic_slice_in_dim(ids_pad, start_index + WINDOW_LENGTH, block_rows, 0)
        scores = lower_bound_backward(jnp.einsum('qgrd,kgd->grqk', query_tile_rows, key_block, precision=HIGH_PRECISION) * scale)
        distance = jnp.arange(block_rows)[:, None] + WINDOW_LENGTH - jnp.arange(block_rows + WINDOW_LENGTH)[None, :]
        allowed = (distance >= 0) & (distance < WINDOW_LENGTH) & (query_ids[:, None] == key_ids[None, :])
        scores = jnp.where(allowed, scores, FLOOR)
        peak = lax.optimization_barrier(jnp.max(scores, axis=-1, keepdims=True))
        expos = jnp.exp(scores - peak)
        probs = lower_bound(expos / lax.optimization_barrier(jnp.sum(expos, axis=-1, keepdims=True)))
        result = jnp.einsum('grqk,kgd->qgrd', probs, value_block, precision=HIGH_PRECISION)
        return result.reshape(block_rows, QUERY_HEADS * HEAD_SIZE)
    starts = jnp.arange(total_length // block_rows, dtype=jnp.int32) * block_rows
    return lax.map(jax.checkpoint(one_block), starts).reshape(total_length, QUERY_HEADS * HEAD_SIZE)

def layer(inwide, attention_gain, query_weight, key_matrix, value_matrix, output_weight, feedforward_gain, gate_weight, up_weight, down_weight, segments):
    total_length = inwide.shape[0]
    normalized_input = lower_bound(normalize(inwide, attention_gain))
    cosine, sine = rope_tables(total_length, 0, HEAD_SIZE)
    query_lin = lower_bound_backward(jnp.dot(normalized_input, query_weight, precision=HIGH_PRECISION)).reshape(total_length, QUERY_HEADS, HEAD_SIZE)
    key_linear = lower_bound_backward(jnp.dot(normalized_input, key_matrix, precision=HIGH_PRECISION)).reshape(total_length, KEY_VALUE_HEADS, HEAD_SIZE)
    value_states = lower_bound_backward(lower_bound(jnp.dot(normalized_input, value_matrix, precision=HIGH_PRECISION))).reshape(total_length, KEY_VALUE_HEADS, HEAD_SIZE)
    query_states = lower_bound(turn(query_lin, cosine, sine))
    key_states = lower_bound(turn(key_linear, cosine, sine))
    attended = lower_bound_backward(lower_bound(attention(query_states, key_states, value_states, segments)))
    residual = inwide + lower_bound_backward(jnp.dot(attended, output_weight, precision=HIGH_PRECISION))

    def feed(rows_block):
        normed_two = lower_bound(normalize(rows_block, feedforward_gain))
        gate = lower_bound_backward(jnp.dot(normed_two, gate_weight, precision=HIGH_PRECISION))
        up = lower_bound_backward(jnp.dot(normed_two, up_weight, precision=HIGH_PRECISION))
        mixed = lower_bound(jax.nn.silu(gate) * up)
        return rows_block + lower_bound_backward(jnp.dot(mixed, down_weight, precision=HIGH_PRECISION))
    blocks = residual.reshape(total_length // TOK_DEV, TOK_DEV, MODEL_WIDTH)
    return lax.map(jax.checkpoint(feed), blocks).reshape(total_length, MODEL_WIDTH)

def reference(inputs, grad_output, segments, attention_gain, query_weight, key_matrix, value_matrix, output_weight, feedforward_gain, gate_weight, up_weight, down_weight):
    params = [p.astype(jnp.float32) for p in (attention_gain, query_weight, key_matrix, value_matrix, output_weight, feedforward_gain, gate_weight, up_weight, down_weight)]

    def whole(inwide, *weights):
        return layer(inwide, *weights, segments)
    result, pull = jax.vjp(whole, inputs.astype(jnp.float32), *params)
    grads = pull(grad_output.astype(jnp.float32))
    return (result.astype(jnp.bfloat16), grads[0], grads[1], grads[2], grads[3], grads[4], grads[5], grads[6], grads[7], grads[8], grads[9])
```

```python
import functools

import jax
import jax.numpy as jnp
from jax import lax
from jax.experimental import pallas as pl
from jax.experimental.pallas import tpu as pltpu
from jax.sharding import PartitionSpec as P

HEAD_SIZE = 80
WINDOW_LENGTH = 512
EPS = 1e-05
THETA = 1000000.0
FLOOR = -1e30
AXES = ("tok", "mp")
FF_CHUNKS = (512, 384)


class Grid:
    def __init__(self):
        self.nz = lax.axis_size("tok") // 2
        tok = lax.axis_index("tok")
        mp = lax.axis_index("mp")
        self.z, self.y = tok // 2, tok % 2
        self.x, self.c = mp // 2, mp % 2
        self.me = self.y * 4 + self.x * 2 + self.c

    def pairs(self, move):
        out = []
        for z in range(self.nz):
            for g in range(8):
                target = move(z, g)
                if target is not None:
                    out.append((z * 8 + g, target[0] * 8 + target[1]))
        return out

    def swap(self, value, bit):
        return lax.ppermute(value, AXES, self.pairs(lambda z, g: (z, g ^ bit)))

    def ring(self, value):
        return lax.ppermute(value, AXES, self.pairs(lambda z, g: ((z + 1) % self.nz, g)))

    def step(self, value, d):
        def move(z, g):
            return (z + d, g) if 0 <= z + d < self.nz else None

        return lax.ppermute(value, AXES, self.pairs(move))


Y, X, C = 4, 2, 1


def rotated(grid, value, back=False):
    width = value.shape[-1] // grid.nz
    parts = []
    for s in range(grid.nz):
        block = lax.rem(grid.z - s + grid.nz, grid.nz)
        parts.append(lax.dynamic_slice_in_dim(value, block * width, width, value.ndim - 1))
    return jnp.concatenate(parts, -1)


def natural(grid, value):
    blocks = value.reshape((8, value.shape[0] // 8) + value.shape[1:])
    parts = [lax.dynamic_index_in_dim(blocks, grid.me ^ b, 0, False) for b in range(8)]
    return jnp.concatenate(parts, 0)


def gather_tokens(grid, block):
    half = block.shape[0] // 2
    bx = grid.swap(block, X)
    by = grid.swap(block, Y)
    bc = grid.swap(block, C)
    top = grid.swap(by[:half], X)
    bottom = grid.swap(bx[half:], Y)
    both = jnp.concatenate([bx, by], 0)
    cboth = grid.swap(both, C)
    bxy = jnp.concatenate([top, bottom], 0)
    bxyc = grid.swap(bxy, C)
    n = block.shape[0]
    return jnp.concatenate([block, bc, bx, cboth[:n], by, cboth[n:], bxy, bxyc], 0)


def scatter_tokens(grid, partial):
    n = partial.shape[0] // 8
    half = n // 2
    p = partial.reshape(4, 2, n, partial.shape[1])
    got = grid.swap(p[:, 1], C)
    q = (p[:, 0].astype(jnp.float32) + got.astype(jnp.float32)).astype(jnp.bfloat16)
    top, bottom = q[:, :half], q[:, half:]
    gx = grid.swap(jnp.stack([top[1], top[3]]), X)
    gy = grid.swap(jnp.stack([bottom[2], bottom[3]]), Y)
    tx = (top[2].astype(jnp.float32) + gx[1].astype(jnp.float32)).astype(jnp.bfloat16)
    by = (bottom[1].astype(jnp.float32) + gy[1].astype(jnp.float32)).astype(jnp.bfloat16)
    gt = grid.swap(tx, Y)
    gb = grid.swap(by, X)
    top = top[0].astype(jnp.float32) + gx[0].astype(jnp.float32) + gt.astype(jnp.float32)
    bottom = bottom[0].astype(jnp.float32) + gy[0].astype(jnp.float32) + gb.astype(jnp.float32)
    return jnp.concatenate([top, bottom], 0)


def halves(value):
    return value.reshape(value.shape[0], 2, value.shape[1] // 2)


def slot_zero(grid, pieces):
    packed = jnp.concatenate(pieces, -1)
    mine = lax.dynamic_index_in_dim(packed, grid.y, 1, False)
    other = lax.dynamic_index_in_dim(packed, 1 - grid.y, 1, False)
    got = grid.swap(other, Y)
    first = jnp.where(grid.y == 0, mine, got)
    second = jnp.where(grid.y == 0, got, mine)
    return jnp.concatenate([first, second], 0)


def gather_weight(grid, slot):
    slots = [slot]
    for _ in range(grid.nz - 1):
        slots.append(grid.ring(slots[-1]))
    return jnp.concatenate(slots, 0)


def scatter_weight(grid, partial):
    rows = partial.shape[0] // grid.nz
    p = partial.reshape(grid.nz, rows, partial.shape[1])
    acc = p[1]
    for s in range(2, grid.nz + 1):
        got = grid.ring(acc)
        acc = (got.astype(jnp.float32) + p[s % grid.nz].astype(jnp.float32)).astype(jnp.bfloat16)
    both = acc.reshape(2, rows // 2, acc.shape[1])
    mine = lax.dynamic_index_in_dim(both, grid.y, 0, False)
    other = lax.dynamic_index_in_dim(both, 1 - grid.y, 0, False)
    got = grid.swap(other, Y)
    first = jnp.where(grid.y == 0, mine, got)
    second = jnp.where(grid.y == 0, got, mine)
    return jnp.stack([first, second], 1).astype(jnp.float32)


LANES = 128
SCALE = HEAD_SIZE ** (-0.5)
LOG2E = 1.4426950408889634
MIB = 1024 * 1024
BF16 = jnp.bfloat16
F32 = jnp.float32
HBM = pl.BlockSpec(memory_space=pl.ANY)
WHOLE = pl.BlockSpec(memory_space=pltpu.VMEM)
MESH = pl.DeviceIdType.MESH


def light(**kwargs):
    return dict(
        cost_estimate=pl.CostEstimate(flops=1000000, bytes_accessed=100000, transcendentals=0),
        **kwargs,
    )


def params(mib, **kwargs):
    return pltpu.CompilerParams(vmem_limit_bytes=mib * MIB, **kwargs)


def rope_tables(count, first, width):
    half = width // 2
    places = (first + jnp.arange(count, dtype=jnp.int32)).astype(F32)
    freqs = THETA ** (-(jnp.arange(half, dtype=jnp.int32).astype(F32) * 2.0 / width))
    angles = places[:, None] * freqs[None, :]
    cosine, sine = jnp.cos(angles), jnp.sin(angles)
    blank = jnp.zeros((count, LANES // 2 - half), F32)
    return (
        jnp.concatenate([cosine, blank, cosine, blank], 1),
        jnp.concatenate([-sine, blank, sine, blank], 1),
    )


def spread_matrix(turned, plain):
    half = HEAD_SIZE // 2
    f = jnp.arange((turned + plain) * HEAD_SIZE, dtype=jnp.int32)
    head, place = f // HEAD_SIZE, f % HEAD_SIZE
    gap = jnp.where((head < turned) & (place >= half), LANES // 2 - half, 0)
    target = head * LANES + place + gap
    lanes = jnp.arange((turned + plain) * LANES, dtype=jnp.int32)
    return (target[:, None] == lanes[None, :]).astype(BF16)


def nt(left, right):
    return lax.dot_general(left, right, (((1,), (1,)), ((), ())), preferred_element_type=F32)


def nn(left, right):
    return lax.dot_general(left, right, (((1,), (0,)), ((), ())), preferred_element_type=F32)


def qkv_kernel(me_ref, a_ref, w_ref, cos_ref, sin_ref, q_ref, k_ref, v_ref):
    acc = nn(a_ref[...], w_ref[...])
    cosine, sine = cos_ref[...], sin_ref[...]
    heads = q_ref.shape[1] // LANES
    for h in range(heads + 1):
        u = acc[:, h * LANES : (h + 1) * LANES]
        turned = (u * cosine + pltpu.roll(u, LANES // 2, 1) * sine).astype(BF16)
        if h < heads:
            q_ref[:, h * LANES : (h + 1) * LANES] = turned
        else:
            k_ref[...] = turned
    v_ref[...] = acc[:, (heads + 1) * LANES :].astype(BF16)


def project_qkv(me, a1, w_pad, cosine, sine):
    length, model = a1.shape
    rows = length // 8
    wide = w_pad.shape[1] - 2 * LANES
    own = lambda b, me_ref: (b, 0)
    return pl.pallas_call(
        qkv_kernel,
        grid_spec=pltpu.PrefetchScalarGridSpec(
            num_scalar_prefetch=1,
            grid=(8,),
            in_specs=[
                pl.BlockSpec((rows, model), lambda b, me_ref: (b ^ me_ref[0], 0)),
                pl.BlockSpec(w_pad.shape, lambda b, me_ref: (0, 0)),
                pl.BlockSpec((rows, LANES), own),
                pl.BlockSpec((rows, LANES), own),
            ],
            out_specs=[
                pl.BlockSpec((rows, wide), own),
                pl.BlockSpec((rows, LANES), own),
                pl.BlockSpec((rows, LANES), own),
            ],
        ),
        out_shape=[
            jax.ShapeDtypeStruct((length, wide), BF16),
            jax.ShapeDtypeStruct((length, LANES), BF16),
            jax.ShapeDtypeStruct((length, LANES), BF16),
        ],
        compiler_params=params(40),
        name="project_qkv",
        **light(),
    )(me, a1, w_pad, cosine, sine)


def mask_bias(kid, qid, keys, rows):
    kk = lax.broadcasted_iota(jnp.int32, (keys, rows), 0)
    qq = lax.broadcasted_iota(jnp.int32, (keys, rows), 1)
    d = qq + WINDOW_LENGTH - kk
    allowed = (d >= 0) & (d < WINDOW_LENGTH) & (kid == qid)
    return jnp.where(allowed, 0.0, FLOOR)


def attend_kernel(me_ref, q_ref, k_ref, v_ref, kid_ref, qid_ref, o_ref, lse_ref):
    rows = q_ref.shape[0]
    keys = rows + WINDOW_LENGTH
    start = pl.multiple_of(pl.program_id(0) * rows, rows)
    span = pl.ds(start, keys)
    kb = k_ref[span, :]
    vt = v_ref[span, :].T
    bias = mask_bias(kid_ref[span, :], qid_ref[...], keys, rows)
    for h in range(q_ref.shape[1] // LANES):
        lanes = slice(h * LANES, (h + 1) * LANES)
        s = nt(kb, q_ref[:, lanes]) * (SCALE * LOG2E) + bias
        peak = jnp.max(s, axis=0, keepdims=True)
        p = jnp.exp2(s - peak)
        total = jnp.sum(p, axis=0, keepdims=True)
        ot = nn(vt, p.astype(BF16)) / total
        o_ref[:, lanes] = ot.T.astype(BF16)
        lse_ref[0, h : h + 1, :] = peak + jnp.log2(total)


def attend(me, q, k_all, v_all, kid, qid):
    length, wide = q.shape
    rows = length // 8
    heads = wide // LANES
    own = lambda b, me_ref: (b, 0)
    full = lambda b, me_ref: (0, 0)
    return pl.pallas_call(
        attend_kernel,
        grid_spec=pltpu.PrefetchScalarGridSpec(
            num_scalar_prefetch=1,
            grid=(8,),
            in_specs=[
                pl.BlockSpec((rows, wide), own),
                pl.BlockSpec(k_all.shape, full),
                pl.BlockSpec(v_all.shape, full),
                pl.BlockSpec(kid.shape, full),
                pl.BlockSpec((1, rows), lambda b, me_ref: (0, b)),
            ],
            out_specs=[
                pl.BlockSpec((rows, wide), lambda b, me_ref: (b ^ me_ref[0], 0)),
                pl.BlockSpec((1, heads, rows), lambda b, me_ref: (b, 0, 0)),
            ],
        ),
        out_shape=[
            jax.ShapeDtypeStruct((length, wide), BF16),
            jax.ShapeDtypeStruct((8, heads, rows), F32),
        ],
        compiler_params=params(40),
        name="attend",
        **light(),
    )(me, q, k_all, v_all, kid, qid)


def attend_back_kernel(
    me_ref, q_ref, do_ref, k_ref, v_ref, kid_ref, qid_ref, lse_ref, cos_ref, sin_ref,
    dq_ref, dk_ref, dv_ref,
):
    rows = q_ref.shape[0]
    keys = rows + WINDOW_LENGTH
    start = pl.multiple_of(pl.program_id(0) * rows, rows)
    span = pl.ds(start, keys)

    @pl.when(pl.program_id(0) == 0)
    def _():
        dk_ref[...] = jnp.zeros_like(dk_ref)
        dv_ref[...] = jnp.zeros_like(dv_ref)

    kb = k_ref[span, :]
    vb = v_ref[span, :]
    kt = kb.T
    bias = mask_bias(kid_ref[span, :], qid_ref[...], keys, rows)
    cosine, sine = cos_ref[...], sin_ref[...]
    dk = None
    for h in range(q_ref.shape[1] // LANES):
        lanes = slice(h * LANES, (h + 1) * LANES)
        qh = q_ref[:, lanes]
        doh = do_ref[:, lanes]
        p = jnp.exp2(nt(kb, qh) * (SCALE * LOG2E) + (bias - lse_ref[0, h : h + 1, :]))
        t = p * nt(vb, doh)
        inner = jnp.sum(t, axis=0, keepdims=True)
        ds = (t - p * inner).astype(BF16)
        dq = nn(kt, ds).T * SCALE
        dq_ref[:, lanes] = (dq * cosine - pltpu.roll(dq, LANES // 2, 1) * sine).astype(BF16)
        dk_h = nn(ds, qh)
        dv_h = nn(p.astype(BF16), doh)
        dk = dk_h if dk is None else dk + dk_h
        dv = dv_h if h == 0 else dv + dv_h
    dk_ref[span, :] += dk
    dv_ref[span, :] += dv


def attend_back(me, q, do, k_all, v_all, kid, qid, lse, cosine, sine):
    length, wide = q.shape
    rows = length // 8
    heads = wide // LANES
    own = lambda b, me_ref: (b, 0)
    mixed = lambda b, me_ref: (b ^ me_ref[0], 0)
    full = lambda b, me_ref: (0, 0)
    return pl.pallas_call(
        attend_back_kernel,
        grid_spec=pltpu.PrefetchScalarGridSpec(
            num_scalar_prefetch=1,
            grid=(8,),
            in_specs=[
                pl.BlockSpec((rows, wide), own),
                pl.BlockSpec((rows, wide), mixed),
                pl.BlockSpec(k_all.shape, full),
                pl.BlockSpec(v_all.shape, full),
                pl.BlockSpec(kid.shape, full),
                pl.BlockSpec((1, rows), lambda b, me_ref: (0, b)),
                pl.BlockSpec((1, heads, rows), lambda b, me_ref: (b, 0, 0)),
                pl.BlockSpec((rows, LANES), own),
                pl.BlockSpec((rows, LANES), own),
            ],
            out_specs=[
                pl.BlockSpec((rows, wide), mixed),
                pl.BlockSpec(k_all.shape, full),
                pl.BlockSpec(k_all.shape, full),
            ],
        ),
        out_shape=[
            jax.ShapeDtypeStruct((length, wide), BF16),
            jax.ShapeDtypeStruct(k_all.shape, F32),
            jax.ShapeDtypeStruct(k_all.shape, F32),
        ],
        compiler_params=params(40),
        name="attend_back",
        **light(),
    )(me, q, do, k_all, v_all, kid, qid, lse, cosine, sine)


def hidden_kernel(a_ref, d_ref, w_ref, m_ref, g_ref):
    n = m_ref.shape[1]
    gate = nn(a_ref[...], w_ref[:, :n])
    up = nn(a_ref[...], w_ref[:, n : 2 * n])
    dmixed = nn(d_ref[...], w_ref[:, 2 * n :])
    sigma = jax.nn.sigmoid(gate)
    silu = gate * sigma
    m_ref[...] = (silu * up).astype(BF16)
    g_ref[:, n:] = (dmixed * silu).astype(BF16)
    g_ref[:, :n] = (dmixed * up * sigma * (1.0 + gate * (1.0 - sigma))).astype(BF16)


def hidden_units(a2, dout, w):
    length, model = a2.shape
    n = w.shape[1] // 3
    rows = length // 4
    block = pl.BlockSpec((rows, model), lambda b: (b, 0))
    return pl.pallas_call(
        hidden_kernel,
        grid=(length // rows,),
        in_specs=[block, block, pl.BlockSpec(w.shape, lambda b: (0, 0))],
        out_specs=[
            pl.BlockSpec((rows, n), lambda b: (b, 0)),
            pl.BlockSpec((rows, 2 * n), lambda b: (b, 0)),
        ],
        out_shape=[
            jax.ShapeDtypeStruct((length, n), BF16),
            jax.ShapeDtypeStruct((length, 2 * n), BF16),
        ],
        compiler_params=params(56),
        name="hidden_units",
        **light(),
    )(a2, dout, w)


def peers():
    tok, mp = lax.axis_index("tok"), lax.axis_index("mp")
    tok_other = tok + 1 - 2 * (tok % 2)
    mp_x = lax.rem(mp + 2, 4)
    mp_c = mp + 1 - 2 * (mp % 2)
    return (tok, mp_x), (tok_other, mp), (tok, mp_c)


class Wires:
    def __init__(self, send, recv):
        self.send, self.recv, self.count = send, recv, 0
        self.copies = []
        self.x, self.y, self.c = peers()

    def greet(self):
        barrier = pltpu.get_barrier_semaphore()
        for peer in (self.x, self.y, self.c):
            pl.semaphore_signal(barrier, inc=1, device_id=peer, device_id_type=MESH)
        pl.semaphore_wait(barrier, 3)

    def start(self, source, target, peer):
        i = self.count
        self.count += 1
        copy = pltpu.make_async_remote_copy(
            src_ref=source,
            dst_ref=target,
            send_sem=self.send.at[i],
            recv_sem=self.recv.at[i],
            device_id=peer,
            device_id_type=MESH,
        )
        copy.start()
        self.copies.append(copy)
        return copy

    def finish(self):
        for copy in self.copies:
            copy.wait_send()


RS_COPIES, AG_COPIES = 10, 13


def reduce_phase(wires, pairs, cs, cr, q, xr, yr, tr, br, emit):
    n = q.shape[1]
    half = n // 2
    top, bottom = pl.ds(0, half), pl.ds(half, half)
    model = q.shape[2]
    tile = 512 if model % 512 == 0 else model

    def product(place, target):
        @pl.loop(0, model // tile)
        def _(t):
            cols = pl.ds(pl.multiple_of(t * tile, tile), tile)
            total = None
            for a, w in pairs:
                part = nt(a[place], w[cols, :])
                total = part if total is None else total + part
            target[:, cols] = total.astype(BF16)

    waits = {}
    for j in (3, 1, 2, 0):
        product(2 * j + 1, cs.at[j])
        got = wires.start(cs.at[j], cr.at[j], wires.c)
        product(2 * j, q.at[j])
        got.wait_recv()
        q[j] = (q[j].astype(F32) + cr[j].astype(F32)).astype(BF16)
        if j == 3:
            waits["x1"] = wires.start(q.at[3, top], xr.at[1], wires.x)
            waits["y1"] = wires.start(q.at[3, bottom], yr.at[1], wires.y)
        if j == 1:
            waits["x0"] = wires.start(q.at[1, top], xr.at[0], wires.x)
        if j == 2:
            waits["y0"] = wires.start(q.at[2, bottom], yr.at[0], wires.y)
    waits["x1"].wait_recv()
    q[2, top] = (q[2, top].astype(F32) + xr[1].astype(F32)).astype(BF16)
    waits["t"] = wires.start(q.at[2, top], tr, wires.y)
    waits["y1"].wait_recv()
    q[1, bottom] = (q[1, bottom].astype(F32) + yr[1].astype(F32)).astype(BF16)
    waits["b"] = wires.start(q.at[1, bottom], br, wires.x)
    waits["x0"].wait_recv()
    waits["t"].wait_recv()
    emit(top, q[0, top].astype(F32) + xr[0].astype(F32) + tr[...].astype(F32))
    waits["y0"].wait_recv()
    waits["b"].wait_recv()
    emit(bottom, q[0, bottom].astype(F32) + yr[0].astype(F32) + br[...].astype(F32))


def reduce_scratch(n, model):
    half = n // 2
    return [
        pltpu.VMEM((4, n, model), BF16),
        pltpu.VMEM((4, n, model), BF16),
        pltpu.VMEM((4, n, model), BF16),
        pltpu.VMEM((2, half, model), BF16),
        pltpu.VMEM((2, half, model), BF16),
        pltpu.VMEM((half, model), BF16),
        pltpu.VMEM((half, model), BF16),
    ]


def gather_phase(wires, block, out, local):
    n = block.shape[0]
    half = n // 2
    top, bottom = pl.ds(0, half), pl.ds(half, half)
    mine = pltpu.make_async_copy(block, out.at[0], local)
    mine.start()
    xb = wires.start(block.at[bottom], out.at[2, bottom], wires.x)
    yt = wires.start(block.at[top], out.at[4, top], wires.y)
    c = [wires.start(block, out.at[1], wires.c)]
    xt = wires.start(block.at[top], out.at[2, top], wires.x)
    yb = wires.start(block.at[bottom], out.at[4, bottom], wires.y)
    xb.wait_recv()
    db = wires.start(out.at[2, bottom], out.at[6, bottom], wires.y)
    c.append(wires.start(out.at[2, bottom], out.at[3, bottom], wires.c))
    yt.wait_recv()
    dt = wires.start(out.at[4, top], out.at[6, top], wires.x)
    c.append(wires.start(out.at[4, top], out.at[5, top], wires.c))
    xt.wait_recv()
    c.append(wires.start(out.at[2, top], out.at[3, top], wires.c))
    yb.wait_recv()
    c.append(wires.start(out.at[4, bottom], out.at[5, bottom], wires.c))
    dt.wait_recv()
    c.append(wires.start(out.at[6, top], out.at[7, top], wires.c))
    db.wait_recv()
    c.append(wires.start(out.at[6, bottom], out.at[7, bottom], wires.c))
    for copy in c:
        copy.wait_recv()
    mine.wait()


def gather_kernel(block, out, send, recv, local):
    wires = Wires(send, recv)
    wires.greet()
    gather_phase(wires, block, out, local)
    wires.finish()


def gather_block(block, number):
    n, model = block.shape
    return pl.pallas_call(
        gather_kernel,
        in_specs=[WHOLE],
        out_specs=HBM,
        out_shape=jax.ShapeDtypeStruct((8, n, model), BF16),
        scratch_shapes=[
            pltpu.SemaphoreType.DMA((AG_COPIES,)),
            pltpu.SemaphoreType.DMA((AG_COPIES,)),
            pltpu.SemaphoreType.DMA(()),
        ],
        compiler_params=params(16, collective_id=number, has_side_effects=True),
        name="gather_block",
        **light(),
    )(block).reshape(8 * n, model)


def forward_kernel(
    a_ref, w_ref, x_ref, gain_ref, res_ref, inv_ref, out_ref,
    block, cs, cr, q, xr, yr, tr, br, send, recv, local,
):
    wires = Wires(send, recv)
    wires.greet()

    def emit(rows, total):
        residual = x_ref[rows, :].astype(F32) + total
        inverse = lax.rsqrt(jnp.mean(residual * residual, axis=1, keepdims=True) + EPS)
        res_ref[rows, :] = residual
        inv_ref[rows, :] = inverse
        block[rows, :] = (residual * inverse * gain_ref[...]).astype(BF16)

    reduce_phase(wires, [(a_ref, w_ref)], cs, cr, q, xr, yr, tr, br, emit)
    gather_phase(wires, block, out_ref, local)
    wires.finish()


def project_out(o, w_out, inputs, gain):
    n, model = inputs.shape
    copies = RS_COPIES + AG_COPIES
    residual, inverse, gathered = pl.pallas_call(
        forward_kernel,
        in_specs=[WHOLE] * 4,
        out_specs=[WHOLE, WHOLE, HBM],
        out_shape=[
            jax.ShapeDtypeStruct((n, model), F32),
            jax.ShapeDtypeStruct((n, 1), F32),
            jax.ShapeDtypeStruct((8, n, model), BF16),
        ],
        scratch_shapes=[pltpu.VMEM((n, model), BF16)]
        + reduce_scratch(n, model)
        + [
            pltpu.SemaphoreType.DMA((copies,)),
            pltpu.SemaphoreType.DMA((copies,)),
            pltpu.SemaphoreType.DMA(()),
        ],
        compiler_params=params(52, collective_id=2, has_side_effects=True),
        name="project_out",
        **light(),
    )(o.reshape(8, n, -1), w_out, inputs, gain)
    return residual, inverse, gathered.reshape(8 * n, model)


def middle_kernel(count, *refs):
    pairs = [(refs[2 * i], refs[2 * i + 1]) for i in range(count)]
    (dout_ref, res_ref, inv_ref, gain_ref, dres_ref, out_ref,
     block, cs, cr, q, xr, yr, tr, br, send, recv, local) = refs[2 * count :]
    wires = Wires(send, recv)
    wires.greet()

    def emit(rows, total):
        inverse = inv_ref[rows, :]
        normed = res_ref[rows, :] * inverse
        e = total * gain_ref[...]
        back = inverse * (e - normed * jnp.mean(e * normed, axis=1, keepdims=True))
        dres = dout_ref[rows, :].astype(F32) + back
        dres_ref[rows, :] = dres
        block[rows, :] = dres.astype(BF16)

    reduce_phase(wires, pairs, cs, cr, q, xr, yr, tr, br, emit)
    gather_phase(wires, block, out_ref, local)
    wires.finish()


def feed_back(pairs, dout, residual, inverse, gain):
    n, model = dout.shape
    copies = RS_COPIES + AG_COPIES
    args, specs = [], []
    for a, w in pairs:
        k = a.shape[1]
        args += [a.reshape(8, n, k), w]
        specs += [WHOLE, pl.BlockSpec((model, k), lambda i: (0, 0))]
    specs[0::2] = [pl.BlockSpec((8, n, a.shape[1]), lambda i: (0, 0, 0)) for a, w in pairs]
    flat = pl.BlockSpec((n, model), lambda i: (0, 0))
    thin = pl.BlockSpec((n, 1), lambda i: (0, 0))
    dres, gathered = pl.pallas_call(
        functools.partial(middle_kernel, len(pairs)),
        grid=(1,),
        in_specs=specs + [flat, flat, thin, pl.BlockSpec((1, model), lambda i: (0, 0))],
        out_specs=[flat, HBM],
        out_shape=[
            jax.ShapeDtypeStruct((n, model), F32),
            jax.ShapeDtypeStruct((8, n, model), BF16),
        ],
        scratch_shapes=[pltpu.VMEM((n, model), BF16)]
        + reduce_scratch(n, model)
        + [
            pltpu.SemaphoreType.DMA((copies,)),
            pltpu.SemaphoreType.DMA((copies,)),
            pltpu.SemaphoreType.DMA(()),
        ],
        compiler_params=params(60, collective_id=3, has_side_effects=True),
        name="feed_back",
        **light(),
    )(*args, dout, residual, inverse, gain)
    return dres, gathered.reshape(8 * n, model)


def last_kernel(
    a_ref, w_ref, x_ref, inv_ref, gain_ref, dres_ref, out_ref,
    cs, cr, q, xr, yr, tr, br, send, recv,
):
    wires = Wires(send, recv)
    wires.greet()

    def emit(rows, total):
        inverse = inv_ref[rows, :]
        normed = x_ref[rows, :].astype(F32) * inverse
        e = total * gain_ref[...]
        back = inverse * (e - normed * jnp.mean(e * normed, axis=1, keepdims=True))
        out_ref[rows, :] = dres_ref[rows, :] + back

    reduce_phase(wires, [(a_ref, w_ref)], cs, cr, q, xr, yr, tr, br, emit)
    wires.finish()


def input_back(dqkv, w, inputs, inverse, gain, dres):
    n, model = inputs.shape
    return pl.pallas_call(
        last_kernel,
        in_specs=[WHOLE] * 6,
        out_specs=WHOLE,
        out_shape=jax.ShapeDtypeStruct((n, model), F32),
        scratch_shapes=reduce_scratch(n, model)
        + [
            pltpu.SemaphoreType.DMA((RS_COPIES,)),
            pltpu.SemaphoreType.DMA((RS_COPIES,)),
        ],
        compiler_params=params(52, collective_id=4, has_side_effects=True),
        name="input_back",
        **light(),
    )(dqkv.reshape(8, n, -1), w, inputs, inverse, gain, dres)


def normalize(value_states, gain):
    inverse = lax.rsqrt(jnp.mean(value_states * value_states, axis=-1, keepdims=True) + EPS)
    return (value_states * inverse * gain.astype(jnp.float32), inverse)


def dot(left, right):
    return jnp.dot(left, right, preferred_element_type=jnp.float32)


def outer_product(left, right):
    return lax.dot_general(
        left, right, (((0,), (0,)), ((), ())), preferred_element_type=jnp.float32
    )


def times_transposed(left, right):
    return lax.dot_general(
        left, right, (((1,), (1,)), ((), ())), preferred_element_type=jnp.float32
    )


def body(
    inputs,
    grad_output,
    segments,
    attention_gain,
    query_weight,
    key_matrix,
    value_matrix,
    output_weight,
    feedforward_gain,
    gate_weight,
    up_weight,
    down_weight,
):
    grid = Grid()
    bf16 = jnp.bfloat16
    model = inputs.shape[1]
    length = inputs.shape[0] * 8
    hidden = gate_weight.shape[1] // 2
    qdim = query_weight.shape[1] // 2
    kdim = key_matrix.shape[1] // 2
    cuts = []
    at = 0
    for n in FF_CHUNKS:
        cuts.append((at, at + n))
        at += n

    gains = slot_zero(
        grid,
        [
            jnp.broadcast_to(
                jnp.stack([attention_gain, feedforward_gain], -1)[:, None, :],
                (attention_gain.shape[0], 2, 2),
            )
        ],
    )
    gains = gather_weight(grid, gains)
    gain_one, gain_two = gains[:, 0], gains[:, 1]
    w_attn = gather_weight(
        grid,
        slot_zero(grid, [halves(query_weight), halves(key_matrix), halves(value_matrix)]),
    )
    w_out = gather_weight(grid, slot_zero(grid, [halves(output_weight.T)]))
    gate_h, up_h, down_h = halves(gate_weight), halves(up_weight), halves(down_weight.T)
    w_ff = [
        gather_weight(grid, slot_zero(grid, [v[:, :, a:b] for v in (gate_h, up_h, down_h)]))
        for a, b in cuts
    ]

    me = jnp.reshape(grid.me, (1,)).astype(jnp.int32)
    heads = qdim // HEAD_SIZE
    spread = spread_matrix(heads + kdim // HEAD_SIZE, kdim // HEAD_SIZE)
    spread_out = spread_matrix(0, heads)
    gain_one = gain_one.astype(F32)[None, :]
    gain_two = gain_two.astype(F32)[None, :]
    own = rotated(grid, inputs)
    normed_one, inverse_one = normalize(own.astype(F32), gain_one)
    a1 = gather_block(normed_one.astype(bf16), 0)
    dout = rotated(grid, grad_output)
    dout_all = gather_tokens(grid, dout)
    cosine, sine = rope_tables(length, grid.z * length, HEAD_SIZE)
    padded_ids = jnp.concatenate([jnp.full((WINDOW_LENGTH,), -1, jnp.int32), segments])
    key_ids = lax.dynamic_slice_in_dim(padded_ids, grid.z * length, length + WINDOW_LENGTH, 0)
    kid, qid = key_ids[:, None], key_ids[None, WINDOW_LENGTH:]
    w_pad = dot(w_attn, spread).astype(bf16)
    w_out_pad = dot(w_out, spread_out).astype(bf16)
    q, k, v = project_qkv(me, a1, w_pad, cosine, sine)
    edge = grid.step(
        jnp.concatenate([k[length - WINDOW_LENGTH :], v[length - WINDOW_LENGTH :]], 1), 1
    )
    k_all = jnp.concatenate([edge[:, :LANES], k], 0)
    v_all = jnp.concatenate([edge[:, LANES:], v], 0)
    o, lse = attend(me, q, k_all, v_all, kid, qid)
    residual, inverse_two, a2 = project_out(o, w_out_pad, own, gain_two)

    result = jnp.zeros((length, model), F32)
    ff_grads, back_pairs = [], []
    for (a, b), w in zip(cuts, w_ff):
        n = b - a
        mixed, dgu = hidden_units(a2, dout_all, w)
        back_pairs.append((dgu, w))
        result = result + times_transposed(mixed, w[:, 2 * n :])
        partial = jnp.concatenate(
            [outer_product(a2, dgu), outer_product(dout_all, mixed)], 1
        ).astype(bf16)
        ff_grads.append(scatter_weight(grid, partial))
    dresidual, da_all = feed_back(back_pairs, dout, residual, inverse_two, gain_two)
    result = residual + scatter_tokens(grid, result.astype(bf16))
    layer_output = rotated(grid, result.astype(bf16))

    do = dot(da_all, w_out_pad).astype(bf16)
    dq, dk, dv = attend_back(me, q, do, k_all, v_all, kid, qid, lse, cosine, sine)
    back = grid.step(
        jnp.concatenate([dk[:WINDOW_LENGTH], dv[:WINDOW_LENGTH]], 1).astype(bf16), -1
    ).astype(F32)
    back = jnp.concatenate([jnp.zeros((length - WINDOW_LENGTH, 2 * LANES), F32), back], 0)
    dk = (dk[WINDOW_LENGTH:] + back[:, :LANES]) * SCALE
    dv = dv[WINDOW_LENGTH:] + back[:, LANES:]
    dk = dk * cosine - jnp.roll(dk, LANES // 2, 1) * sine
    dkv = natural(grid, jnp.concatenate([dk, dv], 1).astype(bf16))
    dqkv = jnp.concatenate([dq, dkv], 1)
    attn_grad = scatter_weight(
        grid, outer_product(a1, times_transposed(dqkv, spread).astype(bf16)).astype(bf16)
    )
    input_gradient = rotated(
        grid, input_back(dqkv, w_pad, own, inverse_one, gain_one, dresidual)
    )
    out_grad = scatter_weight(
        grid, times_transposed(outer_product(da_all, o).astype(bf16), spread_out).astype(bf16)
    )

    def whole(part):
        return part.reshape(part.shape[0], -1)

    query_grad = whole(attn_grad[:, :, :qdim])
    key_grad = whole(attn_grad[:, :, qdim : qdim + kdim])
    value_grad = whole(attn_grad[:, :, qdim + kdim :])
    output_grad = whole(out_grad).T
    parts = []
    for k in range(3):
        parts.append(
            whole(
                jnp.concatenate(
                    [g[:, :, k * (b - a) : (k + 1) * (b - a)] for (a, b), g in zip(cuts, ff_grads)],
                    2,
                )
            )
        )
    gate_grad, up_grad, down_grad = parts[0], parts[1], parts[2].T

    def row_sum(*both):
        return sum(
            jnp.sum(w.astype(jnp.float32) * g, axis=1) for w, g in both
        )

    sums = jnp.stack(
        [
            row_sum((query_weight, query_grad), (key_matrix, key_grad), (value_matrix, value_grad)),
            row_sum((gate_weight, gate_grad), (up_weight, up_grad)),
        ]
    )
    sums = sums + grid.swap(sums, C)
    sums = sums + grid.swap(sums, X)
    return (
        layer_output,
        input_gradient,
        sums[0] / attention_gain.astype(jnp.float32),
        query_grad,
        key_grad,
        value_grad,
        output_grad,
        sums[1] / feedforward_gain.astype(jnp.float32),
        gate_grad,
        up_grad,
        down_grad,
    )


def solution(mesh):
    in_specs = (
        P(("tok", "mp"), None),
        P(("tok", "mp"), None),
        P(),
        P("tok"),
        P("tok", "mp"),
        P("tok", "mp"),
        P("tok", "mp"),
        P("mp", "tok"),
        P("tok"),
        P("tok", "mp"),
        P("tok", "mp"),
        P("mp", "tok"),
    )
    out_specs = (
        P(("tok", "mp"), None),
        P(("tok", "mp"), None),
        P("tok"),
        P("tok", "mp"),
        P("tok", "mp"),
        P("tok", "mp"),
        P("mp", "tok"),
        P("tok"),
        P("tok", "mp"),
        P("tok", "mp"),
        P("mp", "tok"),
    )
    return jax.shard_map(body, mesh=mesh, in_specs=in_specs, out_specs=out_specs, check_vma=False)
```

```python
import functools

import jax
import jax.numpy as jnp
from jax import lax
from jax.experimental import pallas as pl
from jax.experimental.pallas import tpu as pltpu
from jax.sharding import PartitionSpec as P

HEAD_SIZE = 80
WINDOW_LENGTH = 512
EPS = 1e-05
THETA = 1000000.0
FLOOR = -1e30
AXES = ("tok", "mp")
FF_CHUNKS = (128, 384, 256, 128)


class Grid:
    def __init__(self):
        self.nz = lax.axis_size("tok") // 2
        tok = lax.axis_index("tok")
        mp = lax.axis_index("mp")
        self.z, self.y = tok // 2, tok % 2
        self.x, self.c = mp // 2, mp % 2
        self.me = self.y * 4 + self.x * 2 + self.c

    def pairs(self, move):
        out = []
        for z in range(self.nz):
            for g in range(8):
                target = move(z, g)
                if target is not None:
                    out.append((z * 8 + g, target[0] * 8 + target[1]))
        return out

    def swap(self, value, bit):
        return lax.ppermute(value, AXES, self.pairs(lambda z, g: (z, g ^ bit)))

    def ring(self, value):
        return lax.ppermute(value, AXES, self.pairs(lambda z, g: ((z + 1) % self.nz, g)))

    def step(self, value, d):
        def move(z, g):
            return (z + d, g) if 0 <= z + d < self.nz else None

        return lax.ppermute(value, AXES, self.pairs(move))


Y, X, C = 4, 2, 1


def rotated(grid, value, back=False):
    width = value.shape[-1] // grid.nz
    parts = []
    for s in range(grid.nz):
        block = lax.rem(grid.z - s + grid.nz, grid.nz)
        parts.append(lax.dynamic_slice_in_dim(value, block * width, width, value.ndim - 1))
    return jnp.concatenate(parts, -1)


LANES = 128
SCALE = HEAD_SIZE ** (-0.5)
LOG2E = 1.4426950408889634
MIB = 1024 * 1024
BF16 = jnp.bfloat16
F32 = jnp.float32
HBM = pl.BlockSpec(memory_space=pl.ANY)
WHOLE = pl.BlockSpec(memory_space=pltpu.VMEM)
MESH = pl.DeviceIdType.MESH


def light(**kwargs):
    return dict(
        cost_estimate=pl.CostEstimate(flops=1000000, bytes_accessed=100000, transcendentals=0),
        **kwargs,
    )


def params(mib, **kwargs):
    return pltpu.CompilerParams(vmem_limit_bytes=mib * MIB, **kwargs)


def rope_tables(count, first, width):
    half = width // 2
    places = (first + jnp.arange(count, dtype=jnp.int32)).astype(F32)
    freqs = THETA ** (-(jnp.arange(half, dtype=jnp.int32).astype(F32) * 2.0 / width))
    angles = places[:, None] * freqs[None, :]
    cosine, sine = jnp.cos(angles), jnp.sin(angles)
    blank = jnp.zeros((count, LANES // 2 - half), F32)
    return (
        jnp.concatenate([cosine, blank, cosine, blank], 1),
        jnp.concatenate([-sine, blank, sine, blank], 1),
    )


def spread_matrix(turned, plain):
    half = HEAD_SIZE // 2
    f = jnp.arange((turned + plain) * HEAD_SIZE, dtype=jnp.int32)
    head, place = f // HEAD_SIZE, f % HEAD_SIZE
    gap = jnp.where((head < turned) & (place >= half), LANES // 2 - half, 0)
    target = head * LANES + place + gap
    lanes = jnp.arange((turned + plain) * LANES, dtype=jnp.int32)
    return (target[:, None] == lanes[None, :]).astype(BF16)


def nt(left, right):
    return lax.dot_general(left, right, (((1,), (1,)), ((), ())), preferred_element_type=F32)


def nn(left, right):
    return lax.dot_general(left, right, (((1,), (0,)), ((), ())), preferred_element_type=F32)


def tn(left, right):
    return lax.dot_general(left, right, (((0,), (0,)), ((), ())), preferred_element_type=F32)


def mask_bias(kid, qid, keys, rows):
    kk = lax.broadcasted_iota(jnp.int32, (keys, rows), 0)
    qq = lax.broadcasted_iota(jnp.int32, (keys, rows), 1)
    d = qq + WINDOW_LENGTH - kk
    allowed = (d >= 0) & (d < WINDOW_LENGTH) & (kid == qid)
    return jnp.where(allowed, 0.0, FLOOR)


def only(condition, act):
    if condition is None:
        act()
    else:
        pl.when(condition)(act)


class Copy:
    def __init__(self, copy, when, got):
        self.copy, self.when, self.got = copy, when, got

    def wait_recv(self):
        only(self.got, self.copy.wait_recv)

    def wait_send(self):
        only(self.when, self.copy.wait_send)


SEMAPHORES = 96


def semaphores():
    return [
        pltpu.SemaphoreType.DMA((SEMAPHORES,)),
        pltpu.SemaphoreType.DMA((SEMAPHORES,)),
        pltpu.SemaphoreType.DMA((SEMAPHORES,)),
    ]


class Wires:
    def __init__(self, send, recv, local):
        self.send, self.recv, self.here = send, recv, local
        self.count = self.local_count = 0
        self.copies = []
        tokens = lax.axis_size("tok")
        tok, mp = lax.axis_index("tok"), lax.axis_index("mp")
        self.nz = tokens // 2
        self.at_z, self.at_y = tok // 2, tok % 2
        self.at_x, self.at_c = mp // 2, mp % 2
        self.x = (tok, lax.rem(mp + 2, 4))
        self.y = (tok + 1 - 2 * self.at_y, mp)
        self.c = (tok, mp + 1 - 2 * self.at_c)
        self.up = (lax.rem(tok + 2, tokens), mp)
        self.down = (lax.rem(tok + tokens - 2, tokens), mp)

    def greet(self):
        barrier = pltpu.get_barrier_semaphore()
        peers = (self.x, self.y, self.c, self.up, self.down)
        for peer in peers:
            pl.semaphore_signal(barrier, inc=1, device_id=peer, device_id_type=MESH)
        pl.semaphore_wait(barrier, len(peers))

    def start(self, source, target, peer, when=None, got=None):
        i = self.count
        self.count += 1
        copy = pltpu.make_async_remote_copy(
            src_ref=source,
            dst_ref=target,
            send_sem=self.send.at[i],
            recv_sem=self.recv.at[i],
            device_id=peer,
            device_id_type=MESH,
        )
        only(when, copy.start)
        made = Copy(copy, when, got)
        self.copies.append(made)
        return made

    def choose(self, sources, target, peer, got):
        i = self.count
        for when, source in sources:
            self.count = i
            made = self.start(source, target, peer, when, got)
        return made

    def local(self, source, target):
        copy = pltpu.make_async_copy(source, target, self.here.at[self.local_count])
        self.local_count += 1
        copy.start()
        return copy

    def natural(self, b):
        spots = ((self.at_y, 4), (self.at_x, 2), (self.at_c, 1))
        return sum((1 - at if b & bit else at) * bit for at, bit in spots)

    def finish(self):
        for copy in self.copies:
            copy.wait_send()


def drain(*parts):
    parts = list(parts)
    while parts:
        parts = [part for part in parts if next(part, None) is not None]


def run(part):
    next(part, None)


def exchange_halves(wires, sources, slot):
    n = slot.shape[0] // 2
    rows = pl.ds(pl.multiple_of(wires.at_y * n, n), n)
    waits = []
    for pick, lo, hi in sources:
        waits.append(wires.start(pick(1 - wires.at_y), slot.at[rows, lo:hi], wires.y).wait_recv)
        waits.append(wires.local(pick(wires.at_y), slot.at[rows, lo:hi]).wait)
    yield 1
    for wait in waits:
        wait()


def along_z(wires, first, slot):
    nz, z = wires.nz, wires.at_z
    get = lambda s: first if s == 0 else slot(s)
    for s in range(1, nz):
        up = wires.start(get(s - 1), slot(s), wires.up, (z >= s - 1) & (z < nz - 1), z >= s)
        down = wires.start(
            get((nz - s + 1) % nz), slot(nz - s), wires.down, (z + s <= nz) & (z >= 1), z + s < nz
        )
        yield 1
        up.wait_recv()
        down.wait_recv()


def add_into(target, source):
    @pl.loop(0, target.shape[0] // 32)
    def _(t):
        part = pl.ds(pl.multiple_of(t * 32, 32), 32)
        target[part, :] = (target[part, :].astype(F32) + source[part, :].astype(F32)).astype(BF16)


def sum_along_z(wires, p, above, below, stage, mine, got):
    nz, z = wires.nz, wires.at_z
    ups, downs = [], []
    for s in range(1, nz):
        if s > 1:
            loads = [wires.local(p(s), stage.at[0]), wires.local(p(nz - s), stage.at[1])]
            yield 1
            ups[-1].wait_recv()
            downs[-1].wait_recv()
            for load in loads:
                load.wait()
            only((z >= 1) & (z < s), lambda s=s: add_into(above.at[s - 2], stage.at[0]))
            only(
                (z + s >= nz) & (z < nz - 1), lambda s=s: add_into(below.at[s - 2], stage.at[1])
            )
        up = [(z == 0, p(s))]
        down = [(z == nz - 1, p(nz - s))]
        if s > 1:
            up.append(((z >= 1) & (z < s) & (z < nz - 1), above.at[s - 2]))
            down.append(((z + s >= nz) & (z < nz - 1) & (z >= 1), below.at[s - 2]))
        ups.append(wires.choose(up, above.at[s - 1], wires.up, (z >= 1) & (z <= s)))
        downs.append(
            wires.choose(down, below.at[s - 1], wires.down, (z + s >= nz - 1) & (z < nz - 1))
        )
    load = wires.local(p(0), stage.at[0])
    yield 1
    ups[-1].wait_recv()
    downs[-1].wait_recv()
    load.wait()
    only(z >= 1, lambda: add_into(stage.at[0], above.at[nz - 2]))
    only(z < nz - 1, lambda: add_into(stage.at[0], below.at[nz - 2]))
    n = mine.shape[0]
    own = pl.ds(pl.multiple_of(wires.at_y * n, n), n)
    other = pl.ds(pl.multiple_of((1 - wires.at_y) * n, n), n)
    sent = wires.start(stage.at[0, other], got, wires.y)
    kept = wires.local(stage.at[0, own], mine)
    yield 1
    sent.wait_recv()
    kept.wait()


def sum_scratch(nz, rows, cols):
    return [
        pltpu.VMEM((nz - 1, rows, cols), BF16),
        pltpu.VMEM((nz - 1, rows, cols), BF16),
        pltpu.VMEM((2, rows, cols), BF16),
    ]


def sum_outputs(rows, cols):
    return [jax.ShapeDtypeStruct((rows // 2, cols), BF16)] * 2


def columns(ref, rows, lo, hi):
    return lambda s: ref.at[pl.ds(s * rows, rows), lo:hi]


def gather_weight_rows(wires, sources, out):
    n = out.shape[0] // wires.nz
    slot = lambda s: out.at[pl.ds(s * n, n)]
    yield from exchange_halves(wires, sources, slot(0))
    yield from along_z(wires, slot(0), slot)


def gather_phase(wires, block, out, long_x=False):
    n = block.shape[0]
    half = n // 2
    top, bottom = pl.ds(0, half), pl.ds(half, half)
    mine = wires.local(block, out.at[0])
    xb = wires.start(block.at[bottom], out.at[2, bottom], wires.x)
    yt = wires.start(block.at[top], out.at[4, top], wires.y)
    c = [wires.start(block, out.at[1], wires.c)]
    xt = wires.start(block.at[top], out.at[2, top], wires.x)
    yb = wires.start(block.at[bottom], out.at[4, bottom], wires.y)
    yield 1
    yt.wait_recv()
    dt = wires.start(out.at[4, top], out.at[6, top], wires.x)
    c.append(wires.start(out.at[4, top], out.at[5, top], wires.c))
    xb.wait_recv()
    if not long_x:
        db = wires.start(out.at[2, bottom], out.at[6, bottom], wires.y)
    c.append(wires.start(out.at[2, bottom], out.at[3, bottom], wires.c))
    yield 1
    yb.wait_recv()
    if long_x:
        db = wires.start(out.at[4, bottom], out.at[6, bottom], wires.x)
    c.append(wires.start(out.at[4, bottom], out.at[5, bottom], wires.c))
    xt.wait_recv()
    c.append(wires.start(out.at[2, top], out.at[3, top], wires.c))
    yield 1
    dt.wait_recv()
    c.append(wires.start(out.at[6, top], out.at[7, top], wires.c))
    db.wait_recv()
    c.append(wires.start(out.at[6, bottom], out.at[7, bottom], wires.c))
    yield 1
    for copy in c:
        copy.wait_recv()
    mine.wait()


def start_kernel(x_ref, pack_ref, x_all, w_all, send, recv, local):
    wires = Wires(send, recv, local)
    wires.greet()
    weights = gather_weight_rows(
        wires, [(lambda y: pack_ref.at[y], 0, pack_ref.shape[2])], w_all
    )
    run(weights)
    tokens = gather_phase(wires, x_ref, x_all)
    run(tokens)
    drain(weights, tokens)
    wires.finish()


def gather_start(own, pack):
    n, model = own.shape
    return pl.pallas_call(
        start_kernel,
        in_specs=[WHOLE, HBM],
        out_specs=[HBM, HBM],
        out_shape=[
            jax.ShapeDtypeStruct((8, n, model), BF16),
            jax.ShapeDtypeStruct((model, pack.shape[2]), BF16),
        ],
        scratch_shapes=semaphores(),
        compiler_params=params(16, collective_id=0, has_side_effects=True),
        name="gather_start",
        **light(),
    )(own, pack)


def feed_sources(gate, up, down, cut, hidden):
    a, b = cut
    n = b - a
    step = LANES

    def pick(ref):
        return lambda y: ref.at[:, pl.ds(pl.multiple_of(y * hidden + a, step), n)]

    return [(pick(ref), k * n, (k + 1) * n) for k, ref in enumerate((gate, up, down))]


def attention_kernel(
    hidden, cuts,
    x_ref, w_ref, spread_ref, squeeze_ref, cos_ref, sin_ref, kid_ref, qid_ref, dout_ref,
    opack_ref, gate_ref, up_ref, down_ref,
    a1_ref, q_ref, k_ref, v_ref, o_ref, lse_ref, dout_all, w_out, w_zero, w_next,
    x_all, w_flat, w_pad, send, recv, local,
):
    wires = Wires(send, recv, local)
    nz, z = wires.nz, wires.at_z
    rows = x_all.shape[1]
    model = x_all.shape[2]
    heads = q_ref.shape[1] // LANES
    keys = rows + WINDOW_LENGTH
    length = 8 * rows
    wires.greet()
    load_w = wires.local(w_ref, w_flat)
    order = (6, 7, 0, 1, 2, 3, 4, 5)
    loads = {}
    for b in order:
        at = wires.natural(b)
        loads[b] = wires.local(x_ref.at[at], x_all.at[at])
    out_weights = gather_weight_rows(
        wires, [(lambda y: opack_ref.at[y], 0, opack_ref.shape[2])], w_out
    )
    run(out_weights)
    zero_weights = gather_weight_rows(
        wires, feed_sources(gate_ref, up_ref, down_ref, cuts[0], hidden), w_zero
    )
    run(zero_weights)
    next_weights = exchange_halves(
        wires, feed_sources(gate_ref, up_ref, down_ref, cuts[1], hidden), w_next
    )
    run(next_weights)
    cotangents = gather_phase(wires, dout_ref, dout_all, True)
    run(cotangents)
    load_w.wait()

    @pl.loop(0, model // 512)
    def _(t):
        part = pl.ds(pl.multiple_of(t * 512, 512), 512)
        w_pad[part, :] = nn(w_flat[part, :], spread_ref[...]).astype(BF16)

    place = lax.broadcasted_iota(jnp.int32, (8, w_flat.shape[1]), 1)
    which = (place == (heads + 2) * HEAD_SIZE).astype(BF16)
    gain = nt(which, w_flat[...])[0:1, :]

    @pl.when(z == 0)
    def _():
        k_ref[0:WINDOW_LENGTH, :] = jnp.zeros((WINDOW_LENGTH, LANES), BF16)
        v_ref[0:WINDOW_LENGTH, :] = jnp.zeros((WINDOW_LENGTH, LANES), BF16)

    stores = []
    for b in order:
        at = wires.natural(b)
        loads[b].wait()
        x = x_all[at].astype(F32)
        inverse = lax.rsqrt(jnp.mean(x * x, axis=1, keepdims=True) + EPS)
        a1 = (x * inverse * gain).astype(BF16)
        x_all[at] = a1
        stores.append(wires.local(x_all.at[at], a1_ref.at[at]))
        acc = nn(a1, w_pad[...])
        here = slice(b * rows, (b + 1) * rows)
        there = slice(WINDOW_LENGTH + b * rows, WINDOW_LENGTH + (b + 1) * rows)
        cosine, sine = cos_ref[here, :], sin_ref[here, :]
        for h in range(heads + 1):
            u = acc[:, h * LANES : (h + 1) * LANES]
            turned = (u * cosine + pltpu.roll(u, LANES // 2, 1) * sine).astype(BF16)
            if h < heads:
                q_ref[here, h * LANES : (h + 1) * LANES] = turned
            else:
                k_ref[there, :] = turned
        v_ref[there, :] = acc[:, (heads + 1) * LANES :].astype(BF16)
        if b == 7:
            halo = [
                wires.start(
                    ref.at[pl.ds(length, WINDOW_LENGTH)], ref.at[pl.ds(0, WINDOW_LENGTH)],
                    wires.up, z < nz - 1, z > 0,
                )
                for ref in (k_ref, v_ref)
            ]
            run(out_weights)
        if b == 1:
            run(cotangents)
    for copy in halo:
        copy.wait_recv()

    def block(b, at):
        start = pl.multiple_of(b * rows, rows)
        span = pl.ds(start, keys)
        here = pl.ds(start, rows)
        kb = k_ref[span, :]
        vt = v_ref[span, :].T
        bias = mask_bias(kid_ref[span, :], qid_ref[:, here], keys, rows)
        outs = []
        for h in range(heads):
            lanes = slice(h * LANES, (h + 1) * LANES)
            s = nt(kb, q_ref[here, lanes]) * (SCALE * LOG2E) + bias
            peak = jnp.max(s, axis=0, keepdims=True)
            p = jnp.exp2(s - peak)
            total = jnp.sum(p, axis=0, keepdims=True)
            ot = nn(vt, p.astype(BF16)) / total
            outs.append(ot.T.astype(BF16))
            lse_ref[b, h : h + 1, :] = peak + jnp.log2(total)
        o_ref[at] = nn(jnp.concatenate(outs, 1), squeeze_ref[...]).astype(BF16)

    for b in range(8):
        block(b, wires.natural(b))
        if b in (1, 4, 6):
            run(out_weights)
        if b in (3,):
            run(zero_weights)
        if b in (2, 5):
            run(cotangents)
    for store in stores:
        store.wait()
    drain(out_weights, zero_weights, next_weights, cotangents)
    wires.finish()


def attention(x_all, w_attn, cosine, sine, kid, qid, dout, opack, gate, up, down, heads, cuts):
    _, n, model = x_all.shape
    length = 8 * n
    hidden = gate.shape[1] // 2
    wide = heads * LANES
    spread = spread_matrix(heads + 1, 1)
    spread = jnp.concatenate(
        [spread, jnp.zeros((w_attn.shape[1] - spread.shape[0], spread.shape[1]), BF16)], 0
    )
    squeeze = spread_matrix(0, heads).T
    slot = 2 * gate.shape[0]
    first, second = cuts[0][1] - cuts[0][0], cuts[1][1] - cuts[1][0]
    return pl.pallas_call(
        functools.partial(attention_kernel, hidden, cuts),
        in_specs=[HBM, HBM] + [WHOLE] * 7 + [HBM] * 4,
        out_specs=[HBM] + [WHOLE] * 5 + [HBM] * 4,
        out_shape=[
            jax.ShapeDtypeStruct((8, n, model), BF16),
            jax.ShapeDtypeStruct((length, wide), BF16),
            jax.ShapeDtypeStruct((length + WINDOW_LENGTH, LANES), BF16),
            jax.ShapeDtypeStruct((length + WINDOW_LENGTH, LANES), BF16),
            jax.ShapeDtypeStruct((8, n, heads * HEAD_SIZE), BF16),
            jax.ShapeDtypeStruct((8, heads, n), F32),
            jax.ShapeDtypeStruct((8, n, model), BF16),
            jax.ShapeDtypeStruct((model, opack.shape[2]), BF16),
            jax.ShapeDtypeStruct((model, 3 * first), BF16),
            jax.ShapeDtypeStruct((slot, 3 * second), BF16),
        ],
        scratch_shapes=[
            pltpu.VMEM((8, n, model), BF16),
            pltpu.VMEM(w_attn.shape, BF16),
            pltpu.VMEM((model, spread.shape[1]), BF16),
        ]
        + semaphores(),
        compiler_params=params(56, collective_id=5, has_side_effects=True),
        name="attention",
        **light(),
    )(x_all, w_attn, spread, squeeze, cosine, sine, kid, qid, dout, opack, gate, up, down)


def project_kernel(
    a_ref, w_ref, x_ref, gain_ref, slot_ref, res_ref, inv_ref, out_ref, w_all,
    block, cs, cr, q, xr, yr, tr, br, send, recv, local,
):
    wires = Wires(send, recv, local)
    wires.greet()
    n = slot_ref.shape[0]
    own = wires.local(slot_ref, w_all.at[pl.ds(0, n)])
    weights = along_z(wires, slot_ref, lambda s: w_all.at[pl.ds(s * n, n)])
    run(weights)

    def emit(rows, total):
        residual = x_ref[rows, :].astype(F32) + total
        inverse = lax.rsqrt(jnp.mean(residual * residual, axis=1, keepdims=True) + EPS)
        res_ref[rows, :] = residual
        inv_ref[rows, :] = inverse
        block[rows, :] = (residual * inverse * gain_ref[...]).astype(BF16)

    sums = reduce_phase(wires, [(a_ref, w_ref)], cs, cr, q, xr, yr, tr, br, emit)
    run(sums)
    run(sums)
    run(weights)
    drain(sums)
    tokens = gather_phase(wires, block, out_ref)
    run(tokens)
    run(tokens)
    run(weights)
    drain(tokens, weights)
    own.wait()
    wires.finish()


def project_out(o, w_out, inputs, gain, slot):
    n, model = inputs.shape
    return pl.pallas_call(
        project_kernel,
        in_specs=[WHOLE] * 4 + [HBM],
        out_specs=[WHOLE, WHOLE, HBM, HBM],
        out_shape=[
            jax.ShapeDtypeStruct((n, model), F32),
            jax.ShapeDtypeStruct((n, 1), F32),
            jax.ShapeDtypeStruct((8, n, model), BF16),
            jax.ShapeDtypeStruct((model, slot.shape[1]), BF16),
        ],
        scratch_shapes=[pltpu.VMEM((n, model), BF16)] + reduce_scratch(n, model) + semaphores(),
        compiler_params=params(52, collective_id=2, has_side_effects=True),
        name="project_out",
        **light(),
    )(o, w_out, inputs, gain, slot)


def feed_kernel(
    hidden, cuts,
    a_ref, d_ref, w0_ref, w1_ref, gate_ref, up_ref, down_ref,
    m_ref, g_ref, w_ref, grad0, grad1, grad2, mine, got,
    a, d, w, m, g, stage, above, below, extra, send, recv, local,
):
    wires = Wires(send, recv, local)
    nz = wires.nz
    length, model = a.shape
    slot = model // nz
    wires.greet()
    small, large = cuts[0][1] - cuts[0][0], cuts[1][1] - cuts[1][0]
    loads = []
    for ref, (lo, hi) in ((w0_ref, cuts[0]), (w1_ref, cuts[1])):
        for k in range(3):
            loads.append(
                wires.local(
                    ref.at[:, k * (hi - lo) : (k + 1) * (hi - lo)],
                    w.at[:, k * hidden + lo : k * hidden + hi],
                )
            )
    blocks = 4
    rows = length // blocks
    a_loads, d_loads = [], []
    for b in range(blocks):
        part = pl.ds(b * rows, rows)
        a_loads.append(wires.local(a_ref.at[part], a.at[part]))
        d_loads.append(wires.local(d_ref.at[part], d.at[part]))

    def carried(cut):
        lo, hi = cut
        sources = feed_sources(gate_ref, up_ref, down_ref, cut, hidden)
        picks = [(pick, k * hidden + lo, k * hidden + hi) for k, (pick, _, _) in enumerate(sources)]
        head = exchange_halves(wires, picks, w.at[pl.ds(0, slot)])
        yield from head
        hops = [
            along_z(
                wires,
                w.at[pl.ds(0, slot), k * hidden + lo : k * hidden + hi],
                lambda s, k=k: w.at[pl.ds(s * slot, slot), k * hidden + lo : k * hidden + hi],
            )
            for k in range(3)
        ]
        while hops:
            hops = [hop for hop in hops if next(hop, None) is not None]
            yield 1

    later = [carried(cut) for cut in cuts[2:]]
    for part in later:
        run(part)
    for copy in loads:
        copy.wait()

    def units(lo, hi, waits):
        for b in range(blocks):
            if waits:
                a_loads[b].wait()
                d_loads[b].wait()
            part = pl.ds(b * rows, rows)
            gate = nn(a[part, :], w[:, lo:hi])
            up = nn(a[part, :], w[:, hidden + lo : hidden + hi])
            dmixed = nn(d[part, :], w[:, 2 * hidden + lo : 2 * hidden + hi])
            sigma = jax.nn.sigmoid(gate)
            silu = gate * sigma
            m[part, lo:hi] = (silu * up).astype(BF16)
            g[part, hidden + lo : hidden + hi] = (dmixed * silu).astype(BF16)
            g[part, lo:hi] = (dmixed * up * sigma * (1.0 + gate * (1.0 - sigma))).astype(BF16)
            yield 1

    def weight_grads(lo, hi, out):
        n = hi - lo
        tile = 640
        pending = [None, None]
        for t in range(model // tile):
            cols = slice(t * tile, (t + 1) * tile)
            if pending[t % 2] is not None:
                pending[t % 2].wait()
            here = stage.at[t % 2]
            for k in range(3):
                left = d if k == 2 else a
                right = m[:, lo:hi] if k == 2 else g[:, k * hidden + lo : k * hidden + hi]
                here[:, k * n : (k + 1) * n] = tn(left[:, cols], right).astype(BF16)
            pending[t % 2] = wires.local(
                here.at[:, 0 : 3 * n], out.at[pl.ds(t * tile, tile)]
            )
            yield 1
        for copy in pending:
            copy.wait()

    first = (cuts[0][0], cuts[1][1])
    for i, _ in enumerate(units(*first, True)):
        if i == 0:
            run(later[0])
    run(later[0])
    for _ in weight_grads(*first, grad0):
        pass
    sums = sum_along_z(
        wires, columns(grad0, slot, 0, mine.shape[1]), above, below, extra, mine, got
    )
    run(sums)
    run(later[0])
    run(later[1])
    drain(later[0])
    for _ in units(*cuts[2], False):
        pass
    run(sums)
    run(later[1])
    for i, _ in enumerate(weight_grads(*cuts[2], grad1)):
        if i == 1:
            run(later[1])
    run(sums)
    drain(later[1])
    for _ in units(*cuts[3], False):
        pass
    outs = [wires.local(w, w_ref), wires.local(m, m_ref), wires.local(g, g_ref)]
    for _ in weight_grads(*cuts[3], grad2):
        pass
    drain(sums)
    for copy in outs:
        copy.wait()
    wires.finish()


def feed_forward(a2, dout, w0, w1, gate, up, down, cuts):
    length, model = a2.shape
    hidden = gate.shape[1] // 2
    first = cuts[1][1]
    sizes = [first] + [b - a for a, b in cuts[2:]]
    rows = 2 * gate.shape[0]
    nz = model // rows
    share = 3 * first // 2
    return pl.pallas_call(
        functools.partial(feed_kernel, hidden, cuts),
        in_specs=[HBM] * 7,
        out_specs=[HBM] * 8,
        out_shape=[
            jax.ShapeDtypeStruct((length, hidden), BF16),
            jax.ShapeDtypeStruct((length, 2 * hidden), BF16),
            jax.ShapeDtypeStruct((model, 3 * hidden), BF16),
        ]
        + [jax.ShapeDtypeStruct((model, 3 * n), BF16) for n in sizes]
        + sum_outputs(rows, share),
        scratch_shapes=[
            pltpu.VMEM((length, model), BF16),
            pltpu.VMEM((length, model), BF16),
            pltpu.VMEM((model, 3 * hidden), BF16),
            pltpu.VMEM((length, hidden), BF16),
            pltpu.VMEM((length, 2 * hidden), BF16),
            pltpu.VMEM((2, 640, 3 * first), BF16),
        ]
        + sum_scratch(nz, rows, share)
        + semaphores(),
        compiler_params=params(60, collective_id=1, has_side_effects=True),
        name="feed_forward",
        **light(),
    )(a2, dout, w0, w1, gate, up, down)


def reduce_phase(wires, pairs, cs, cr, q, xr, yr, tr, br, emit):
    n = q.shape[1]
    half = n // 2
    top, bottom = pl.ds(0, half), pl.ds(half, half)
    model = q.shape[2]
    tile = 512

    def product(place, target):
        @pl.loop(0, model // tile)
        def _(t):
            cols = pl.ds(pl.multiple_of(t * tile, tile), tile)
            total = None
            for a, w in pairs:
                part = nt(a[place], w[cols, :])
                total = part if total is None else total + part
            target[:, cols] = total.astype(BF16)

    waits = {}
    for j in (3, 1, 2, 0):
        product(2 * j + 1, cs.at[j])
        got = wires.start(cs.at[j], cr.at[j], wires.c)
        product(2 * j, q.at[j])
        got.wait_recv()
        q[j] = (q[j].astype(F32) + cr[j].astype(F32)).astype(BF16)
        if j == 3:
            waits["x1"] = wires.start(q.at[3, top], xr.at[1], wires.x)
            waits["y1"] = wires.start(q.at[3, bottom], yr.at[1], wires.y)
        if j == 1:
            waits["x0"] = wires.start(q.at[1, top], xr.at[0], wires.x)
        if j == 2:
            waits["y0"] = wires.start(q.at[2, bottom], yr.at[0], wires.y)
    yield 1
    waits["x1"].wait_recv()
    q[2, top] = (q[2, top].astype(F32) + xr[1].astype(F32)).astype(BF16)
    waits["t"] = wires.start(q.at[2, top], tr, wires.y)
    waits["y1"].wait_recv()
    q[1, bottom] = (q[1, bottom].astype(F32) + yr[1].astype(F32)).astype(BF16)
    waits["b"] = wires.start(q.at[1, bottom], br, wires.x)
    waits["x0"].wait_recv()
    yield 1
    waits["t"].wait_recv()
    emit(top, q[0, top].astype(F32) + xr[0].astype(F32) + tr[...].astype(F32))
    waits["y0"].wait_recv()
    waits["b"].wait_recv()
    emit(bottom, q[0, bottom].astype(F32) + yr[0].astype(F32) + br[...].astype(F32))


def reduce_scratch(n, model):
    half = n // 2
    return [
        pltpu.VMEM((4, n, model), BF16),
        pltpu.VMEM((4, n, model), BF16),
        pltpu.VMEM((4, n, model), BF16),
        pltpu.VMEM((2, half, model), BF16),
        pltpu.VMEM((2, half, model), BF16),
        pltpu.VMEM((half, model), BF16),
        pltpu.VMEM((half, model), BF16),
    ]


def middle_kernel(
    a_ref, w_ref, dout_ref, res_ref, inv_ref, gain_ref, grad0, grad2,
    dres_ref, out_ref, mine0, got0, mine2, got2,
    block, cs, cr, q, xr, yr, tr, br,
    above0, below0, stage0, above2, below2, stage2, send, recv, local,
):
    wires = Wires(send, recv, local)
    wires.greet()
    rows = mine0.shape[0] * 2
    wide = grad0.shape[1]
    first = sum_along_z(
        wires, columns(grad0, rows, wide - mine0.shape[1], wide), above0, below0, stage0, mine0, got0
    )
    second = sum_along_z(
        wires, columns(grad2, rows, 0, mine2.shape[1]), above2, below2, stage2, mine2, got2
    )
    run(first)

    def emit(rows, total):
        inverse = inv_ref[rows, :]
        normed = res_ref[rows, :] * inverse
        e = total * gain_ref[...]
        back = inverse * (e - normed * jnp.mean(e * normed, axis=1, keepdims=True))
        dres = dout_ref[rows, :].astype(F32) + back
        dres_ref[rows, :] = dres
        block[rows, :] = dres.astype(BF16)

    sums = reduce_phase(wires, [(a_ref, w_ref)], cs, cr, q, xr, yr, tr, br, emit)
    run(sums)
    run(first)
    run(sums)
    run(first)
    run(second)
    drain(sums)
    tokens = gather_phase(wires, block, out_ref)
    run(tokens)
    run(tokens)
    run(first)
    run(second)
    run(tokens)
    run(second)
    run(tokens)
    run(second)
    drain(tokens, first, second)
    wires.finish()


def feed_back(dgu, w, dout, residual, inverse, gain, grad0, grad2):
    n, model = dout.shape
    k = dgu.shape[1]
    rows = 2 * model // lax.axis_size("tok")
    nz = model // rows
    flat = pl.BlockSpec((n, model), lambda i: (0, 0))
    thin = pl.BlockSpec((n, 1), lambda i: (0, 0))
    half, small = grad0.shape[1] // 2, grad2.shape[1]
    return pl.pallas_call(
        middle_kernel,
        grid=(1,),
        in_specs=[
            pl.BlockSpec((8, n, k), lambda i: (0, 0, 0)),
            pl.BlockSpec((model, k), lambda i: (0, 0)),
            flat, flat, thin, pl.BlockSpec((1, model), lambda i: (0, 0)), HBM, HBM,
        ],
        out_specs=[flat] + [HBM] * 5,
        out_shape=[
            jax.ShapeDtypeStruct((n, model), F32),
            jax.ShapeDtypeStruct((8, n, model), BF16),
        ]
        + sum_outputs(rows, half)
        + sum_outputs(rows, small),
        scratch_shapes=[pltpu.VMEM((n, model), BF16)]
        + reduce_scratch(n, model)
        + sum_scratch(nz, rows, half)
        + sum_scratch(nz, rows, small)
        + semaphores(),
        compiler_params=params(62, collective_id=3, has_side_effects=True),
        name="feed_back",
        **light(),
    )(dgu.reshape(8, n, k), w, dout, residual, inverse, gain, grad0, grad2)


def back_kernel(
    da_ref, w_ref, o_ref, q_ref, k_ref, v_ref, lse_ref, kid_ref, qid_ref, cos_ref, sin_ref,
    spread_ref, squeeze_ref, final_ref, m_ref, down_ref, res_ref, grad1,
    dqkv_ref, grad_out, out_ref, mine, got,
    da, do, dk, dv, halo, fetched, m, w_down, cr, xr, yr, tr, br, gstage,
    above, below, stage, send, recv, local,
):
    wires = Wires(send, recv, local)
    nz, z = wires.nz, wires.at_z
    wires.greet()
    n, model = da.shape[1], da.shape[2]
    heads = q_ref.shape[1] // LANES
    wide = heads * HEAD_SIZE
    keys = n + WINDOW_LENGTH
    length = 8 * n
    loads = [wires.local(da_ref.at[b], da.at[b]) for b in range(8)]
    late = [
        wires.local(m_ref, m),
        wires.local(down_ref.at[:, 2 * m.shape[2] :], w_down),
    ]
    rows = 2 * mine.shape[0]
    carried = sum_along_z(
        wires, columns(grad1, rows, 0, mine.shape[1]), above, below, stage, mine, got
    )
    run(carried)
    dk[...] = jnp.zeros_like(dk)
    dv[...] = jnp.zeros_like(dv)
    for b in range(8):
        loads[b].wait()
        flat = nn(da[b], w_ref[...]).astype(BF16)
        do[b] = nn(flat, spread_ref[...]).astype(BF16)

    tile = 640
    for t in range(model // tile):
        cols = slice(t * tile, (t + 1) * tile)
        total = None
        for b in range(8):
            part = tn(da[b, :, cols], o_ref[b])
            total = part if total is None else total + part
        gstage[cols, :] = total.astype(BF16)
    save = wires.local(gstage, grad_out)
    for load in late:
        load.wait()

    def emit(part, total):
        out_ref[part, :] = (res_ref[part, :] + total).astype(BF16)

    sums = reduce_phase(
        wires, [(m, w_down)], da.at[pl.ds(0, 4)], cr, da.at[pl.ds(4, 4)], xr, yr, tr, br, emit
    )
    run(sums)
    run(carried)

    def block(b, at):
        start = pl.multiple_of(b * n, n)
        span = pl.ds(start, keys)
        here = pl.ds(start, n)
        kb = k_ref[span, :]
        vb = v_ref[span, :]
        kt = kb.T
        bias = mask_bias(kid_ref[span, :], qid_ref[:, here], keys, n)
        cosine, sine = cos_ref[here, :], sin_ref[here, :]
        dqs = []
        dk_sum = dv_sum = None
        for h in range(heads):
            lanes = slice(h * LANES, (h + 1) * LANES)
            qh = q_ref[here, lanes]
            doh = do[at, :, lanes]
            p = jnp.exp2(nt(kb, qh) * (SCALE * LOG2E) + (bias - lse_ref[b, h : h + 1, :]))
            t = p * nt(vb, doh)
            inner = jnp.sum(t, axis=0, keepdims=True)
            ds = (t - p * inner).astype(BF16)
            dq = nn(kt, ds).T * SCALE
            dqs.append((dq * cosine - pltpu.roll(dq, LANES // 2, 1) * sine).astype(BF16))
            dk_h = nn(ds, qh)
            dv_h = nn(p.astype(BF16), doh)
            dk_sum = dk_h if dk_sum is None else dk_sum + dk_h
            dv_sum = dv_h if dv_sum is None else dv_sum + dv_h
        dqkv_ref[at, :, 0:wide] = nn(jnp.concatenate(dqs, 1), squeeze_ref[...]).astype(BF16)
        dk[span, :] += dk_sum
        dv[span, :] += dv_sum

    for b in range(8):
        block(b, wires.natural(b))
        if b == 1:
            halo[:, 0:LANES] = dk[0:WINDOW_LENGTH, :].astype(BF16)
            halo[:, LANES:] = dv[0:WINDOW_LENGTH, :].astype(BF16)
            borrowed = wires.start(halo, fetched, wires.down, z >= 1, z < nz - 1)
        if b in (2, 5):
            run(sums)
        if b == 4:
            run(carried)
    borrowed.wait_recv()

    @pl.when(z < nz - 1)
    def _():
        dk[length:, :] += fetched[:, 0:LANES].astype(F32)
        dv[length:, :] += fetched[:, LANES:].astype(F32)

    for b in range(8):
        here = slice(b * n, (b + 1) * n)
        there = slice(WINDOW_LENGTH + b * n, WINDOW_LENGTH + (b + 1) * n)
        dkb = dk[there, :] * SCALE
        dkb = dkb * cos_ref[here, :] - pltpu.roll(dkb, LANES // 2, 1) * sin_ref[here, :]
        both = jnp.concatenate([dkb.astype(BF16), dv[there, :].astype(BF16)], 1)
        dqkv_ref[wires.natural(b), :, wide:] = nn(both, final_ref[...]).astype(BF16)
    drain(sums, carried)
    save.wait()
    wires.finish()


def attention_back(
    da_all, w_out, o, q, k_all, v_all, lse, kid, qid, cosine, sine, mixed, w_feed, residual, grad1
):
    _, n, model = da_all.shape
    length = 8 * n
    heads = q.shape[1] // LANES
    wide = heads * HEAD_SIZE
    spread = spread_matrix(0, heads)
    squeeze = spread_matrix(heads, 0).T
    final = spread_matrix(1, 1).T
    rows = 2 * model // lax.axis_size("tok")
    nz = model // rows
    hidden = mixed.shape[1]
    half = n // 2
    return pl.pallas_call(
        back_kernel,
        in_specs=[HBM] + [WHOLE] * 13 + [HBM, HBM, WHOLE, HBM],
        out_specs=[WHOLE, HBM, WHOLE, HBM, HBM],
        out_shape=[
            jax.ShapeDtypeStruct((8, n, wide + 2 * HEAD_SIZE), BF16),
            jax.ShapeDtypeStruct((model, wide), BF16),
            jax.ShapeDtypeStruct((n, model), BF16),
        ]
        + sum_outputs(rows, grad1.shape[1]),
        scratch_shapes=[
            pltpu.VMEM((8, n, model), BF16),
            pltpu.VMEM((8, n, heads * LANES), BF16),
            pltpu.VMEM(k_all.shape, F32),
            pltpu.VMEM(k_all.shape, F32),
            pltpu.VMEM((WINDOW_LENGTH, 2 * LANES), BF16),
            pltpu.VMEM((WINDOW_LENGTH, 2 * LANES), BF16),
            pltpu.VMEM((8, n, hidden), BF16),
            pltpu.VMEM((model, hidden), BF16),
            pltpu.VMEM((4, n, model), BF16),
            pltpu.VMEM((2, half, model), BF16),
            pltpu.VMEM((2, half, model), BF16),
            pltpu.VMEM((half, model), BF16),
            pltpu.VMEM((half, model), BF16),
            pltpu.VMEM((model, wide), BF16),
        ]
        + sum_scratch(nz, rows, grad1.shape[1])
        + semaphores(),
        compiler_params=params(62, collective_id=6, has_side_effects=True),
        name="attention_back",
        **light(),
    )(
        da_all, w_out, o, q, k_all, v_all, lse, kid, qid, cosine, sine, spread, squeeze, final,
        mixed.reshape(8, n, hidden), w_feed, residual, grad1,
    )


def last_kernel(
    a_ref, w_ref, x_ref, inv_ref, gain_ref, dres_ref, a1_ref, grad_out,
    out_ref, mine0, got0, mine1, got1,
    cs, cr, q, xr, yr, tr, br, a1, grad,
    above0, below0, stage0, above1, below1, stage1, send, recv, local,
):
    wires = Wires(send, recv, local)
    wires.greet()
    rows = 2 * mine0.shape[0]
    model = a1.shape[2]
    loads = [wires.local(a1_ref.at[b], a1.at[b]) for b in range(8)]
    first = sum_along_z(
        wires, columns(grad_out, rows, 0, mine0.shape[1]), above0, below0, stage0, mine0, got0
    )
    run(first)

    def emit(rows, total):
        inverse = inv_ref[rows, :]
        normed = x_ref[rows, :].astype(F32) * inverse
        e = total * gain_ref[...]
        back = inverse * (e - normed * jnp.mean(e * normed, axis=1, keepdims=True))
        out_ref[rows, :] = dres_ref[rows, :] + back

    sums = reduce_phase(wires, [(a_ref, w_ref)], cs, cr, q, xr, yr, tr, br, emit)
    run(sums)
    run(first)
    for load in loads:
        load.wait()
    tile = 640
    for t in range(model // tile):
        cols = slice(t * tile, (t + 1) * tile)
        total = None
        for b in range(8):
            part = tn(a1[b, :, cols], a_ref[b])
            total = part if total is None else total + part
        grad[cols, :] = total.astype(BF16)
        if t == 1:
            run(first)
    second = sum_along_z(
        wires, columns(grad, rows, 0, mine1.shape[1]), above1, below1, stage1, mine1, got1
    )
    run(second)
    run(first)
    run(sums)
    run(second)
    drain(sums, second, first)
    wires.finish()


def input_back(dqkv, w, inputs, inverse, gain, dres, a1, grad_out):
    n, model = inputs.shape
    rows = 2 * model // lax.axis_size("tok")
    nz = model // rows
    wide = dqkv.shape[2]
    return pl.pallas_call(
        last_kernel,
        in_specs=[WHOLE] * 6 + [HBM] * 2,
        out_specs=[WHOLE] + [HBM] * 4,
        out_shape=[jax.ShapeDtypeStruct((n, model), F32)]
        + sum_outputs(rows, grad_out.shape[1])
        + sum_outputs(rows, wide),
        scratch_shapes=reduce_scratch(n, model)
        + [pltpu.VMEM((8, n, model), BF16), pltpu.VMEM((model, wide), BF16)]
        + sum_scratch(nz, rows, grad_out.shape[1])
        + sum_scratch(nz, rows, wide)
        + semaphores(),
        compiler_params=params(60, collective_id=4, has_side_effects=True),
        name="input_back",
        **light(),
    )(dqkv, w, inputs, inverse, gain, dres, a1, grad_out)


def body(
    inputs,
    grad_output,
    segments,
    attention_gain,
    query_weight,
    key_matrix,
    value_matrix,
    output_weight,
    feedforward_gain,
    gate_weight,
    up_weight,
    down_weight,
):
    grid = Grid()
    bf16 = jnp.bfloat16
    model = inputs.shape[1]
    length = inputs.shape[0] * 8
    hidden = gate_weight.shape[1] // 2
    qdim = query_weight.shape[1] // 2
    kdim = key_matrix.shape[1] // 2
    cuts = []
    at = 0
    for n in FF_CHUNKS:
        cuts.append((at, at + n))
        at += n
    heads = qdim // HEAD_SIZE

    def packed(*arrays):
        cut = [v.reshape(v.shape[0], 2, -1) for v in arrays]
        return jnp.transpose(jnp.concatenate(cut, 2), (1, 0, 2))

    gains = jnp.stack([attention_gain, feedforward_gain], 1)
    blank = jnp.zeros((gains.shape[0], LANES - (qdim + 2 * kdim + 2) % LANES), bf16)
    tail = jnp.concatenate([gains, blank], 1)
    qkv_pack = packed(
        query_weight, key_matrix, value_matrix, jnp.concatenate([tail, tail], 1)
    )
    out_pack = packed(output_weight.T)
    down_t = down_weight.T

    me = jnp.reshape(grid.me, (1,)).astype(jnp.int32)
    own = rotated(grid, inputs)
    x_all, w_attn = gather_start(own, qkv_pack)
    dout = rotated(grid, grad_output)
    cosine, sine = rope_tables(length, grid.z * length, HEAD_SIZE)
    padded_ids = jnp.concatenate([jnp.full((WINDOW_LENGTH,), -1, jnp.int32), segments])
    key_ids = lax.dynamic_slice_in_dim(padded_ids, grid.z * length, length + WINDOW_LENGTH, 0)
    kid, qid = key_ids[:, None], key_ids[None, WINDOW_LENGTH:]
    gain_rows = w_attn[:, qdim + 2 * kdim : qdim + 2 * kdim + 2].astype(F32).T
    gain_one, gain_two = gain_rows[0:1], gain_rows[1:2]
    a1, q, k_all, v_all, o, lse, dout_all, w_out, w_zero, w_next = attention(
        x_all, w_attn, cosine, sine, kid, qid, dout, out_pack, gate_weight, up_weight, down_t,
        heads, cuts,
    )
    flat = lambda v: v.reshape(length, v.shape[-1])
    residual, inverse_two, a2, w_one = project_out(o, w_out, own, gain_two, w_next)

    mixed, dgu, w_feed, grad0, grad1, grad2, mine_a, got_a = feed_forward(
        flat(a2), flat(dout_all), w_zero, w_one, gate_weight, up_weight, down_t, cuts
    )
    dresidual, da_all, mine_b, got_b, mine_d, got_d = feed_back(
        dgu, w_feed, dout, residual, inverse_two, gain_two, grad0, grad2
    )
    dqkv, grad_o, layer, mine_c, got_c = attention_back(
        da_all, w_out, o, q, k_all, v_all, lse, kid, qid, cosine, sine, mixed, w_feed, residual,
        grad1,
    )
    layer_output = rotated(grid, layer)
    own_wide = own.astype(F32)
    inverse_one = lax.rsqrt(jnp.mean(own_wide * own_wide, axis=-1, keepdims=True) + EPS)
    dinput, mine_o, got_o, mine_q, got_q = input_back(
        dqkv, w_attn[:, : qdim + 2 * kdim], own, inverse_one, gain_one, dresidual, a1, grad_o
    )
    input_gradient = rotated(grid, dinput)

    def paired(mine, got):
        first = jnp.where(grid.y == 0, mine, got)
        second = jnp.where(grid.y == 0, got, mine)
        return jnp.stack([first, second], 1).astype(F32)

    both = lambda left, right: jnp.concatenate([left, right], 1)
    ff_grads = [
        paired(both(mine_a, mine_b), both(got_a, got_b)),
        paired(mine_c, got_c),
        paired(mine_d, got_d),
    ]
    attn_grad = paired(mine_q, got_q)
    out_grad = paired(mine_o, got_o)
    groups = [(cuts[0][0], cuts[1][1])] + cuts[2:]

    def whole(part):
        return part.reshape(part.shape[0], -1)

    query_grad = whole(attn_grad[:, :, :qdim])
    key_grad = whole(attn_grad[:, :, qdim : qdim + kdim])
    value_grad = whole(attn_grad[:, :, qdim + kdim :])
    output_grad = whole(out_grad).T
    parts = []
    for k in range(3):
        parts.append(
            whole(
                jnp.concatenate(
                    [g[:, :, k * (b - a) : (k + 1) * (b - a)] for (a, b), g in zip(groups, ff_grads)],
                    2,
                )
            )
        )
    gate_grad, up_grad, down_grad = parts[0], parts[1], parts[2].T

    def row_sum(*both):
        return sum(
            jnp.sum(w.astype(jnp.float32) * g, axis=1) for w, g in both
        )

    sums = jnp.stack(
        [
            row_sum((query_weight, query_grad), (key_matrix, key_grad), (value_matrix, value_grad)),
            row_sum((gate_weight, gate_grad), (up_weight, up_grad)),
        ]
    )
    sums = sums + grid.swap(sums, C)
    sums = sums + grid.swap(sums, X)
    return (
        layer_output,
        input_gradient,
        sums[0] / attention_gain.astype(jnp.float32),
        query_grad,
        key_grad,
        value_grad,
        output_grad,
        sums[1] / feedforward_gain.astype(jnp.float32),
        gate_grad,
        up_grad,
        down_grad,
    )


def solution(mesh):
    in_specs = (
        P(("tok", "mp"), None),
        P(("tok", "mp"), None),
        P(),
        P("tok"),
        P("tok", "mp"),
        P("tok", "mp"),
        P("tok", "mp"),
        P("mp", "tok"),
        P("tok"),
        P("tok", "mp"),
        P("tok", "mp"),
        P("mp", "tok"),
    )
    out_specs = (
        P(("tok", "mp"), None),
        P(("tok", "mp"), None),
        P("tok"),
        P("tok", "mp"),
        P("tok", "mp"),
        P("tok", "mp"),
        P("mp", "tok"),
        P("tok"),
        P("tok", "mp"),
        P("tok", "mp"),
        P("mp", "tok"),
    )
    return jax.shard_map(body, mesh=mesh, in_specs=in_specs, out_specs=out_specs, check_vma=False)
```

```python
import functools

import jax
import jax.numpy as jnp
import ml_dtypes
import numpy as np
from jax import lax
from jax.experimental import pallas as pl
from jax.experimental.pallas import tpu as pltpu
from jax.sharding import PartitionSpec as P

HEAD_SIZE = 80
WINDOW_LENGTH = 512
EPS = 1e-05
THETA = 1000000.0
FLOOR = -1e30
AXES = ("tok", "mp")
FF_CHUNKS = (128, 384, 256, 128)
FF_PARTS = (256, 256, 256, 128)


class Grid:
    def __init__(self):
        self.nz = lax.axis_size("tok") // 2
        tok = lax.axis_index("tok")
        mp = lax.axis_index("mp")
        self.z, self.y = tok // 2, tok % 2
        self.x, self.c = mp // 2, mp % 2
        self.me = self.y * 4 + self.x * 2 + self.c

    def pairs(self, move):
        out = []
        for z in range(self.nz):
            for g in range(8):
                target = move(z, g)
                if target is not None:
                    out.append((z * 8 + g, target[0] * 8 + target[1]))
        return out

    def swap(self, value, bit):
        return lax.ppermute(value, AXES, self.pairs(lambda z, g: (z, g ^ bit)))

    def ring(self, value):
        return lax.ppermute(value, AXES, self.pairs(lambda z, g: ((z + 1) % self.nz, g)))

    def step(self, value, d):
        def move(z, g):
            return (z + d, g) if 0 <= z + d < self.nz else None

        return lax.ppermute(value, AXES, self.pairs(move))


Y, X, C = 4, 2, 1


LANES = 128
SCALE = HEAD_SIZE ** (-0.5)
LOG2E = 1.4426950408889634
MIB = 1024 * 1024
BF16 = jnp.bfloat16
F32 = jnp.float32
HBM = pl.BlockSpec(memory_space=pl.ANY)
WHOLE = pl.BlockSpec(memory_space=pltpu.VMEM)
MESH = pl.DeviceIdType.MESH


def light(**kwargs):
    return dict(
        cost_estimate=pl.CostEstimate(flops=1000000, bytes_accessed=100000, transcendentals=0),
        **kwargs,
    )


def params(mib, **kwargs):
    return pltpu.CompilerParams(vmem_limit_bytes=mib * MIB, **kwargs)


ROPE_STEP = 64


def rope_parts(count, first, width):
    half = width // 2
    freqs = THETA ** (-(jnp.arange(half, dtype=jnp.int32).astype(F32) * 2.0 / width))
    high = first + ROPE_STEP * jnp.arange(count // ROPE_STEP, dtype=jnp.int32)
    places = jnp.concatenate([high, jnp.arange(ROPE_STEP, dtype=jnp.int32)]).astype(F32)
    blank = jnp.zeros((LANES // 2 - half,), F32)
    lanes = jnp.concatenate([freqs, blank, freqs, blank])
    angles = places[:, None] * lanes[None, :]
    return jnp.stack([jnp.cos(angles), jnp.sin(angles)])


def spread_matrix(turned, plain, rows=0, columns=0):
    half = HEAD_SIZE // 2
    f = np.arange((turned + plain) * HEAD_SIZE)
    head, place = f // HEAD_SIZE, f % HEAD_SIZE
    target = head * LANES + place
    target = target + np.where((head < turned) & (place >= half), LANES // 2 - half, 0)
    out = np.zeros(
        (max(rows, f.size), max(columns, (turned + plain) * LANES)), ml_dtypes.bfloat16
    )
    out[f, target] = 1
    return out


def nt(left, right):
    return lax.dot_general(left, right, (((1,), (1,)), ((), ())), preferred_element_type=F32)


def nn(left, right):
    return lax.dot_general(left, right, (((1,), (0,)), ((), ())), preferred_element_type=F32)


def tn(left, right):
    return lax.dot_general(left, right, (((0,), (0,)), ((), ())), preferred_element_type=F32)


def mask_bias(first, keys, rows):
    kk = lax.broadcasted_iota(jnp.int32, (keys, rows), 0)
    qq = lax.broadcasted_iota(jnp.int32, (keys, rows), 1)
    return jnp.where((kk >= first) & (kk - qq <= WINDOW_LENGTH), 0.0, FLOOR)


def identity(n):
    i = lax.broadcasted_iota(jnp.int32, (n, n), 0)
    return (i == lax.broadcasted_iota(jnp.int32, (n, n), 1)).astype(BF16)


def rotation(wires, model):
    width = model // wires.nz
    if width % LANES:
        return [(slice(0, model), slice(0, model))]
    out = []
    for s in range(wires.nz):
        block = lax.rem(wires.at_z - s + wires.nz, wires.nz)
        start = pl.multiple_of(block * width, LANES)
        out.append((slice(s * width, (s + 1) * width), pl.ds(start, width)))
    return out


def outside_rotation(grid, value, back=False):
    width = value.shape[-1] // grid.nz
    if width % LANES == 0:
        return value
    parts = []
    for s in range(grid.nz):
        block = lax.rem(grid.z - s + grid.nz, grid.nz)
        parts.append(lax.dynamic_slice_in_dim(value, block * width, width, value.ndim - 1))
    return jnp.concatenate(parts, -1)


def only(condition, act):
    if condition is None:
        act()
    else:
        pl.when(condition)(act)


class Copy:
    def __init__(self, copy, when, got, index):
        self.copy, self.when, self.got, self.index = copy, when, got, index

    def wait_recv(self):
        only(self.got, self.copy.wait_recv)

    def wait_send(self):
        only(self.when, self.copy.wait_send)


SEMAPHORES = 96


def semaphores():
    return [
        pltpu.SemaphoreType.DMA((SEMAPHORES,)),
        pltpu.SemaphoreType.DMA((SEMAPHORES,)),
        pltpu.SemaphoreType.DMA((SEMAPHORES,)),
    ]


class Wires:
    def __init__(self, send, recv, local):
        self.send, self.recv, self.here = send, recv, local
        self.count = self.local_count = 0
        self.copies = []
        tokens = lax.axis_size("tok")
        tok, mp = lax.axis_index("tok"), lax.axis_index("mp")
        self.nz = tokens // 2
        self.at_z, self.at_y = tok // 2, tok % 2
        self.at_x, self.at_c = mp // 2, mp % 2
        self.x = (tok, lax.rem(mp + 2, 4))
        self.y = (tok + 1 - 2 * self.at_y, mp)
        self.c = (tok, mp + 1 - 2 * self.at_c)
        self.up = (lax.rem(tok + 2, tokens), mp)
        self.down = (lax.rem(tok + tokens - 2, tokens), mp)

    def hello(self):
        barrier = pltpu.get_barrier_semaphore()
        for peer in (self.x, self.y, self.c, self.up, self.down):
            pl.semaphore_signal(barrier, inc=1, device_id=peer, device_id_type=MESH)

    def ready(self):
        pl.semaphore_wait(pltpu.get_barrier_semaphore(), 5)

    def greet(self):
        self.hello()
        self.ready()

    def start(self, source, target, peer, when=None, got=None, index=None):
        i = index
        if index is None:
            i = self.count
            self.count += 1
        copy = pltpu.make_async_remote_copy(
            src_ref=source,
            dst_ref=target,
            send_sem=self.send.at[i],
            recv_sem=self.recv.at[i],
            device_id=peer,
            device_id_type=MESH,
        )
        only(when, copy.start)
        made = Copy(copy, when, got, i)
        self.copies.append(made)
        return made

    def local(self, source, target):
        copy = pltpu.make_async_copy(source, target, self.here.at[self.local_count])
        self.local_count += 1
        copy.start()
        return copy

    def natural(self, b):
        spots = ((self.at_y, b // 4), (self.at_x, b // 2 % 2), (self.at_c, b % 2))
        place = 0
        for at, bit in spots:
            place = 2 * place + at + bit - 2 * at * bit
        return place

    def finish(self):
        for copy in self.copies:
            copy.wait_send()


def drain(*parts):
    parts = list(parts)
    while parts:
        parts = [part for part in parts if next(part, None) is not None]


def run(part):
    next(part, None)


def exchange_halves(wires, sources, slot, bounce=None):
    n = slot.shape[0] // 2
    rows = pl.ds(pl.multiple_of(wires.at_y * n, n), n)
    arrivals, copies = [], []
    for pick, lo, hi in sources:
        arrivals.append(wires.start(pick(1 - wires.at_y), slot.at[rows, lo:hi], wires.y))
        to = slot.at[rows, lo:hi] if bounce is None else bounce.at[:, lo:hi]
        copies.append(wires.local(pick(wires.at_y), to))
    yield 1
    for copy in copies:
        copy.wait()
    if bounce is not None:
        wires.local(bounce, slot.at[rows]).wait()
    for arrival in arrivals:
        arrival.wait_recv()


def along_z(wires, first, slot):
    nz, z = wires.nz, wires.at_z
    get = lambda s: first if s == 0 else slot(s)
    for s in range(1, nz):
        up = wires.start(get(s - 1), slot(s), wires.up, (z >= s - 1) & (z < nz - 1), z >= s)
        down = wires.start(
            get((nz - s + 1) % nz), slot(nz - s), wires.down, (z + s <= nz) & (z >= 1), z + s < nz
        )
        yield 1
        up.wait_recv()
        down.wait_recv()


def add_into(target, source):
    @pl.loop(0, target.shape[0] // 32)
    def _(t):
        part = pl.ds(pl.multiple_of(t * 32, 32), 32)
        target[part, :] = (target[part, :].astype(F32) + source[part, :].astype(F32)).astype(BF16)


def sum_along_z(wires, p, above, below, stage, total):
    nz, z = wires.nz, wires.at_z
    ups, downs = {}, {}

    def ends(s):
        ups[s] = wires.start(p(s), above.at[s - 1], wires.up, z == 0, (z >= 1) & (z <= s))
        downs[s] = wires.start(
            p(nz - s), below.at[s - 1], wires.down, z == nz - 1, (z + s >= nz - 1) & (z < nz - 1)
        )

    ends(1)
    for s in range(2, nz):
        loads = [wires.local(p(s), stage.at[0]), wires.local(p(nz - s), stage.at[1])]
        yield 1
        ups[s - 1].wait_recv()
        downs[s - 1].wait_recv()
        for load in loads:
            load.wait()
        ends(s)
        rising = (z >= 1) & (z < s) & (z < nz - 1)
        falling = (z + s >= nz) & (z < nz - 1) & (z >= 1)
        only(rising, lambda s=s: add_into(above.at[s - 2], stage.at[0]))
        wires.start(above.at[s - 2], above.at[s - 1], wires.up, rising, None, ups[s].index)
        only(falling, lambda s=s: add_into(below.at[s - 2], stage.at[1]))
        wires.start(below.at[s - 2], below.at[s - 1], wires.down, falling, None, downs[s].index)
    load = wires.local(p(0), stage.at[0])
    yield 1
    ups[nz - 1].wait_recv()
    downs[nz - 1].wait_recv()
    load.wait()
    only(z >= 1, lambda: add_into(stage.at[0], above.at[nz - 2]))
    only(z < nz - 1, lambda: add_into(stage.at[0], below.at[nz - 2]))
    kept = wires.local(stage.at[0], total)
    yield 1
    kept.wait()


def swap_rows(wires, total, got):
    n = got.shape[0]
    other = pl.ds(pl.multiple_of((1 - wires.at_y) * n, n), n)
    sent = wires.start(total.at[other], got, wires.y)
    yield 1
    sent.wait_recv()


def sum_scratch(nz, rows, cols):
    return [
        pltpu.VMEM((nz - 1, rows, cols), BF16),
        pltpu.VMEM((nz - 1, rows, cols), BF16),
        pltpu.VMEM((2, rows, cols), BF16),
    ]


def swap_outputs(*totals):
    return [jax.ShapeDtypeStruct((t.shape[0] // 2, t.shape[1]), BF16) for t in totals]


def columns(ref, rows, lo, hi):
    return lambda s: ref.at[pl.ds(s * rows, rows), lo:hi]


def gather_weight_rows(wires, sources, out, bounce=None):
    n = out.shape[0] // wires.nz
    slot = lambda s: out.at[pl.ds(s * n, n)]
    yield from exchange_halves(wires, sources, slot(0), bounce)
    yield from along_z(wires, slot(0), slot)


def gather_phase(wires, block, out, parts):
    views = [(pl.ds(lo, hi - lo), link) for lo, hi, link in parts]
    on_y = [v for v in views if v[1] == "x"] + [v for v in views if v[1] == "y"]
    on_x = on_y[::-1]
    mine = wires.local(block, out.at[0])
    from_y, from_x, diagonal = {}, {}, []
    c = [wires.start(block, out.at[1], wires.c)]
    for k, (rows, _) in enumerate(on_x):
        from_x[k] = wires.start(block.at[rows], out.at[2, rows], wires.x)
    yield 1
    for k, (rows, _) in enumerate(on_y):
        from_y[k] = wires.start(block.at[rows], out.at[4, rows], wires.y)
    yield 1
    for k in range(len(views)):
        for place, arrived, (rows, link), via, own in (
            (4, from_y[k], on_y[k], wires.x, "x"), (2, from_x[k], on_x[k], wires.y, "y"),
        ):
            arrived.wait_recv()
            if link == own:
                relay = wires.start(out.at[place, rows], out.at[6, rows], via)
                diagonal.append((relay, rows))
            c.append(wires.start(out.at[place, rows], out.at[place + 1, rows], wires.c))
        yield 1
    for relay, rows in diagonal:
        relay.wait_recv()
        c.append(wires.start(out.at[6, rows], out.at[7, rows], wires.c))
        yield 1
    for copy in c:
        copy.wait_recv()
    mine.wait()


def halved(n, cut=None):
    cut = n // 2 if cut is None else cut
    return [(0, cut, "x"), (cut, n, "y")]


def start_kernel(
    x_ref, dout_ref, gain_ref, qw_ref, kw_ref, vw_ref, ow_ref, ids_ref, rope_ref,
    x_own, dout_own, opack, cos_ref, sin_ref, first_ref, x_all, w_all,
    pack, send, recv, local,
):
    wires = Wires(send, recv, local)
    wires.hello()
    model = x_ref.shape[1]
    turns = rotation(wires, model)
    at = qw_ref.shape[1] // 2
    for h in range(2):
        pack[h, :, 0:at] = qw_ref[:, h * at : (h + 1) * at]
    for ref in (kw_ref, vw_ref):
        n = ref.shape[0] // 2
        eye = identity(n)
        for h in range(2):
            pack[h, :, at : at + n] = tn(ref[h * n : (h + 1) * n, :], eye).astype(BF16)
        at += n
    rest = pack.shape[2] - at
    row = lax.broadcasted_iota(jnp.int32, (2, rest), 0)
    lane = lax.broadcasted_iota(jnp.int32, (2, rest), 1)
    tail = tn(gain_ref[...], (row == lane).astype(BF16)).astype(BF16)
    for h in range(2):
        pack[h, :, at:] = tail
    wires.ready()
    weights = gather_weight_rows(wires, [(lambda y: pack.at[y], 0, pack.shape[2])], w_all)
    run(weights)
    for to, of in turns:
        x_own[:, to] = x_ref[:, of]
    tokens = gather_phase(wires, x_own, x_all, halved(x_own.shape[0], START_CUT))
    run(tokens)
    run(weights)
    run(tokens)
    for to, of in turns:
        dout_own[:, to] = dout_ref[:, of]
    run(tokens)
    n = ow_ref.shape[1] // 2
    for h in range(2):
        opack[h] = ow_ref[:, h * n : (h + 1) * n]
    run(weights)
    run(tokens)
    length = first_ref.shape[1]
    lane = lax.broadcasted_iota(jnp.int32, (1, LANES), 1)
    sign = jnp.where(lane < LANES // 2, -1.0, 1.0)
    steps = length // ROPE_STEP
    cos_low, sin_low = rope_ref[0, steps:, :], rope_ref[1, steps:, :]
    for t in range(steps):
        part = slice(t * ROPE_STEP, (t + 1) * ROPE_STEP)
        cos_high, sin_high = rope_ref[0, t : t + 1, :], rope_ref[1, t : t + 1, :]
        cos_ref[part, :] = cos_high * cos_low - sin_high * sin_low
        sin_ref[part, :] = (sin_high * cos_low + cos_high * sin_low) * sign
    offset = pl.multiple_of(wires.at_z * length, length)
    ids = ids_ref[:, pl.ds(offset, length)]
    begin = jnp.zeros((1, length), jnp.int32)
    for number in range(1, 5):
        count = jnp.sum((ids_ref[...] < number).astype(jnp.int32), axis=1, keepdims=True)
        begin = jnp.where(ids >= number, count, begin)
    window = lax.broadcasted_iota(jnp.int32, (1, length), 1) - (WINDOW_LENGTH - 1)
    first_ref[...] = jnp.maximum(begin - offset, window) + WINDOW_LENGTH
    drain(weights, tokens)
    wires.finish()


START_CUT = 160


def gather_start(inputs, dout, gains, query, key_t, value_t, out_t, ids, rope, width):
    n, model = inputs.shape
    rows = query.shape[0]
    length = 8 * n
    return pl.pallas_call(
        start_kernel,
        in_specs=[WHOLE] * 9,
        out_specs=[WHOLE] * 6 + [HBM] * 2,
        out_shape=[
            jax.ShapeDtypeStruct((n, model), BF16),
            jax.ShapeDtypeStruct((n, model), BF16),
            jax.ShapeDtypeStruct((2, rows, out_t.shape[1] // 2), BF16),
            jax.ShapeDtypeStruct((length, LANES), F32),
            jax.ShapeDtypeStruct((length, LANES), F32),
            jax.ShapeDtypeStruct((1, length), jnp.int32),
            jax.ShapeDtypeStruct((8, n, model), BF16),
            jax.ShapeDtypeStruct((model, width), BF16),
        ],
        scratch_shapes=[pltpu.VMEM((2, rows, width), BF16)] + semaphores(),
        compiler_params=params(62, collective_id=0, has_side_effects=True),
        name="gather_start",
        **light(),
    )(inputs, dout, gains, query, key_t, value_t, out_t, ids, rope)


def feed_sources(gate, up, down, cut, hidden):
    a, b = cut
    n = b - a
    step = LANES

    def pick(ref):
        return lambda y: ref.at[:, pl.ds(pl.multiple_of(y * hidden + a, step), n)]

    return [(pick(ref), k * n, (k + 1) * n) for k, ref in enumerate((gate, up, down))]


def attention_kernel(
    hidden, cuts,
    x_ref, w_ref, spread_ref, squeeze_ref, cos_ref, sin_ref, first_ref, dout_ref,
    opack_ref, gate_ref, up_ref, down_ref,
    q_ref, k_ref, v_ref, o_ref, lse_ref, gain_ref, a1_ref, dout_all, w_out, w_zero, *rest,
):
    slots, rest = rest[: len(cuts) - 1], rest[len(cuts) - 1 :]
    x_all, w_flat, w_pad, bounce_out, *bounces, send, recv, local = rest
    wires = Wires(send, recv, local)
    nz, z = wires.nz, wires.at_z
    rows = x_all.shape[1]
    model = x_all.shape[2]
    heads = q_ref.shape[1] // LANES
    keys = rows + WINDOW_LENGTH
    length = 8 * rows
    wires.greet()
    load_w = wires.local(w_ref, w_flat)
    order = (6, 7, 0, 1, 2, 3, 4, 5)
    loads = {}
    for b in order:
        at = wires.natural(b)
        loads[b] = wires.local(x_ref.at[at], x_all.at[at])
    out_weights = gather_weight_rows(
        wires, [(lambda y: opack_ref.at[y], 0, opack_ref.shape[2])], w_out, bounce_out
    )
    run(out_weights)
    quarter = rows // 4
    cotangents = gather_phase(
        wires, dout_ref, dout_all, [(t * quarter, (t + 1) * quarter, "x") for t in range(4)]
    )
    run(cotangents)
    load_w.wait()

    @pl.loop(0, model // 512)
    def _(t):
        part = pl.ds(pl.multiple_of(t * 512, 512), 512)
        w_pad[part, :] = nn(w_flat[part, :], spread_ref[...]).astype(BF16)

    zero_weights = gather_weight_rows(
        wires, feed_sources(gate_ref, up_ref, down_ref, cuts[0], hidden), w_zero, bounces[0]
    )
    run(zero_weights)
    run(out_weights)
    place = lax.broadcasted_iota(jnp.int32, (8, w_flat.shape[1]), 1)
    row = lax.broadcasted_iota(jnp.int32, (8, w_flat.shape[1]), 0)
    which = (place == (heads + 2) * HEAD_SIZE + row).astype(BF16)
    gain_ref[...] = nt(which, w_flat[...])
    gain = gain_ref[0:1, :]

    @pl.when(z == 0)
    def _():
        k_ref[0:WINDOW_LENGTH, :] = jnp.zeros((WINDOW_LENGTH, LANES), BF16)
        v_ref[0:WINDOW_LENGTH, :] = jnp.zeros((WINDOW_LENGTH, LANES), BF16)

    stores = []
    for b in order:
        at = wires.natural(b)
        loads[b].wait()
        x = x_all[at].astype(F32)
        inverse = lax.rsqrt(jnp.mean(x * x, axis=1, keepdims=True) + EPS)
        a1 = (x * inverse * gain).astype(BF16)
        x_all[at] = a1
        stores.append(wires.local(x_all.at[at], a1_ref.at[at]))
        acc = nn(a1, w_pad[...])
        here = slice(b * rows, (b + 1) * rows)
        there = slice(WINDOW_LENGTH + b * rows, WINDOW_LENGTH + (b + 1) * rows)
        cosine, sine = cos_ref[here, :], sin_ref[here, :]
        for h in range(heads + 1):
            u = acc[:, h * LANES : (h + 1) * LANES]
            turned = (u * cosine + pltpu.roll(u, LANES // 2, 1) * sine).astype(BF16)
            if h < heads:
                q_ref[here, h * LANES : (h + 1) * LANES] = turned
            else:
                k_ref[there, :] = turned
        v_ref[there, :] = acc[:, (heads + 1) * LANES :].astype(BF16)
        if b == 7:
            halo = [
                wires.start(
                    ref.at[pl.ds(length, WINDOW_LENGTH)], ref.at[pl.ds(0, WINDOW_LENGTH)],
                    wires.up, z < nz - 1, z > 0,
                )
                for ref in (k_ref, v_ref)
            ]
        if b == 0:
            run(zero_weights)
            run(cotangents)
        if b == 2:
            run(out_weights)
    for copy in halo:
        copy.wait_recv()

    def block(b, at):
        start = pl.multiple_of(b * rows, rows)
        span = pl.ds(start, keys)
        here = pl.ds(start, rows)
        kb = k_ref[span, :]
        vt = v_ref[span, :].T
        bias = mask_bias(first_ref[:, here] - start, keys, rows)
        outs = []
        for h in range(heads):
            lanes = slice(h * LANES, (h + 1) * LANES)
            s = nt(kb, q_ref[here, lanes]) * (SCALE * LOG2E) + bias
            peak = jnp.max(s, axis=0, keepdims=True)
            p = jnp.exp2(s - peak)
            total = jnp.sum(p, axis=0, keepdims=True)
            ot = nn(vt, p.astype(BF16)) / total
            outs.append(ot.T.astype(BF16))
            lse_ref[b, h : h + 1, :] = peak + jnp.log2(total)
        o_ref[at] = nn(jnp.concatenate(outs, 1), squeeze_ref[...]).astype(BF16)

    def blocks(lo, hi):
        @pl.loop(lo, hi)
        def _(b):
            block(b, wires.natural(b))

    run(zero_weights)
    run(cotangents)
    run(cotangents)
    blocks(0, 2)
    run(out_weights)
    run(cotangents)
    blocks(2, 4)
    run(cotangents)
    run(zero_weights)
    exchanges = [
        exchange_halves(
            wires, feed_sources(gate_ref, up_ref, down_ref, cut, hidden), slot, bounce
        )
        for cut, slot, bounce in zip(cuts[1:], slots, bounces[1:])
    ]
    run(exchanges[0])
    blocks(4, 6)
    for exchange in exchanges[1:]:
        run(exchange)
    blocks(6, 8)
    for store in stores:
        store.wait()
    drain(out_weights, zero_weights, cotangents, *exchanges)
    wires.finish()


def attention(x_all, w_attn, cosine, sine, first_key, dout, opack, gate, up, down, heads, cuts):
    _, n, model = x_all.shape
    length = 8 * n
    hidden = gate.shape[1] // 2
    wide = heads * LANES
    spread = spread_matrix(heads + 1, 1, rows=w_attn.shape[1])
    squeeze = spread_matrix(0, heads).T
    slot = 2 * gate.shape[0]
    sizes = [3 * (b - a) for a, b in cuts]
    return pl.pallas_call(
        functools.partial(attention_kernel, hidden, cuts),
        in_specs=[HBM, HBM] + [WHOLE] * 6 + [HBM] * 4,
        out_specs=[WHOLE] * 6 + [HBM] * (3 + len(cuts)),
        out_shape=[
            jax.ShapeDtypeStruct((length, wide), BF16),
            jax.ShapeDtypeStruct((length + WINDOW_LENGTH, LANES), BF16),
            jax.ShapeDtypeStruct((length + WINDOW_LENGTH, LANES), BF16),
            jax.ShapeDtypeStruct((8, n, heads * HEAD_SIZE), BF16),
            jax.ShapeDtypeStruct((8, heads, n), F32),
            jax.ShapeDtypeStruct((8, model), F32),
            jax.ShapeDtypeStruct((8, n, model), BF16),
            jax.ShapeDtypeStruct((8, n, model), BF16),
            jax.ShapeDtypeStruct((model, opack.shape[2]), BF16),
            jax.ShapeDtypeStruct((model, sizes[0]), BF16),
        ]
        + [jax.ShapeDtypeStruct((slot, size), BF16) for size in sizes[1:]],
        scratch_shapes=[
            pltpu.VMEM((8, n, model), BF16),
            pltpu.VMEM(w_attn.shape, BF16),
            pltpu.VMEM((model, spread.shape[1]), BF16),
            pltpu.VMEM(opack.shape[1:], BF16),
        ]
        + [pltpu.VMEM((gate.shape[0], size), BF16) for size in sizes]
        + semaphores(),
        compiler_params=params(62, collective_id=5, has_side_effects=True),
        name="attention",
        **light(),
    )(x_all, w_attn, spread, squeeze, cosine, sine, first_key, dout, opack, gate, up, down)


def project_kernel(
    a_ref, w_ref, x_ref, gain_ref, slot_ref, res_ref, inv_ref, out_ref, w_all,
    block, cs, cr, q, xr, yr, tr, br, send, recv, local,
):
    wires = Wires(send, recv, local)
    wires.greet()
    n = slot_ref.shape[0]
    own = wires.local(slot_ref, w_all.at[pl.ds(0, n)])
    weights = along_z(wires, slot_ref, lambda s: w_all.at[pl.ds(s * n, n)])
    run(weights)

    def emit(rows, total):
        residual = x_ref[rows, :].astype(F32) + total
        inverse = lax.rsqrt(jnp.mean(residual * residual, axis=1, keepdims=True) + EPS)
        res_ref[rows, :] = residual
        inv_ref[rows, :] = inverse
        block[rows, :] = (residual * inverse * gain_ref[1:2, :]).astype(BF16)

    sums = reduce_phase(wires, a_ref, w_ref, cs, cr, q, xr, yr, tr, br, emit)
    for _ in range(6):
        run(sums)
    run(weights)
    drain(sums)
    tokens = gather_phase(wires, block, out_ref, halved(block.shape[0]))
    run(tokens)
    run(tokens)
    run(tokens)
    run(weights)
    drain(tokens, weights)
    own.wait()
    wires.finish()


def project_out(o, w_out, inputs, gain, slot):
    n, model = inputs.shape
    return pl.pallas_call(
        project_kernel,
        in_specs=[WHOLE] * 5,
        out_specs=[WHOLE, WHOLE, HBM, HBM],
        out_shape=[
            jax.ShapeDtypeStruct((n, model), F32),
            jax.ShapeDtypeStruct((n, 1), F32),
            jax.ShapeDtypeStruct((8, n, model), BF16),
            jax.ShapeDtypeStruct((model, slot.shape[1]), BF16),
        ],
        scratch_shapes=[pltpu.VMEM((n, model), BF16)] + reduce_scratch(n, model) + semaphores(),
        compiler_params=params(62, collective_id=2, has_side_effects=True),
        name="project_out",
        **light(),
    )(o, w_out, inputs, gain, slot)


def feed_kernel(
    hidden, cuts, chunks,
    a_ref, d_ref, w0_ref, w1_ref, w2_ref, w3_ref,
    m_ref, g_ref, w_ref, grad0, grad1, grad2, grad3, total,
    a, d, w, m, g, stage, above, below, extra, send, recv, local,
):
    wires = Wires(send, recv, local)
    nz = wires.nz
    length, model = a.shape
    slot = model // nz
    wires.hello()

    def spots(lo, hi):
        out = []
        for k in range(3):
            for first, last in chunks:
                left, right = max(lo, first), min(hi, last)
                if left < right:
                    base = 2 * hidden if k == 2 else first + k * (last - first)
                    start = base + left
                    out.append((k * (hi - lo) + left - lo, start, right - left, k, left))
        return out

    loads = []
    for ref, (lo, hi) in ((w0_ref, cuts[0]), (w1_ref, cuts[1])):
        for of, to, n, _, _ in spots(lo, hi):
            loads.append(wires.local(ref.at[:, of : of + n], w.at[:, to : to + n]))
    rows = length // 8
    a_loads, d_loads = [], []

    def fetch(half):
        part = pl.ds(half * 4 * rows, 4 * rows)
        a_loads.append(wires.local(a_ref.at[part], a.at[part]))
        d_loads.append(wires.local(d_ref.at[part], d.at[part]))

    fetch(0)

    def carried(ref, cut):
        pieces, copies = [], []
        for of, to, n, _, _ in spots(*cut):
            pieces.append((to, to + n))
            copies.append(wires.local(ref.at[:, of : of + n], w.at[pl.ds(0, slot), to : to + n]))
        yield 1
        for copy in copies:
            copy.wait()
        hops = [
            along_z(
                wires,
                w.at[pl.ds(0, slot), lo:hi],
                lambda s, lo=lo, hi=hi: w.at[pl.ds(s * slot, slot), lo:hi],
            )
            for lo, hi in pieces
        ]
        while hops:
            hops = [hop for hop in hops if next(hop, None) is not None]
            yield 1

    later = [carried(ref, cut) for ref, cut in zip((w2_ref, w3_ref), cuts[2:])]
    for part in later:
        run(part)
    wires.ready()
    run(later[0])
    for copy in loads:
        copy.wait()

    def units(lo, hi, blocks):
        n = hi - lo

        @pl.loop(*blocks)
        def _(b):
            part = pl.ds(pl.multiple_of(b * rows, rows), rows)
            both = nn(a[part, :], w[:, 2 * lo : 2 * hi])
            gate, up = both[:, :n], both[:, n:]
            dmixed = nn(d[part, :], w[:, 2 * hidden + lo : 2 * hidden + hi])
            sigma = jax.nn.sigmoid(gate)
            silu = gate * sigma
            m[part, lo:hi] = (silu * up).astype(BF16)
            g[part, lo + hi : 2 * hi] = (dmixed * silu).astype(BF16)
            g[part, 2 * lo : lo + hi] = (
                dmixed * up * sigma * (1.0 + gate * (1.0 - sigma))
            ).astype(BF16)

    tile = stage.shape[1]
    last = model // tile

    def weight_grads(lo, hi, out, tiles=None):
        n = hi - lo
        tiles = (0, last) if tiles is None else tiles

        def save(t):
            return pltpu.make_async_copy(
                stage.at[t % 2, :, 0 : 3 * n],
                out.at[pl.ds(pl.multiple_of(t * tile, tile), tile)],
                local.at[SEMAPHORES - 1 - t % 2],
            )

        @pl.loop(*tiles)
        def _(t):
            @pl.when(t >= 2)
            def _():
                save(t - 2).wait()

            cols = pl.ds(pl.multiple_of(t * tile, tile), tile)
            stage[t % 2, :, 0 : 2 * n] = tn(a[:, cols], g[:, 2 * lo : 2 * hi]).astype(BF16)
            stage[t % 2, :, 2 * n : 3 * n] = tn(d[:, cols], m[:, lo:hi]).astype(BF16)
            save(t).start()

        if tiles[1] == last:
            save(last - 2).wait()
            save(last - 1).wait()

    a_loads[0].wait()
    d_loads[0].wait()
    fetch(1)
    units(*chunks[0], (0, 4))
    a_loads[1].wait()
    d_loads[1].wait()
    units(*chunks[0], (4, 8))
    weight_grads(*chunks[0], grad0, (0, 2))
    run(later[0])
    weight_grads(*chunks[0], grad0, (2, last))
    sums = sum_along_z(
        wires, columns(grad0, slot, 0, total.shape[1]), above, below, extra, total
    )
    run(sums)
    units(*chunks[1], (0, 8))
    run(later[0])
    weight_grads(*chunks[1], grad1, (0, 4))
    run(sums)
    run(later[1])
    weight_grads(*chunks[1], grad1, (4, last))
    drain(later[0])
    units(*chunks[2], (0, 4))
    run(later[1])
    run(sums)
    units(*chunks[2], (4, 8))
    weight_grads(*chunks[2], grad2, (0, 2))
    run(later[1])
    weight_grads(*chunks[2], grad2, (2, last))
    drain(later[1])
    outs = [wires.local(w, w_ref)]
    units(*chunks[3], (0, 8))
    outs += [wires.local(m, m_ref), wires.local(g, g_ref)]
    run(sums)
    weight_grads(*chunks[3], grad3)
    drain(sums)
    for copy in outs:
        copy.wait()
    wires.finish()


def feed_forward(a2, dout, w0, w1, w2, w3, cuts, chunks):
    length, model = a2.shape
    hidden = cuts[-1][1]
    sizes = [b - a for a, b in chunks]
    rows = w3.shape[0]
    nz = model // rows
    return pl.pallas_call(
        functools.partial(feed_kernel, hidden, cuts, chunks),
        in_specs=[HBM] * 6,
        out_specs=[HBM] * 8,
        out_shape=[
            jax.ShapeDtypeStruct((length, hidden), BF16),
            jax.ShapeDtypeStruct((length, 2 * hidden), BF16),
            jax.ShapeDtypeStruct((model, 3 * hidden), BF16),
        ]
        + [jax.ShapeDtypeStruct((model, 3 * n), BF16) for n in sizes]
        + [jax.ShapeDtypeStruct((rows, 3 * sizes[0]), BF16)],
        scratch_shapes=[
            pltpu.VMEM((length, model), BF16),
            pltpu.VMEM((length, model), BF16),
            pltpu.VMEM((model, 3 * hidden), BF16),
            pltpu.VMEM((length, hidden), BF16),
            pltpu.VMEM((length, 2 * hidden), BF16),
            pltpu.VMEM((2, 512, 3 * max(sizes)), BF16),
        ]
        + sum_scratch(nz, rows, 3 * sizes[0])
        + semaphores(),
        compiler_params=params(62, collective_id=1, has_side_effects=True),
        name="feed_forward",
        **light(),
    )(a2, dout, w0, w1, w2, w3)


def reduce_phase(wires, a, w, cs, cr, q, xr, yr, tr, br, emit, ready=None):
    n = q.shape[1]
    half = n // 2
    top, bottom = pl.ds(0, half), pl.ds(half, half)
    model = q.shape[2]
    tile = 512
    deep = a.shape[2]

    def product(place, target):
        if ready is not None:
            ready(place)

        @pl.loop(0, model // tile)
        def _(t):
            cols = pl.ds(pl.multiple_of(t * tile, tile), tile)
            target[:, cols] = nt(a[place], w[cols, 0:deep]).astype(BF16)

    waits = {}
    for j in (3, 1, 2, 0):
        product(2 * j + 1, cs.at[j])
        got = wires.start(cs.at[j], cr.at[j], wires.c)
        product(2 * j, q.at[j])
        got.wait_recv()
        q[j] = (q[j].astype(F32) + cr[j].astype(F32)).astype(BF16)
        if j == 3:
            waits["x1"] = wires.start(q.at[3, top], xr.at[1], wires.x)
            waits["y1"] = wires.start(q.at[3, bottom], yr.at[1], wires.y)
        if j == 1:
            waits["x0"] = wires.start(q.at[1, top], xr.at[0], wires.x)
        if j == 2:
            waits["y0"] = wires.start(q.at[2, bottom], yr.at[0], wires.y)
        yield 1
    waits["x1"].wait_recv()
    q[2, top] = (q[2, top].astype(F32) + xr[1].astype(F32)).astype(BF16)
    waits["t"] = wires.start(q.at[2, top], tr, wires.y)
    waits["y1"].wait_recv()
    q[1, bottom] = (q[1, bottom].astype(F32) + yr[1].astype(F32)).astype(BF16)
    waits["b"] = wires.start(q.at[1, bottom], br, wires.x)
    yield 1
    waits["x0"].wait_recv()
    yield 1
    waits["t"].wait_recv()
    emit(top, q[0, top].astype(F32) + xr[0].astype(F32) + tr[...].astype(F32))
    waits["y0"].wait_recv()
    waits["b"].wait_recv()
    emit(bottom, q[0, bottom].astype(F32) + yr[0].astype(F32) + br[...].astype(F32))


def reduce_scratch(n, model):
    half = n // 2
    return [
        pltpu.VMEM((4, n, model), BF16),
        pltpu.VMEM((4, n, model), BF16),
        pltpu.VMEM((4, n, model), BF16),
        pltpu.VMEM((2, half, model), BF16),
        pltpu.VMEM((2, half, model), BF16),
        pltpu.VMEM((half, model), BF16),
        pltpu.VMEM((half, model), BF16),
    ]


def middle_kernel(
    a_ref, w_ref, dout_ref, res_ref, inv_ref, gain_ref, grad0, grad2,
    dres_ref, out_ref, total0, total2,
    a, w, block, cs, cr, q, xr, yr, tr, br,
    above0, below0, stage0, above2, below2, stage2, send, recv, local,
):
    wires = Wires(send, recv, local)
    wires.hello()
    load_w = wires.local(w_ref.at[:, 0 : w.shape[1]], w)
    loads = {place: wires.local(a_ref.at[place], a.at[place]) for place in (7, 6, 3, 2, 5, 4, 1, 0)}
    wires.ready()
    rows = total0.shape[0]
    first = sum_along_z(
        wires, columns(grad0, rows, 0, total0.shape[1]), above0, below0, stage0, total0
    )
    second = sum_along_z(
        wires, columns(grad2, rows, 0, total2.shape[1]), above2, below2, stage2, total2
    )
    run(first)

    def emit(rows, total):
        inverse = inv_ref[rows, :]
        normed = res_ref[rows, :] * inverse
        e = total * gain_ref[1:2, :]
        back = inverse * (e - normed * jnp.mean(e * normed, axis=1, keepdims=True))
        dres = dout_ref[rows, :].astype(F32) + back
        dres_ref[rows, :] = dres
        block[rows, :] = dres.astype(BF16)

    load_w.wait()
    sums = reduce_phase(
        wires, a, w, cs, cr, q, xr, yr, tr, br, emit, lambda place: loads[place].wait()
    )
    for _ in range(4):
        run(sums)
    run(first)
    run(sums)
    run(sums)
    run(first)
    drain(sums)
    tokens = gather_phase(wires, block, out_ref, halved(block.shape[0], BACK_CUT))
    run(tokens)
    run(tokens)
    run(first)
    run(second)
    run(tokens)
    run(second)
    run(tokens)
    run(second)
    drain(tokens, second, first)
    wires.finish()


BACK_CUT = 208


def feed_back(dgu, w, dout, residual, inverse, gain, grad0, grad2):
    n, model = dout.shape
    k = dgu.shape[1]
    rows = 2 * model // lax.axis_size("tok")
    nz = model // rows
    half, small = grad0.shape[1], grad2.shape[1]
    return pl.pallas_call(
        middle_kernel,
        in_specs=[HBM] * 2 + [WHOLE] * 4 + [HBM] * 2,
        out_specs=[WHOLE] + [HBM] * 3,
        out_shape=[
            jax.ShapeDtypeStruct((n, model), F32),
            jax.ShapeDtypeStruct((8, n, model), BF16),
            jax.ShapeDtypeStruct((rows, half), BF16),
            jax.ShapeDtypeStruct((rows, small), BF16),
        ],
        scratch_shapes=[
            pltpu.VMEM((8, n, k), BF16),
            pltpu.VMEM((model, k), BF16),
            pltpu.VMEM((n, model), BF16),
        ]
        + reduce_scratch(n, model)
        + sum_scratch(nz, rows, half)
        + sum_scratch(nz, rows, small)
        + semaphores(),
        compiler_params=params(62, collective_id=3, has_side_effects=True),
        name="feed_back",
        **light(),
    )(dgu.reshape(8, n, k), w, dout, residual, inverse, gain, grad0, grad2)


def back_kernel(
    da_ref, w_ref, o_ref, q_ref, k_ref, v_ref, lse_ref, first_ref, cos_ref, sin_ref,
    spread_ref, squeeze_ref, final_ref, m_ref, down_ref, res_ref, grad1, sum0, sum1, sum2,
    dqkv_ref, out_ref, grad_out, total, got0, got1, got2,
    da, do, dk, dv, halo, fetched, m, w_down, cr, xr, yr, tr, br,
    above, below, stage, stage1, res, send, recv, local,
):
    wires = Wires(send, recv, local)
    nz, z = wires.nz, wires.at_z
    wires.hello()
    n, model = da.shape[1], da.shape[2]
    heads = q_ref.shape[1] // LANES
    wide = heads * HEAD_SIZE
    keys = n + WINDOW_LENGTH
    length = 8 * n
    loads = [wires.local(da_ref.at[b], da.at[b]) for b in range(8)]
    late = [
        wires.local(m_ref, m),
        wires.local(down_ref.at[:, 2 * m.shape[2] :], w_down),
    ]
    rows = total.shape[0]
    wires.ready()
    carried = sum_along_z(
        wires, columns(grad1, rows, 0, total.shape[1]), above, below, stage, total
    )
    run(carried)
    swaps = [
        swap_rows(wires, s, got) for s, got in ((sum0, got0), (sum1, got1), (sum2, got2))
    ]
    for swap in swaps:
        run(swap)
    dk[...] = jnp.zeros_like(dk)
    dv[...] = jnp.zeros_like(dv)
    for b in range(8):
        loads[b].wait()
        flat = nn(da[b], w_ref[...]).astype(BF16)
        do[b] = nn(flat, spread_ref[...]).astype(BF16)

    saves = []
    for t in range(nz):
        cols = slice(t * rows, (t + 1) * rows)
        if t >= 2:
            saves[t - 2].wait()
        total = None
        for b in range(8):
            part = tn(da[b, :, cols], o_ref[b])
            total = part if total is None else total + part
        stage1[t % 2] = total.astype(BF16)
        saves.append(wires.local(stage1.at[t % 2], grad_out.at[pl.ds(t * rows, rows)]))
    for save in saves[-2:]:
        save.wait()
    for load in late:
        load.wait()
    turns = rotation(wires, model)

    def emit(part, total):
        load = wires.local(res_ref.at[part], res)
        load.wait()
        layer = (res[...] + total).astype(BF16)
        for of, to in turns:
            out_ref[part, to] = layer[:, of]

    sums = reduce_phase(
        wires, m, w_down, da.at[pl.ds(0, 4)], cr, da.at[pl.ds(4, 4)], xr, yr, tr, br, emit
    )
    run(sums)
    run(sums)
    run(carried)
    run(sums)
    run(sums)

    def block(b, at):
        start = pl.multiple_of(b * n, n)
        span = pl.ds(start, keys)
        here = pl.ds(start, n)
        kb = k_ref[span, :]
        vb = v_ref[span, :]
        kt = kb.T
        bias = mask_bias(first_ref[:, here] - start, keys, n)
        cosine, sine = cos_ref[here, :], sin_ref[here, :]
        dqs = []
        dk_sum = dv_sum = None
        for h in range(heads):
            lanes = slice(h * LANES, (h + 1) * LANES)
            qh = q_ref[here, lanes]
            doh = do[at, :, lanes]
            p = jnp.exp2(nt(kb, qh) * (SCALE * LOG2E) + (bias - lse_ref[b, h : h + 1, :]))
            t = p * nt(vb, doh)
            inner = jnp.sum(t, axis=0, keepdims=True)
            ds = (t - p * inner).astype(BF16)
            dq = nn(kt, ds).T * SCALE
            dqs.append((dq * cosine - pltpu.roll(dq, LANES // 2, 1) * sine).astype(BF16))
            dk_h = nn(ds, qh)
            dv_h = nn(p.astype(BF16), doh)
            dk_sum = dk_h if dk_sum is None else dk_sum + dk_h
            dv_sum = dv_h if dv_sum is None else dv_sum + dv_h
        dqkv_ref[at, :, 0:wide] = nn(jnp.concatenate(dqs, 1), squeeze_ref[...]).astype(BF16)
        dk[span, :] += dk_sum
        dv[span, :] += dv_sum

    def blocks(lo, hi):
        @pl.loop(lo, hi)
        def _(b):
            block(b, wires.natural(b))

    blocks(0, 2)
    halo[:, 0:LANES] = dk[0:WINDOW_LENGTH, :].astype(BF16)
    halo[:, LANES:] = dv[0:WINDOW_LENGTH, :].astype(BF16)
    borrowed = wires.start(halo, fetched, wires.down, z >= 1, z < nz - 1)
    run(sums)
    blocks(2, 4)
    run(carried)
    blocks(4, 8)
    drain(sums)
    borrowed.wait_recv()

    @pl.when(z < nz - 1)
    def _():
        dk[length:, :] += fetched[:, 0:LANES].astype(F32)
        dv[length:, :] += fetched[:, LANES:].astype(F32)

    for b in range(8):
        here = slice(b * n, (b + 1) * n)
        there = slice(WINDOW_LENGTH + b * n, WINDOW_LENGTH + (b + 1) * n)
        dkb = dk[there, :] * SCALE
        dkb = dkb * cos_ref[here, :] - pltpu.roll(dkb, LANES // 2, 1) * sin_ref[here, :]
        both = jnp.concatenate([dkb.astype(BF16), dv[there, :].astype(BF16)], 1)
        dqkv_ref[wires.natural(b), :, wide:] = nn(both, final_ref[...]).astype(BF16)
    drain(carried, *swaps)
    wires.finish()


def attention_back(
    da_all, w_out, o, q, k_all, v_all, lse, first_key, cosine, sine, mixed, w_feed, residual, grad1,
    sums, width,
):
    _, n, model = da_all.shape
    length = 8 * n
    heads = q.shape[1] // LANES
    wide = heads * HEAD_SIZE
    spread = spread_matrix(0, heads)
    squeeze = spread_matrix(heads, 0).T
    final = spread_matrix(1, 1, rows=width - wide).T
    rows = 2 * model // lax.axis_size("tok")
    nz = model // rows
    hidden = mixed.shape[1]
    half = n // 2
    return pl.pallas_call(
        back_kernel,
        in_specs=[HBM] + [WHOLE] * 12 + [HBM] * 7,
        out_specs=[WHOLE, WHOLE] + [HBM] * 5,
        out_shape=[
            jax.ShapeDtypeStruct((8, n, width), BF16),
            jax.ShapeDtypeStruct((n, model), BF16),
            jax.ShapeDtypeStruct((model, wide), BF16),
            jax.ShapeDtypeStruct((rows, grad1.shape[1]), BF16),
        ]
        + swap_outputs(*sums),
        scratch_shapes=[
            pltpu.VMEM((8, n, model), BF16),
            pltpu.VMEM((8, n, heads * LANES), BF16),
            pltpu.VMEM(k_all.shape, F32),
            pltpu.VMEM(k_all.shape, F32),
            pltpu.VMEM((WINDOW_LENGTH, 2 * LANES), BF16),
            pltpu.VMEM((WINDOW_LENGTH, 2 * LANES), BF16),
            pltpu.VMEM((8, n, hidden), BF16),
            pltpu.VMEM((model, hidden), BF16),
            pltpu.VMEM((4, n, model), BF16),
            pltpu.VMEM((2, half, model), BF16),
            pltpu.VMEM((2, half, model), BF16),
            pltpu.VMEM((half, model), BF16),
            pltpu.VMEM((half, model), BF16),
        ]
        + sum_scratch(nz, rows, grad1.shape[1])
        + [pltpu.VMEM((2, rows, wide), BF16), pltpu.VMEM((half, model), F32)]
        + semaphores(),
        compiler_params=params(63, collective_id=6, has_side_effects=True),
        name="attention_back",
        **light(),
    )(
        da_all, w_out, o, q, k_all, v_all, lse, first_key, cosine, sine, spread, squeeze, final,
        mixed.reshape(8, n, hidden), w_feed, residual, grad1, *sums,
    )


def last_kernel(
    a_ref, w_ref, x_ref, gain_ref, dres_ref, a1_ref, grad_out, sum0,
    out_ref, total, total1, got0, got, got1,
    cs, cr, q, xr, yr, tr, br, a1, grad, above, below, stage, above1, below1, stage1,
    send, recv, local,
):
    wires = Wires(send, recv, local)
    wires.hello()
    rows = total.shape[0]
    model = a1.shape[2]
    loads = [wires.local(a1_ref.at[b], a1.at[b]) for b in range(8)]
    turns = rotation(wires, model)

    def emit(rows, total):
        x = x_ref[rows, :].astype(F32)
        inverse = lax.rsqrt(jnp.mean(x * x, axis=1, keepdims=True) + EPS)
        normed = x * inverse
        e = total * gain_ref[0:1, :]
        back = inverse * (e - normed * jnp.mean(e * normed, axis=1, keepdims=True))
        done = dres_ref[rows, :] + back
        for of, to in turns:
            out_ref[rows, to] = done[:, of]

    wires.ready()
    first = sum_along_z(
        wires, columns(grad_out, rows, 0, total1.shape[1]), above1, below1, stage1, total1
    )
    run(first)
    swap = swap_rows(wires, sum0, got0)
    run(swap)
    for load in loads:
        load.wait()
    tile = 640

    def weight_grads(lo, hi):
        @pl.loop(lo, hi)
        def _(t):
            cols = pl.ds(pl.multiple_of(t * tile, tile), tile)
            total = None
            for b in range(8):
                part = tn(a1[b, :, cols], a_ref[b])
                total = part if total is None else total + part
            grad[cols, :] = total.astype(BF16)

    weight_grads(0, 2)
    run(first)
    weight_grads(2, 4)
    carried = sum_along_z(
        wires, columns(grad, rows, 0, total.shape[1]), above, below, stage, total
    )
    run(carried)
    sums = reduce_phase(wires, a_ref, w_ref, cs, cr, q, xr, yr, tr, br, emit)
    run(sums)
    run(sums)
    run(first)
    run(sums)
    run(sums)
    run(sums)
    run(carried)
    run(first)
    run(sums)
    run(carried)
    drain(sums)
    drain(first)
    first = swap_rows(wires, total1, got1)
    run(first)
    drain(carried)
    drain(swap_rows(wires, total, got), first, swap)
    wires.finish()


def input_back(dqkv, w, inputs, gain, dres, a1, grad_out, total):
    n, model = inputs.shape
    rows = 2 * model // lax.axis_size("tok")
    nz = model // rows
    wide = dqkv.shape[2]
    return pl.pallas_call(
        last_kernel,
        in_specs=[WHOLE] * 5 + [HBM] * 3,
        out_specs=[WHOLE] + [HBM] * 5,
        out_shape=[
            jax.ShapeDtypeStruct((n, model), F32),
            jax.ShapeDtypeStruct((rows, wide), BF16),
            jax.ShapeDtypeStruct((rows, grad_out.shape[1]), BF16),
            jax.ShapeDtypeStruct((rows // 2, total.shape[1]), BF16),
            jax.ShapeDtypeStruct((rows // 2, wide), BF16),
            jax.ShapeDtypeStruct((rows // 2, grad_out.shape[1]), BF16),
        ],
        scratch_shapes=reduce_scratch(n, model)
        + [pltpu.VMEM((8, n, model), BF16), pltpu.VMEM((model, wide), BF16)]
        + sum_scratch(nz, rows, wide)
        + sum_scratch(nz, rows, grad_out.shape[1])
        + semaphores(),
        compiler_params=params(62, collective_id=4, has_side_effects=True),
        name="input_back",
        **light(),
    )(dqkv, w, inputs, gain, dres, a1, grad_out, total)


def finish_kernel(
    chunks, y_ref, *refs,
):
    count = len(chunks) + 2
    mine, got = refs[0 : 2 * count : 2], refs[1 : 2 * count : 2]
    qw, kw, vw, gw, uw, layer, dinput = refs[2 * count : 2 * count + 7]
    gate, up, down, out, query, key, value, sums, row_sums, layer_out, dinput_out, local = refs[
        2 * count + 7 :
    ]
    copies = [
        pltpu.make_async_copy(layer, layer_out, local.at[0]),
        pltpu.make_async_copy(dinput, dinput_out, local.at[1]),
    ]
    for copy in copies:
        copy.start()
    rows = gate.shape[0]
    hidden = gate.shape[1] // 2
    eye = identity(rows)
    wide = lambda v: v.astype(F32)

    def place(h, pieces):
        for (lo, hi), piece in zip(chunks, pieces):
            n = hi - lo
            at = slice(h * hidden + lo, h * hidden + hi)
            for k, ref in enumerate((gate, up, down)):
                ref[:, at] = wide(piece[:, k * n : (k + 1) * n])
        o, q = pieces[-2:]
        for ref, piece in ((out, o), (query, q)):
            n = ref.shape[1] // 2
            ref[:, h * n : (h + 1) * n] = wide(piece[:, 0:n])
        start = query.shape[1] // 2
        for ref in (key, value):
            n = ref.shape[0] // 2
            ref[h * n : (h + 1) * n, :] = tn(q[:, start : start + n], eye)
            start += n

    @pl.when(y_ref[0] == 0)
    def _():
        place(0, [ref.at[0:rows] for ref in mine])
        place(1, got)

    @pl.when(y_ref[0] == 1)
    def _():
        place(0, got)
        place(1, [ref.at[rows:] for ref in mine])

    def total(w, g, axis):
        return jnp.sum(w[...].astype(F32) * g[...], axis=axis, keepdims=True)

    sums[:, 0:1] = total(qw, query, 1)
    sums[:, 1:2] = total(gw, gate, 1) + total(uw, up, 1)
    row_sums[...] = total(kw, key, 0) + total(vw, value, 0)
    for copy in copies:
        copy.wait()


def finish(y, pieces, weights, out_columns, chunks, layer, dinput):
    query, key_t, _, gate, _ = weights
    rows, hidden = gate.shape
    f32 = lambda *shape: jax.ShapeDtypeStruct(shape, F32)
    return pl.pallas_call(
        functools.partial(finish_kernel, chunks),
        in_specs=[pl.BlockSpec(memory_space=pltpu.SMEM)]
        + [WHOLE] * (len(pieces) + len(weights) + 2),
        out_specs=[WHOLE] * 9 + [HBM] * 2,
        out_shape=[
            f32(rows, hidden), f32(rows, hidden), f32(rows, hidden), f32(rows, out_columns),
            f32(*query.shape), f32(*key_t.shape), f32(*key_t.shape), f32(rows, 2), f32(1, rows),
            jax.ShapeDtypeStruct(layer.shape, layer.dtype),
            jax.ShapeDtypeStruct(dinput.shape, dinput.dtype),
        ],
        scratch_shapes=[pltpu.SemaphoreType.DMA((2,))],
        compiler_params=params(62),
        name="finish",
        **light(),
    )(y, *pieces, *weights, layer, dinput)


def body(
    inputs,
    grad_output,
    segments,
    attention_gain,
    query_weight,
    key_matrix,
    value_matrix,
    output_weight,
    feedforward_gain,
    gate_weight,
    up_weight,
    down_weight,
):
    grid = Grid()
    bf16 = jnp.bfloat16
    model = inputs.shape[1]
    length = inputs.shape[0] * 8
    hidden = gate_weight.shape[1] // 2
    qdim = query_weight.shape[1] // 2
    kdim = key_matrix.shape[1] // 2
    cuts = []
    at = 0
    for n in FF_CHUNKS:
        cuts.append((at, at + n))
        at += n
    heads = qdim // HEAD_SIZE

    width = -(-(qdim + 2 * kdim + 2) // LANES) * LANES

    down_t = down_weight.T
    own, dout, out_pack, cosine, sine, first_key, x_all, w_attn = gather_start(
        outside_rotation(grid, inputs), outside_rotation(grid, grad_output),
        jnp.stack([attention_gain, feedforward_gain]),
        query_weight, key_matrix.T, value_matrix.T, output_weight.T,
        segments[None, :], rope_parts(length, grid.z * length, HEAD_SIZE), width,
    )
    q, k_all, v_all, o, lse, gains, a1, dout_all, w_out, w_zero, *slots = attention(
        x_all, w_attn, cosine, sine, first_key, dout, out_pack, gate_weight, up_weight, down_t,
        heads, cuts,
    )
    flat = lambda v: v.reshape(length, v.shape[-1])
    residual, inverse_two, a2, w_one = project_out(o, w_out, own, gains, slots[0])

    chunks = []
    at = 0
    for n in FF_PARTS:
        chunks.append((at, at + n))
        at += n
    mixed, dgu, w_feed, grad0, grad1, grad2, grad3, sum_0 = feed_forward(
        flat(a2), flat(dout_all), w_zero, w_one, *slots[1:], cuts, chunks
    )
    dresidual, da_all, sum_1, sum_3 = feed_back(
        dgu, w_feed, dout, residual, inverse_two, gains, grad1, grad3
    )
    dqkv, layer, grad_o, sum_2, got_0, got_1, got_3 = attention_back(
        da_all, w_out, o, q, k_all, v_all, lse, first_key, cosine, sine, mixed, w_feed, residual,
        grad2, (sum_0, sum_1, sum_3), width,
    )
    dinput, sum_q, sum_o, got_2, got_q, got_o = input_back(
        dqkv, w_attn, own, gains, dresidual, a1, grad_o, sum_2
    )
    pieces = (
        sum_0, got_0, sum_1, got_1, sum_2, got_2, sum_3, got_3, sum_o, got_o, sum_q, got_q
    )
    (
        gate_grad, up_grad, down_grad, output_grad, query_grad, key_grad, value_grad, sums,
        row_sums, layer, dinput,
    ) = finish(
        jnp.reshape(grid.y, (1,)).astype(jnp.int32),
        pieces,
        (query_weight, key_matrix.T, value_matrix.T, gate_weight, up_weight),
        output_weight.shape[0],
        chunks,
        layer,
        dinput,
    )
    sums = jnp.stack([sums[:, 0] + row_sums[0], sums[:, 1]])
    sums = sums + grid.swap(sums, C)
    sums = sums + grid.swap(sums, X)
    return (
        outside_rotation(grid, layer),
        outside_rotation(grid, dinput),
        sums[0] / attention_gain.astype(jnp.float32),
        query_grad,
        key_grad.T,
        value_grad.T,
        output_grad.T,
        sums[1] / feedforward_gain.astype(jnp.float32),
        gate_grad,
        up_grad,
        down_grad.T,
    )


def solution(mesh):
    in_specs = (
        P(("tok", "mp"), None),
        P(("tok", "mp"), None),
        P(),
        P("tok"),
        P("tok", "mp"),
        P("tok", "mp"),
        P("tok", "mp"),
        P("mp", "tok"),
        P("tok"),
        P("tok", "mp"),
        P("tok", "mp"),
        P("mp", "tok"),
    )
    out_specs = (
        P(("tok", "mp"), None),
        P(("tok", "mp"), None),
        P("tok"),
        P("tok", "mp"),
        P("tok", "mp"),
        P("tok", "mp"),
        P("mp", "tok"),
        P("tok"),
        P("tok", "mp"),
        P("tok", "mp"),
        P("mp", "tok"),
    )
    return jax.shard_map(body, mesh=mesh, in_specs=in_specs, out_specs=out_specs, check_vma=False)
```

```python
import functools

import jax
import jax.numpy as jnp
import ml_dtypes
import numpy as np
from jax import lax
from jax.experimental import pallas as pl
from jax.experimental.pallas import tpu as pltpu
from jax.sharding import PartitionSpec as P

HEAD_SIZE = 80
WINDOW_LENGTH = 512
EPS = 1e-05
THETA = 1000000.0
FLOOR = -1e30
AXES = ("tok", "mp")
FF_CHUNKS = (128, 384, 256, 128)
FF_PARTS = (256, 256, 256, 128)


class Grid:
    def __init__(self):
        self.nz = lax.axis_size("tok") // 2
        tok = lax.axis_index("tok")
        mp = lax.axis_index("mp")
        self.z, self.y = tok // 2, tok % 2
        self.x, self.c = mp // 2, mp % 2
        self.me = self.y * 4 + self.x * 2 + self.c

    def pairs(self, move):
        out = []
        for z in range(self.nz):
            for g in range(8):
                target = move(z, g)
                if target is not None:
                    out.append((z * 8 + g, target[0] * 8 + target[1]))
        return out

    def swap(self, value, bit):
        return lax.ppermute(value, AXES, self.pairs(lambda z, g: (z, g ^ bit)))

    def ring(self, value):
        return lax.ppermute(value, AXES, self.pairs(lambda z, g: ((z + 1) % self.nz, g)))

    def step(self, value, d):
        def move(z, g):
            return (z + d, g) if 0 <= z + d < self.nz else None

        return lax.ppermute(value, AXES, self.pairs(move))


Y, X, C = 4, 2, 1


LANES = 128
SCALE = HEAD_SIZE ** (-0.5)
LOG2E = 1.4426950408889634
MIB = 1024 * 1024
BF16 = jnp.bfloat16
F32 = jnp.float32
HBM = pl.BlockSpec(memory_space=pl.ANY)
WHOLE = pl.BlockSpec(memory_space=pltpu.VMEM)
MESH = pl.DeviceIdType.MESH


def light(**kwargs):
    return dict(
        cost_estimate=pl.CostEstimate(flops=1000000, bytes_accessed=100000, transcendentals=0),
        **kwargs,
    )


def params(mib, **kwargs):
    return pltpu.CompilerParams(vmem_limit_bytes=mib * MIB, **kwargs)


ROPE_STEP = 64


def rope_parts(count, first, width):
    half = width // 2
    freqs = THETA ** (-(jnp.arange(half, dtype=jnp.int32).astype(F32) * 2.0 / width))
    high = first + ROPE_STEP * jnp.arange(count // ROPE_STEP, dtype=jnp.int32)
    places = jnp.concatenate([high, jnp.arange(ROPE_STEP, dtype=jnp.int32)]).astype(F32)
    blank = jnp.zeros((LANES // 2 - half,), F32)
    lanes = jnp.concatenate([freqs, blank, freqs, blank])
    angles = places[:, None] * lanes[None, :]
    return jnp.stack([jnp.cos(angles), jnp.sin(angles)])


def spread_matrix(turned, plain, rows=0, columns=0):
    half = HEAD_SIZE // 2
    f = np.arange((turned + plain) * HEAD_SIZE)
    head, place = f // HEAD_SIZE, f % HEAD_SIZE
    target = head * LANES + place
    target = target + np.where((head < turned) & (place >= half), LANES // 2 - half, 0)
    out = np.zeros(
        (max(rows, f.size), max(columns, (turned + plain) * LANES)), ml_dtypes.bfloat16
    )
    out[f, target] = 1
    return out


def nt(left, right):
    return lax.dot_general(left, right, (((1,), (1,)), ((), ())), preferred_element_type=F32)


def nn(left, right):
    return lax.dot_general(left, right, (((1,), (0,)), ((), ())), preferred_element_type=F32)


def tn(left, right):
    return lax.dot_general(left, right, (((0,), (0,)), ((), ())), preferred_element_type=F32)


def mask_bias(first, keys, rows):
    kk = lax.broadcasted_iota(jnp.int32, (keys, rows), 0)
    qq = lax.broadcasted_iota(jnp.int32, (keys, rows), 1)
    return jnp.where((kk >= first) & (kk - qq <= WINDOW_LENGTH), 0.0, FLOOR)


def identity(n):
    i = lax.broadcasted_iota(jnp.int32, (n, n), 0)
    return (i == lax.broadcasted_iota(jnp.int32, (n, n), 1)).astype(BF16)


def rotation(wires, model):
    width = model // wires.nz
    if width % LANES:
        return [(slice(0, model), slice(0, model))]
    out = []
    for s in range(wires.nz):
        block = lax.rem(wires.at_z - s + wires.nz, wires.nz)
        start = pl.multiple_of(block * width, LANES)
        out.append((slice(s * width, (s + 1) * width), pl.ds(start, width)))
    return out


def outside_rotation(grid, value, back=False):
    width = value.shape[-1] // grid.nz
    if width % LANES == 0:
        return value
    parts = []
    for s in range(grid.nz):
        block = lax.rem(grid.z - s + grid.nz, grid.nz)
        parts.append(lax.dynamic_slice_in_dim(value, block * width, width, value.ndim - 1))
    return jnp.concatenate(parts, -1)


def only(condition, act):
    if condition is None:
        act()
    else:
        pl.when(condition)(act)


class Copy:
    def __init__(self, copy, when, got, index):
        self.copy, self.when, self.got, self.index = copy, when, got, index
        self.sent = False

    def wait_recv(self):
        only(self.got, self.copy.wait_recv)

    def wait_send(self):
        if not self.sent:
            only(self.when, self.copy.wait_send)
        self.sent = True


def semaphores():
    nz = lax.axis_size("tok") // 2
    return [
        pltpu.SemaphoreType.DMA((48 + 16 * nz,)),
        pltpu.SemaphoreType.DMA((48 + 16 * nz,)),
        pltpu.SemaphoreType.DMA((24 + 4 * nz,)),
    ]


class Wires:
    def __init__(self, send, recv, local):
        self.send, self.recv, self.here = send, recv, local
        self.count = self.local_count = 0
        self.copies = []
        tokens = lax.axis_size("tok")
        tok, mp = lax.axis_index("tok"), lax.axis_index("mp")
        self.nz = tokens // 2
        self.at_z, self.at_y = tok // 2, tok % 2
        self.at_x, self.at_c = mp // 2, mp % 2
        self.x = (tok, lax.rem(mp + 2, 4))
        self.y = (tok + 1 - 2 * self.at_y, mp)
        self.c = (tok, mp + 1 - 2 * self.at_c)
        self.up = (lax.rem(tok + 2, tokens), mp)
        self.down = (lax.rem(tok + tokens - 2, tokens), mp)

    def hello(self):
        barrier = pltpu.get_barrier_semaphore()
        for peer in (self.x, self.y, self.c, self.up, self.down):
            pl.semaphore_signal(barrier, inc=1, device_id=peer, device_id_type=MESH)

    def ready(self):
        pl.semaphore_wait(pltpu.get_barrier_semaphore(), 5)

    def greet(self):
        self.hello()
        self.ready()

    def start(self, source, target, peer, when=None, got=None, index=None):
        i = index
        if index is None:
            i = self.count
            self.count += 1
        copy = pltpu.make_async_remote_copy(
            src_ref=source,
            dst_ref=target,
            send_sem=self.send.at[i],
            recv_sem=self.recv.at[i],
            device_id=peer,
            device_id_type=MESH,
        )
        only(when, copy.start)
        made = Copy(copy, when, got, i)
        self.copies.append(made)
        return made

    def local(self, source, target):
        copy = pltpu.make_async_copy(source, target, self.here.at[self.local_count])
        self.local_count += 1
        copy.start()
        return copy

    def natural(self, b):
        spots = ((self.at_y, b // 4), (self.at_x, b // 2 % 2), (self.at_c, b % 2))
        place = 0
        for at, bit in spots:
            place = 2 * place + at + bit - 2 * at * bit
        return place

    def finish(self):
        for copy in self.copies:
            copy.wait_send()


def drain(*parts):
    parts = list(parts)
    while parts:
        parts = [part for part in parts if next(part, None) is not None]


def run(part):
    next(part, None)


def exchange_halves(wires, sources, slot, bounce=None):
    n = slot.shape[0] // 2
    rows = pl.ds(pl.multiple_of(wires.at_y * n, n), n)
    arrivals, copies = [], []
    for pick, lo, hi in sources:
        arrivals.append(wires.start(pick(1 - wires.at_y), slot.at[rows, lo:hi], wires.y))
        to = slot.at[rows, lo:hi] if bounce is None else bounce.at[:, lo:hi]
        copies.append(wires.local(pick(wires.at_y), to))
    yield 1
    for copy in copies:
        copy.wait()
    if bounce is not None:
        wires.local(bounce, slot.at[rows]).wait()
    for arrival in arrivals:
        arrival.wait_recv()


def along_z(wires, first, slot):
    nz, z = wires.nz, wires.at_z
    get = lambda s: first if s == 0 else slot(s)
    for s in range(1, nz):
        up = wires.start(get(s - 1), slot(s), wires.up, (z >= s - 1) & (z < nz - 1), z >= s)
        down = wires.start(
            get((nz - s + 1) % nz), slot(nz - s), wires.down, (z + s <= nz) & (z >= 1), z + s < nz
        )
        yield 1
        up.wait_recv()
        down.wait_recv()


EARLY = True


def add_into(target, source):
    @pl.loop(0, target.shape[0] // 32)
    def _(t):
        part = pl.ds(pl.multiple_of(t * 32, 32), 32)
        target[part, :] = (target[part, :].astype(F32) + source[part, :].astype(F32)).astype(BF16)


def sum_along_z(wires, p, above, below, stage, total, early=EARLY):
    nz, z = wires.nz, wires.at_z
    ups, downs = {}, {}

    def ends(s):
        ups[s] = wires.start(p(s), above.at[s - 1], wires.up, z == 0, (z >= 1) & (z <= s))
        downs[s] = wires.start(
            p(nz - s), below.at[s - 1], wires.down, z == nz - 1, (z + s >= nz - 1) & (z < nz - 1)
        )

    for s in range(1, nz if early else 2):
        ends(s)
    for s in range(2, nz):
        loads = [wires.local(p(s), stage.at[0]), wires.local(p(nz - s), stage.at[1])]
        yield 1
        ups[s - 1].wait_recv()
        downs[s - 1].wait_recv()
        for load in loads:
            load.wait()
        if not early:
            ends(s)
        rising = (z >= 1) & (z < s) & (z < nz - 1)
        falling = (z + s >= nz) & (z < nz - 1) & (z >= 1)
        only(rising, lambda s=s: add_into(above.at[s - 2], stage.at[0]))
        wires.start(above.at[s - 2], above.at[s - 1], wires.up, rising, None, ups[s].index)
        only(falling, lambda s=s: add_into(below.at[s - 2], stage.at[1]))
        wires.start(below.at[s - 2], below.at[s - 1], wires.down, falling, None, downs[s].index)
    load = wires.local(p(0), stage.at[0])
    yield 1
    ups[nz - 1].wait_recv()
    downs[nz - 1].wait_recv()
    load.wait()
    only(z >= 1, lambda: add_into(stage.at[0], above.at[nz - 2]))
    only(z < nz - 1, lambda: add_into(stage.at[0], below.at[nz - 2]))
    kept = wires.local(stage.at[0], total)
    yield 1
    kept.wait()


def swap_rows(wires, total, got):
    n = got.shape[0]
    other = pl.ds(pl.multiple_of((1 - wires.at_y) * n, n), n)
    sent = wires.start(total.at[other], got, wires.y)
    yield 1
    sent.wait_recv()


def sum_scratch(nz, rows, cols):
    return [
        pltpu.VMEM((nz - 1, rows, cols), BF16),
        pltpu.VMEM((nz - 1, rows, cols), BF16),
        pltpu.VMEM((2, rows, cols), BF16),
    ]


def swap_outputs(*totals):
    return [jax.ShapeDtypeStruct((t.shape[0] // 2, t.shape[1]), BF16) for t in totals]


def columns(ref, rows, lo, hi):
    return lambda s: ref.at[pl.ds(s * rows, rows), lo:hi]


def gather_weight_rows(wires, sources, out, bounce=None):
    n = out.shape[0] // wires.nz
    slot = lambda s: out.at[pl.ds(s * n, n)]
    yield from exchange_halves(wires, sources, slot(0), bounce)
    yield from along_z(wires, slot(0), slot)


def gather_phase(wires, block, out, parts):
    views = [(pl.ds(lo, hi - lo), link) for lo, hi, link in parts]
    on_y = [v for v in views if v[1] == "x"] + [v for v in views if v[1] == "y"]
    on_x = on_y[::-1]
    mine = wires.local(block, out.at[0])
    from_y, from_x, diagonal = {}, {}, []
    c = [wires.start(block, out.at[1], wires.c)]
    for k, (rows, _) in enumerate(on_x):
        from_x[k] = wires.start(block.at[rows], out.at[2, rows], wires.x)
    yield 1
    for k, (rows, _) in enumerate(on_y):
        from_y[k] = wires.start(block.at[rows], out.at[4, rows], wires.y)
    yield 1
    for k in range(len(views)):
        for place, arrived, (rows, link), via, own in (
            (4, from_y[k], on_y[k], wires.x, "x"), (2, from_x[k], on_x[k], wires.y, "y"),
        ):
            arrived.wait_recv()
            if link == own:
                relay = wires.start(out.at[place, rows], out.at[6, rows], via)
                diagonal.append((relay, rows))
            c.append(wires.start(out.at[place, rows], out.at[place + 1, rows], wires.c))
        yield 1
    for relay, rows in diagonal:
        relay.wait_recv()
        c.append(wires.start(out.at[6, rows], out.at[7, rows], wires.c))
        yield 1
    for copy in c:
        copy.wait_recv()
    mine.wait()


def halved(n, cut=None):
    cut = n // 2 if cut is None else cut
    return [(0, cut, "x"), (cut, n, "y")]


def feed_sources(gate, up, down, cut, hidden):
    a, b = cut
    n = b - a
    step = LANES

    def pick(ref):
        return lambda y: ref.at[:, pl.ds(pl.multiple_of(y * hidden + a, step), n)]

    return [(pick(ref), k * n, (k + 1) * n) for k, ref in enumerate((gate, up, down))]


def forward_kernel(
    hidden, cuts,
    x_ref, dout_ref, gain_in, qw_ref, kw_ref, vw_ref, ow_ref, ids_ref, rope_ref, spread_ref,
    squeeze_ref, gate_ref, up_ref, down_ref,
    x_own, dout_own, cos_ref, sin_ref, first_ref, q_ref, k_ref, v_ref, o_ref, lse_ref, gain_ref,
    res_ref, inv_ref, a1_ref, dout_all, w_attn, w_out, w_zero, w_one, w_two, w_three, a2_ref,
    pack, opack, x_all, w_flat, w_pad, w_o, bounce_out, bounce_zero, bounce_one, bounce_two,
    bounce_three, block, cr, xr, yr, tr, br, send, recv, local,
):
    wires = Wires(send, recv, local)
    wires.hello()
    nz, z = wires.nz, wires.at_z
    rows, model = x_ref.shape
    length = 8 * rows
    heads = q_ref.shape[1] // LANES
    keys = rows + WINDOW_LENGTH

    turns = rotation(wires, model)
    at = qw_ref.shape[1] // 2
    for h in range(2):
        pack[h, :, 0:at] = qw_ref[:, h * at : (h + 1) * at]
    for ref in (kw_ref, vw_ref):
        n = ref.shape[0] // 2
        eye = identity(n)
        for h in range(2):
            pack[h, :, at : at + n] = tn(ref[h * n : (h + 1) * n, :], eye).astype(BF16)
        at += n
    rest = pack.shape[2] - at
    row = lax.broadcasted_iota(jnp.int32, (2, rest), 0)
    lane = lax.broadcasted_iota(jnp.int32, (2, rest), 1)
    tail = tn(gain_in[...], (row == lane).astype(BF16)).astype(BF16)
    for h in range(2):
        pack[h, :, at:] = tail
    wires.ready()
    weights = gather_weight_rows(wires, [(lambda y: pack.at[y], 0, pack.shape[2])], w_flat)
    run(weights)
    for to, of in turns:
        x_own[:, to] = x_ref[:, of]
    tokens = gather_phase(wires, x_own, x_all, halved(rows, START_CUT))
    run(tokens)
    run(weights)
    run(tokens)
    for to, of in turns:
        dout_own[:, to] = dout_ref[:, of]
    n = ow_ref.shape[1] // 2
    for h in range(2):
        opack[h] = ow_ref[:, h * n : (h + 1) * n]
    run(tokens)
    run(weights)

    lane = lax.broadcasted_iota(jnp.int32, (1, LANES), 1)
    sign = jnp.where(lane < LANES // 2, -1.0, 1.0)
    steps = length // ROPE_STEP
    cos_low, sin_low = rope_ref[0, steps:, :], rope_ref[1, steps:, :]
    for t in range(steps):
        part = slice(t * ROPE_STEP, (t + 1) * ROPE_STEP)
        cos_high, sin_high = rope_ref[0, t : t + 1, :], rope_ref[1, t : t + 1, :]
        cos_ref[part, :] = cos_high * cos_low - sin_high * sin_low
        sin_ref[part, :] = (sin_high * cos_low + cos_high * sin_low) * sign
    offset = pl.multiple_of(z * length, length)
    ids = ids_ref[:, pl.ds(offset, length)]
    begin = jnp.zeros((1, length), jnp.int32)
    for number in range(1, 5):
        count = jnp.sum((ids_ref[...] < number).astype(jnp.int32), axis=1, keepdims=True)
        begin = jnp.where(ids >= number, count, begin)
    window = lax.broadcasted_iota(jnp.int32, (1, length), 1) - (WINDOW_LENGTH - 1)
    first_ref[...] = jnp.maximum(begin - offset, window) + WINDOW_LENGTH

    run(tokens)
    run(weights)
    out_weights = gather_weight_rows(
        wires, [(lambda y: opack.at[y], 0, opack.shape[2])], w_out, bounce_out
    )
    zero_weights, one_weights = [
        gather_weight_rows(
            wires, feed_sources(gate_ref, up_ref, down_ref, cut, hidden), out, bounce
        )
        for cut, out, bounce in zip(cuts, (w_zero, w_one), (bounce_zero, bounce_one))
    ]
    exchanges = [
        exchange_halves(
            wires, feed_sources(gate_ref, up_ref, down_ref, cut, hidden), slot, bounce
        )
        for cut, slot, bounce in zip(cuts[2:], (w_two, w_three), (bounce_two, bounce_three))
    ]
    run(out_weights)
    run(zero_weights)
    drain(tokens)
    sent = list(wires.copies)
    quarter = rows // 4
    cotangents = gather_phase(
        wires, dout_own, dout_all, [(t * quarter, (t + 1) * quarter, "x") for t in range(4)]
    )
    run(cotangents)
    drain(weights)
    run(out_weights)
    run(cotangents)
    for copy in sent:
        copy.wait_send()
    saves = [wires.local(w_flat, w_attn)]

    @pl.loop(0, model // 512)
    def _(t):
        part = pl.ds(pl.multiple_of(t * 512, 512), 512)
        w_pad[part, :] = nn(w_flat[part, :], spread_ref[...]).astype(BF16)

    place = lax.broadcasted_iota(jnp.int32, (8, w_flat.shape[1]), 1)
    row = lax.broadcasted_iota(jnp.int32, (8, w_flat.shape[1]), 0)
    which = (place == (heads + 2) * HEAD_SIZE + row).astype(BF16)
    gain_ref[...] = nt(which, w_flat[...])
    gain = gain_ref[0:1, :]

    @pl.when(z == 0)
    def _():
        k_ref[0:WINDOW_LENGTH, :] = jnp.zeros((WINDOW_LENGTH, LANES), BF16)
        v_ref[0:WINDOW_LENGTH, :] = jnp.zeros((WINDOW_LENGTH, LANES), BF16)

    def project(b, at):
        x = x_all[at].astype(F32)
        inverse = lax.rsqrt(jnp.mean(x * x, axis=1, keepdims=True) + EPS)
        a1 = (x * inverse * gain).astype(BF16)
        x_all[at] = a1
        acc = nn(a1, w_pad[...])
        here = pl.ds(pl.multiple_of(b * rows, rows), rows)
        there = pl.ds(pl.multiple_of(WINDOW_LENGTH + b * rows, rows), rows)
        cosine, sine = cos_ref[here, :], sin_ref[here, :]
        for h in range(heads + 1):
            u = acc[:, h * LANES : (h + 1) * LANES]
            turned = (u * cosine + pltpu.roll(u, LANES // 2, 1) * sine).astype(BF16)
            if h < heads:
                q_ref[here, h * LANES : (h + 1) * LANES] = turned
            else:
                k_ref[there, :] = turned
        v_ref[there, :] = acc[:, (heads + 1) * LANES :].astype(BF16)

    def projected(lo, hi):
        @pl.loop(lo, hi)
        def _(b):
            project(b, wires.natural(b))

        for b in range(lo, hi):
            at = wires.natural(b)
            saves.append(wires.local(x_all.at[at], a1_ref.at[at]))

    projected(6, 8)
    halo = [
        wires.start(
            ref.at[pl.ds(length, WINDOW_LENGTH)], ref.at[pl.ds(0, WINDOW_LENGTH)],
            wires.up, z < nz - 1, z > 0,
        )
        for ref in (k_ref, v_ref)
    ]
    run(zero_weights)
    projected(0, 2)
    run(out_weights)
    projected(2, 6)
    run(zero_weights)
    run(cotangents)
    run(cotangents)
    run(one_weights)
    for copy in halo:
        copy.wait_recv()

    def attend(b, at):
        start = pl.multiple_of(b * rows, rows)
        span = pl.ds(start, keys)
        here = pl.ds(start, rows)
        kb = k_ref[span, :]
        vt = v_ref[span, :].T
        bias = mask_bias(first_ref[:, here] - start, keys, rows)
        outs = []
        for h in range(heads):
            lanes = slice(h * LANES, (h + 1) * LANES)
            s = nt(kb, q_ref[here, lanes]) * (SCALE * LOG2E) + bias
            peak = jnp.max(s, axis=0, keepdims=True)
            p = jnp.exp2(s - peak)
            total = jnp.sum(p, axis=0, keepdims=True)
            ot = nn(vt, p.astype(BF16)) / total
            outs.append(ot.T.astype(BF16))
            lse_ref[b, h : h + 1, :] = peak + jnp.log2(total)
        o_ref[at] = nn(jnp.concatenate(outs, 1), squeeze_ref[...]).astype(BF16)

    def attended(lo, hi):
        @pl.loop(lo, hi)
        def _(b):
            attend(b, wires.natural(b))

    attended(0, 2)
    run(out_weights)
    run(cotangents)
    attended(2, 4)
    run(cotangents)
    run(zero_weights)
    for exchange in exchanges:
        run(exchange)
    attended(4, 6)
    drain(out_weights)
    load_o = wires.local(w_out, w_o)
    run(one_weights)
    attended(6, 8)
    load_o.wait()
    for save in saves:
        save.wait()

    def emit(part, total):
        residual = x_own[part, :].astype(F32) + total
        inverse = lax.rsqrt(jnp.mean(residual * residual, axis=1, keepdims=True) + EPS)
        res_ref[part, :] = residual
        inv_ref[part, :] = inverse
        block[part, :] = (residual * inverse * gain_ref[1:2, :]).astype(BF16)

    sums = reduce_phase(
        wires, o_ref, w_o, x_all.at[pl.ds(0, 4)], cr, x_all.at[pl.ds(4, 4)], xr, yr, tr, br, emit
    )
    for _ in range(4):
        run(sums)
    drain(zero_weights, cotangents)
    run(sums)
    run(one_weights)
    drain(sums)
    normed = gather_phase(wires, block, a2_ref, halved(rows))
    run(normed)
    run(normed)
    run(normed)
    run(one_weights)
    drain(normed, one_weights, *exchanges)
    wires.finish()


START_CUT = 160


def attention_forward(
    inputs, dout, gains, query, key_t, value_t, out_t, ids, rope, gate, up, down_t, width, cuts
):
    n, model = inputs.shape
    rows = query.shape[0]
    length = 8 * n
    heads = query.shape[1] // 2 // HEAD_SIZE
    hidden = gate.shape[1] // 2
    wide = heads * LANES
    flat = heads * HEAD_SIZE
    half = n // 2
    spread = spread_matrix(heads + 1, 1, rows=width)
    squeeze = spread_matrix(0, heads).T
    sizes = [3 * (b - a) for a, b in cuts]
    b16 = lambda *shape: jax.ShapeDtypeStruct(shape, BF16)
    f32 = lambda *shape: jax.ShapeDtypeStruct(shape, F32)
    v16 = lambda *shape: pltpu.VMEM(shape, BF16)
    return pl.pallas_call(
        functools.partial(forward_kernel, hidden, cuts),
        in_specs=[WHOLE] * 11 + [HBM] * 3,
        out_specs=[WHOLE] * 13 + [HBM] * 9,
        out_shape=[
            b16(n, model), b16(n, model), f32(length, LANES), f32(length, LANES),
            jax.ShapeDtypeStruct((1, length), jnp.int32), b16(length, wide),
            b16(length + WINDOW_LENGTH, LANES), b16(length + WINDOW_LENGTH, LANES),
            b16(8, n, flat), f32(8, heads, n), f32(8, model), f32(n, model), f32(n, 1),
            b16(8, n, model), b16(8, n, model), b16(model, width), b16(model, flat),
            b16(model, sizes[0]), b16(model, sizes[1]), b16(2 * rows, sizes[2]),
            b16(2 * rows, sizes[3]), b16(8, n, model),
        ],
        scratch_shapes=[
            v16(2, rows, width), v16(2, rows, flat), v16(8, n, model), v16(model, width),
            v16(model, spread.shape[1]), v16(model, flat), v16(rows, flat),
        ]
        + [v16(rows, size) for size in sizes]
        + [
            v16(n, model), v16(4, n, model), v16(2, half, model), v16(2, half, model),
            v16(half, model), v16(half, model),
        ]
        + semaphores(),
        compiler_params=params(62, collective_id=0, has_side_effects=True),
        name="attention_forward",
        **light(),
    )(
        inputs, dout, gains, query, key_t, value_t, out_t, ids, rope, spread, squeeze, gate, up,
        down_t,
    )


def feed_kernel(
    hidden, cuts, chunks,
    a_ref, d_ref, w0_ref, w1_ref, w2_ref, w3_ref,
    m_ref, g_ref, w_ref, grad0, grad1, grad2, grad3, total,
    a, d, w, m, g, stage, above, below, extra, send, recv, local,
):
    wires = Wires(send, recv, local)
    nz = wires.nz
    length, model = a.shape
    slot = model // nz
    wires.hello()

    def spots(lo, hi):
        out = []
        for k in range(3):
            for first, last in chunks:
                left, right = max(lo, first), min(hi, last)
                if left < right:
                    base = 2 * hidden if k == 2 else first + k * (last - first)
                    start = base + left
                    out.append((k * (hi - lo) + left - lo, start, right - left, k, left))
        return out

    loads = []
    for ref, (lo, hi) in ((w0_ref, cuts[0]), (w1_ref, cuts[1])):
        for of, to, n, _, _ in spots(lo, hi):
            loads.append(wires.local(ref.at[:, of : of + n], w.at[:, to : to + n]))
    rows = length // 8
    a_loads, d_loads = [], []

    def fetch(half):
        part = pl.ds(half * 4 * rows, 4 * rows)
        a_loads.append(wires.local(a_ref.at[part], a.at[part]))
        d_loads.append(wires.local(d_ref.at[part], d.at[part]))

    fetch(0)

    def carried(ref, cut):
        pieces, copies = [], []
        for of, to, n, _, _ in spots(*cut):
            pieces.append((to, to + n))
            copies.append(wires.local(ref.at[:, of : of + n], w.at[pl.ds(0, slot), to : to + n]))
        yield 1
        for copy in copies:
            copy.wait()
        hops = [
            along_z(
                wires,
                w.at[pl.ds(0, slot), lo:hi],
                lambda s, lo=lo, hi=hi: w.at[pl.ds(s * slot, slot), lo:hi],
            )
            for lo, hi in pieces
        ]
        while hops:
            hops = [hop for hop in hops if next(hop, None) is not None]
            yield 1

    later = [carried(ref, cut) for ref, cut in zip((w2_ref, w3_ref), cuts[2:])]
    for part in later:
        run(part)
    wires.ready()
    run(later[0])
    for copy in loads:
        copy.wait()

    def units(lo, hi, blocks):
        n = hi - lo

        @pl.loop(*blocks)
        def _(b):
            part = pl.ds(pl.multiple_of(b * rows, rows), rows)
            both = nn(a[part, :], w[:, 2 * lo : 2 * hi])
            gate, up = both[:, :n], both[:, n:]
            dmixed = nn(d[part, :], w[:, 2 * hidden + lo : 2 * hidden + hi])
            sigma = jax.nn.sigmoid(gate)
            silu = gate * sigma
            m[part, lo:hi] = (silu * up).astype(BF16)
            g[part, lo + hi : 2 * hi] = (dmixed * silu).astype(BF16)
            g[part, 2 * lo : lo + hi] = (
                dmixed * up * sigma * (1.0 + gate * (1.0 - sigma))
            ).astype(BF16)

    tile = stage.shape[1]
    last = model // tile

    def weight_grads(lo, hi, out, tiles=None):
        n = hi - lo
        tiles = (0, last) if tiles is None else tiles

        def save(t):
            return pltpu.make_async_copy(
                stage.at[t % 2, :, 0 : 3 * n],
                out.at[pl.ds(pl.multiple_of(t * tile, tile), tile)],
                local.at[24 + 4 * nz - 1 - t % 2],
            )

        @pl.loop(*tiles)
        def _(t):
            @pl.when(t >= 2)
            def _():
                save(t - 2).wait()

            cols = pl.ds(pl.multiple_of(t * tile, tile), tile)
            stage[t % 2, :, 0 : 2 * n] = tn(a[:, cols], g[:, 2 * lo : 2 * hi]).astype(BF16)
            stage[t % 2, :, 2 * n : 3 * n] = tn(d[:, cols], m[:, lo:hi]).astype(BF16)
            save(t).start()

        if tiles[1] == last:
            save(last - 2).wait()
            save(last - 1).wait()

    a_loads[0].wait()
    d_loads[0].wait()
    fetch(1)
    units(*chunks[0], (0, 4))
    a_loads[1].wait()
    d_loads[1].wait()
    units(*chunks[0], (4, 8))
    weight_grads(*chunks[0], grad0, (0, 2))
    run(later[0])
    weight_grads(*chunks[0], grad0, (2, last))
    sums = sum_along_z(
        wires, columns(grad0, slot, 0, total.shape[1]), above, below, extra, total, False
    )
    run(sums)
    units(*chunks[1], (0, 8))
    run(later[0])
    weight_grads(*chunks[1], grad1, (0, 4))
    run(later[1])
    weight_grads(*chunks[1], grad1, (4, last))
    drain(later[0])
    run(sums)
    units(*chunks[2], (0, 4))
    run(later[1])
    units(*chunks[2], (4, 8))
    weight_grads(*chunks[2], grad2, (0, 2))
    run(later[1])
    weight_grads(*chunks[2], grad2, (2, last))
    drain(later[1])
    run(sums)
    outs = [wires.local(w, w_ref)]
    units(*chunks[3], (0, 8))
    outs += [wires.local(m, m_ref), wires.local(g, g_ref)]
    weight_grads(*chunks[3], grad3)
    drain(sums)
    for copy in outs:
        copy.wait()
    wires.finish()


def feed_forward(a2, dout, w0, w1, w2, w3, cuts, chunks):
    length, model = a2.shape
    hidden = cuts[-1][1]
    sizes = [b - a for a, b in chunks]
    rows = w3.shape[0]
    nz = model // rows
    return pl.pallas_call(
        functools.partial(feed_kernel, hidden, cuts, chunks),
        in_specs=[HBM] * 6,
        out_specs=[HBM] * 8,
        out_shape=[
            jax.ShapeDtypeStruct((length, hidden), BF16),
            jax.ShapeDtypeStruct((length, 2 * hidden), BF16),
            jax.ShapeDtypeStruct((model, 3 * hidden), BF16),
        ]
        + [jax.ShapeDtypeStruct((model, 3 * n), BF16) for n in sizes]
        + [jax.ShapeDtypeStruct((rows, 3 * sizes[0]), BF16)],
        scratch_shapes=[
            pltpu.VMEM((length, model), BF16),
            pltpu.VMEM((length, model), BF16),
            pltpu.VMEM((model, 3 * hidden), BF16),
            pltpu.VMEM((length, hidden), BF16),
            pltpu.VMEM((length, 2 * hidden), BF16),
            pltpu.VMEM((2, 512, 3 * max(sizes)), BF16),
        ]
        + sum_scratch(nz, rows, 3 * sizes[0])
        + semaphores(),
        compiler_params=params(62, collective_id=1, has_side_effects=True),
        name="feed_forward",
        **light(),
    )(a2, dout, w0, w1, w2, w3)


def reduce_phase(wires, a, w, cs, cr, q, xr, yr, tr, br, emit, ready=None):
    n = q.shape[1]
    half = n // 2
    top, bottom = pl.ds(0, half), pl.ds(half, half)
    model = q.shape[2]
    tile = 512
    deep = a.shape[2]

    def product(place, target):
        if ready is not None:
            ready(place)

        @pl.loop(0, model // tile)
        def _(t):
            cols = pl.ds(pl.multiple_of(t * tile, tile), tile)
            target[:, cols] = nt(a[place], w[cols, 0:deep]).astype(BF16)

    waits = {}
    for j in (3, 1, 2, 0):
        product(2 * j + 1, cs.at[j])
        got = wires.start(cs.at[j], cr.at[j], wires.c)
        product(2 * j, q.at[j])
        got.wait_recv()
        q[j] = (q[j].astype(F32) + cr[j].astype(F32)).astype(BF16)
        if j == 3:
            waits["x1"] = wires.start(q.at[3, top], xr.at[1], wires.x)
            waits["y1"] = wires.start(q.at[3, bottom], yr.at[1], wires.y)
        if j == 1:
            waits["x0"] = wires.start(q.at[1, top], xr.at[0], wires.x)
        if j == 2:
            waits["y0"] = wires.start(q.at[2, bottom], yr.at[0], wires.y)
        yield 1
    waits["x1"].wait_recv()
    q[2, top] = (q[2, top].astype(F32) + xr[1].astype(F32)).astype(BF16)
    waits["t"] = wires.start(q.at[2, top], tr, wires.y)
    waits["y1"].wait_recv()
    q[1, bottom] = (q[1, bottom].astype(F32) + yr[1].astype(F32)).astype(BF16)
    waits["b"] = wires.start(q.at[1, bottom], br, wires.x)
    yield 1
    waits["x0"].wait_recv()
    yield 1
    waits["t"].wait_recv()
    emit(top, q[0, top].astype(F32) + xr[0].astype(F32) + tr[...].astype(F32))
    waits["y0"].wait_recv()
    waits["b"].wait_recv()
    emit(bottom, q[0, bottom].astype(F32) + yr[0].astype(F32) + br[...].astype(F32))


def reduce_scratch(n, model):
    half = n // 2
    return [
        pltpu.VMEM((4, n, model), BF16),
        pltpu.VMEM((4, n, model), BF16),
        pltpu.VMEM((4, n, model), BF16),
        pltpu.VMEM((2, half, model), BF16),
        pltpu.VMEM((2, half, model), BF16),
        pltpu.VMEM((half, model), BF16),
        pltpu.VMEM((half, model), BF16),
    ]


def middle_kernel(
    a_ref, w_ref, dout_ref, res_ref, inv_ref, gain_ref, grad0, grad2,
    dres_ref, out_ref, total0, total2,
    a, w, block, cs, cr, q, xr, yr, tr, br,
    above0, below0, stage0, above2, below2, stage2, send, recv, local,
):
    wires = Wires(send, recv, local)
    wires.hello()
    load_w = wires.local(w_ref.at[:, 0 : w.shape[1]], w)
    loads = {place: wires.local(a_ref.at[place], a.at[place]) for place in (7, 6, 3, 2, 5, 4, 1, 0)}
    wires.ready()
    rows = total0.shape[0]
    first = sum_along_z(
        wires, columns(grad0, rows, 0, total0.shape[1]), above0, below0, stage0, total0
    )
    second = sum_along_z(
        wires, columns(grad2, rows, 0, total2.shape[1]), above2, below2, stage2, total2, False
    )
    run(first)

    def emit(rows, total):
        inverse = inv_ref[rows, :]
        normed = res_ref[rows, :] * inverse
        e = total * gain_ref[1:2, :]
        back = inverse * (e - normed * jnp.mean(e * normed, axis=1, keepdims=True))
        dres = dout_ref[rows, :].astype(F32) + back
        dres_ref[rows, :] = dres
        block[rows, :] = dres.astype(BF16)

    load_w.wait()
    sums = reduce_phase(
        wires, a, w, cs, cr, q, xr, yr, tr, br, emit, lambda place: loads[place].wait()
    )
    for _ in range(4):
        run(sums)
    run(first)
    run(sums)
    run(sums)
    run(first)
    run(second)
    drain(sums)
    tokens = gather_phase(wires, block, out_ref, halved(block.shape[0]))
    run(tokens)
    run(tokens)
    run(first)
    run(second)
    run(tokens)
    run(second)
    run(tokens)
    drain(second, tokens, first)
    wires.finish()


def feed_back(dgu, w, dout, residual, inverse, gain, grad0, grad2):
    n, model = dout.shape
    k = dgu.shape[1]
    rows = 2 * model // lax.axis_size("tok")
    nz = model // rows
    half, small = grad0.shape[1], grad2.shape[1]
    return pl.pallas_call(
        middle_kernel,
        in_specs=[HBM] * 2 + [WHOLE] * 4 + [HBM] * 2,
        out_specs=[WHOLE] + [HBM] * 3,
        out_shape=[
            jax.ShapeDtypeStruct((n, model), F32),
            jax.ShapeDtypeStruct((8, n, model), BF16),
            jax.ShapeDtypeStruct((rows, half), BF16),
            jax.ShapeDtypeStruct((rows, small), BF16),
        ],
        scratch_shapes=[
            pltpu.VMEM((8, n, k), BF16),
            pltpu.VMEM((model, k), BF16),
            pltpu.VMEM((n, model), BF16),
        ]
        + reduce_scratch(n, model)
        + sum_scratch(nz, rows, half)
        + sum_scratch(nz, rows, small)
        + semaphores(),
        compiler_params=params(62, collective_id=3, has_side_effects=True),
        name="feed_back",
        **light(),
    )(dgu.reshape(8, n, k), w, dout, residual, inverse, gain, grad0, grad2)


def back_kernel(
    da_ref, w_ref, o_ref, q_ref, k_ref, v_ref, lse_ref, first_ref, cos_ref, sin_ref,
    spread_ref, squeeze_ref, final_ref, m_ref, down_ref, res_ref, grad1, sum0, sum1, sum2,
    dqkv_ref, out_ref, grad_out, total, got0, got1, got2,
    da, do, dk, dv, halo, fetched, m, w_down, cr, xr, yr, tr, br,
    above, below, stage, stage1, res, send, recv, local,
):
    wires = Wires(send, recv, local)
    nz, z = wires.nz, wires.at_z
    wires.hello()
    n, model = da.shape[1], da.shape[2]
    heads = q_ref.shape[1] // LANES
    wide = heads * HEAD_SIZE
    keys = n + WINDOW_LENGTH
    length = 8 * n
    loads = [wires.local(da_ref.at[b], da.at[b]) for b in range(8)]
    late = [
        wires.local(m_ref, m),
        wires.local(down_ref.at[:, 2 * m.shape[2] :], w_down),
    ]
    rows = total.shape[0]
    wires.ready()
    carried = sum_along_z(
        wires, columns(grad1, rows, 0, total.shape[1]), above, below, stage, total
    )
    run(carried)
    swaps = [
        swap_rows(wires, s, got) for s, got in ((sum0, got0), (sum1, got1), (sum2, got2))
    ]
    for swap in swaps:
        run(swap)
    dk[...] = jnp.zeros_like(dk)
    dv[...] = jnp.zeros_like(dv)
    for b in range(8):
        loads[b].wait()
        flat = nn(da[b], w_ref[...]).astype(BF16)
        do[b] = nn(flat, spread_ref[...]).astype(BF16)

    saves = []
    for t in range(nz):
        cols = slice(t * rows, (t + 1) * rows)
        if t >= 2:
            saves[t - 2].wait()
        total = None
        for b in range(8):
            part = tn(da[b, :, cols], o_ref[b])
            total = part if total is None else total + part
        stage1[t % 2] = total.astype(BF16)
        saves.append(wires.local(stage1.at[t % 2], grad_out.at[pl.ds(t * rows, rows)]))
    for save in saves[-2:]:
        save.wait()
    for load in late:
        load.wait()
    turns = rotation(wires, model)

    def emit(part, total):
        load = wires.local(res_ref.at[part], res)
        load.wait()
        layer = (res[...] + total).astype(BF16)
        for of, to in turns:
            out_ref[part, to] = layer[:, of]

    sums = reduce_phase(
        wires, m, w_down, da.at[pl.ds(0, 4)], cr, da.at[pl.ds(4, 4)], xr, yr, tr, br, emit
    )
    run(sums)
    run(sums)
    run(carried)
    run(sums)
    run(sums)

    def block(b, at):
        start = pl.multiple_of(b * n, n)
        span = pl.ds(start, keys)
        here = pl.ds(start, n)
        kb = k_ref[span, :]
        vb = v_ref[span, :]
        kt = kb.T
        bias = mask_bias(first_ref[:, here] - start, keys, n)
        cosine, sine = cos_ref[here, :], sin_ref[here, :]
        dqs = []
        dk_sum = dv_sum = None
        for h in range(heads):
            lanes = slice(h * LANES, (h + 1) * LANES)
            qh = q_ref[here, lanes]
            doh = do[at, :, lanes]
            p = jnp.exp2(nt(kb, qh) * (SCALE * LOG2E) + (bias - lse_ref[b, h : h + 1, :]))
            t = p * nt(vb, doh)
            inner = jnp.sum(t, axis=0, keepdims=True)
            ds = (t - p * inner).astype(BF16)
            dq = nn(kt, ds).T * SCALE
            dqs.append((dq * cosine - pltpu.roll(dq, LANES // 2, 1) * sine).astype(BF16))
            dk_h = nn(ds, qh)
            dv_h = nn(p.astype(BF16), doh)
            dk_sum = dk_h if dk_sum is None else dk_sum + dk_h
            dv_sum = dv_h if dv_sum is None else dv_sum + dv_h
        dqkv_ref[at, :, 0:wide] = nn(jnp.concatenate(dqs, 1), squeeze_ref[...]).astype(BF16)
        dk[span, :] += dk_sum
        dv[span, :] += dv_sum

    def blocks(lo, hi):
        @pl.loop(lo, hi)
        def _(b):
            block(b, wires.natural(b))

    blocks(0, 2)
    halo[:, 0:LANES] = dk[0:WINDOW_LENGTH, :].astype(BF16)
    halo[:, LANES:] = dv[0:WINDOW_LENGTH, :].astype(BF16)
    borrowed = wires.start(halo, fetched, wires.down, z >= 1, z < nz - 1)
    run(sums)
    blocks(2, 4)
    run(carried)
    blocks(4, 8)
    drain(sums)
    borrowed.wait_recv()

    @pl.when(z < nz - 1)
    def _():
        dk[length:, :] += fetched[:, 0:LANES].astype(F32)
        dv[length:, :] += fetched[:, LANES:].astype(F32)

    for b in range(8):
        here = slice(b * n, (b + 1) * n)
        there = slice(WINDOW_LENGTH + b * n, WINDOW_LENGTH + (b + 1) * n)
        dkb = dk[there, :] * SCALE
        dkb = dkb * cos_ref[here, :] - pltpu.roll(dkb, LANES // 2, 1) * sin_ref[here, :]
        both = jnp.concatenate([dkb.astype(BF16), dv[there, :].astype(BF16)], 1)
        dqkv_ref[wires.natural(b), :, wide:] = nn(both, final_ref[...]).astype(BF16)
    drain(carried, *swaps)
    wires.finish()


def attention_back(
    da_all, w_out, o, q, k_all, v_all, lse, first_key, cosine, sine, mixed, w_feed, residual, grad1,
    sums, width,
):
    _, n, model = da_all.shape
    length = 8 * n
    heads = q.shape[1] // LANES
    wide = heads * HEAD_SIZE
    spread = spread_matrix(0, heads)
    squeeze = spread_matrix(heads, 0).T
    final = spread_matrix(1, 1, rows=width - wide).T
    rows = 2 * model // lax.axis_size("tok")
    nz = model // rows
    hidden = mixed.shape[1]
    half = n // 2
    return pl.pallas_call(
        back_kernel,
        in_specs=[HBM] + [WHOLE] * 12 + [HBM] * 7,
        out_specs=[WHOLE, WHOLE] + [HBM] * 5,
        out_shape=[
            jax.ShapeDtypeStruct((8, n, width), BF16),
            jax.ShapeDtypeStruct((n, model), BF16),
            jax.ShapeDtypeStruct((model, wide), BF16),
            jax.ShapeDtypeStruct((rows, grad1.shape[1]), BF16),
        ]
        + swap_outputs(*sums),
        scratch_shapes=[
            pltpu.VMEM((8, n, model), BF16),
            pltpu.VMEM((8, n, heads * LANES), BF16),
            pltpu.VMEM(k_all.shape, F32),
            pltpu.VMEM(k_all.shape, F32),
            pltpu.VMEM((WINDOW_LENGTH, 2 * LANES), BF16),
            pltpu.VMEM((WINDOW_LENGTH, 2 * LANES), BF16),
            pltpu.VMEM((8, n, hidden), BF16),
            pltpu.VMEM((model, hidden), BF16),
            pltpu.VMEM((4, n, model), BF16),
            pltpu.VMEM((2, half, model), BF16),
            pltpu.VMEM((2, half, model), BF16),
            pltpu.VMEM((half, model), BF16),
            pltpu.VMEM((half, model), BF16),
        ]
        + sum_scratch(nz, rows, grad1.shape[1])
        + [pltpu.VMEM((2, rows, wide), BF16), pltpu.VMEM((half, model), F32)]
        + semaphores(),
        compiler_params=params(63, collective_id=6, has_side_effects=True),
        name="attention_back",
        **light(),
    )(
        da_all, w_out, o, q, k_all, v_all, lse, first_key, cosine, sine, spread, squeeze, final,
        mixed.reshape(8, n, hidden), w_feed, residual, grad1, *sums,
    )


def last_kernel(
    a_ref, w_ref, x_ref, gain_ref, dres_ref, a1_ref, grad_out, sum0,
    out_ref, total, total1, got0, got, got1,
    cs, cr, q, xr, yr, tr, br, a1, grad, above, below, stage, above1, below1, stage1,
    send, recv, local,
):
    wires = Wires(send, recv, local)
    wires.hello()
    rows = total.shape[0]
    model = a1.shape[2]
    loads = [wires.local(a1_ref.at[b], a1.at[b]) for b in range(8)]
    turns = rotation(wires, model)

    def emit(rows, total):
        x = x_ref[rows, :].astype(F32)
        inverse = lax.rsqrt(jnp.mean(x * x, axis=1, keepdims=True) + EPS)
        normed = x * inverse
        e = total * gain_ref[0:1, :]
        back = inverse * (e - normed * jnp.mean(e * normed, axis=1, keepdims=True))
        done = dres_ref[rows, :] + back
        for of, to in turns:
            out_ref[rows, to] = done[:, of]

    wires.ready()
    first = sum_along_z(
        wires, columns(grad_out, rows, 0, total1.shape[1]), above1, below1, stage1, total1
    )
    run(first)
    swap = swap_rows(wires, sum0, got0)
    run(swap)
    for load in loads:
        load.wait()
    tile = 640

    def weight_grads(lo, hi):
        @pl.loop(lo, hi)
        def _(t):
            cols = pl.ds(pl.multiple_of(t * tile, tile), tile)
            total = None
            for b in range(8):
                part = tn(a1[b, :, cols], a_ref[b])
                total = part if total is None else total + part
            grad[cols, :] = total.astype(BF16)

    weight_grads(0, 2)
    run(first)
    weight_grads(2, 4)
    carried = sum_along_z(
        wires, columns(grad, rows, 0, total.shape[1]), above, below, stage, total
    )
    run(carried)
    sums = reduce_phase(wires, a_ref, w_ref, cs, cr, q, xr, yr, tr, br, emit)
    run(sums)
    run(sums)
    run(first)
    run(sums)
    run(sums)
    run(sums)
    run(carried)
    run(first)
    run(sums)
    run(carried)
    drain(sums)
    drain(first)
    first = swap_rows(wires, total1, got1)
    run(first)
    drain(carried)
    drain(swap_rows(wires, total, got), first, swap)
    wires.finish()


def input_back(dqkv, w, inputs, gain, dres, a1, grad_out, total):
    n, model = inputs.shape
    rows = 2 * model // lax.axis_size("tok")
    nz = model // rows
    wide = dqkv.shape[2]
    return pl.pallas_call(
        last_kernel,
        in_specs=[WHOLE] * 5 + [HBM] * 3,
        out_specs=[WHOLE] + [HBM] * 5,
        out_shape=[
            jax.ShapeDtypeStruct((n, model), F32),
            jax.ShapeDtypeStruct((rows, wide), BF16),
            jax.ShapeDtypeStruct((rows, grad_out.shape[1]), BF16),
            jax.ShapeDtypeStruct((rows // 2, total.shape[1]), BF16),
            jax.ShapeDtypeStruct((rows // 2, wide), BF16),
            jax.ShapeDtypeStruct((rows // 2, grad_out.shape[1]), BF16),
        ],
        scratch_shapes=reduce_scratch(n, model)
        + [pltpu.VMEM((8, n, model), BF16), pltpu.VMEM((model, wide), BF16)]
        + sum_scratch(nz, rows, wide)
        + sum_scratch(nz, rows, grad_out.shape[1])
        + semaphores(),
        compiler_params=params(62, collective_id=4, has_side_effects=True),
        name="input_back",
        **light(),
    )(dqkv, w, inputs, gain, dres, a1, grad_out, total)


def finish_kernel(
    chunks, y_ref, *refs,
):
    count = len(chunks) + 2
    mine, got = refs[0 : 2 * count : 2], refs[1 : 2 * count : 2]
    qw, kw, vw, gw, uw, layer, dinput = refs[2 * count : 2 * count + 7]
    gate, up, down, out, query, key, value, sums, row_sums, layer_out, dinput_out, local = refs[
        2 * count + 7 :
    ]
    copies = [
        pltpu.make_async_copy(layer, layer_out, local.at[0]),
        pltpu.make_async_copy(dinput, dinput_out, local.at[1]),
    ]
    for copy in copies:
        copy.start()
    rows = gate.shape[0]
    hidden = gate.shape[1] // 2
    eye = identity(rows)
    wide = lambda v: v.astype(F32)

    def place(h, pieces):
        for (lo, hi), piece in zip(chunks, pieces):
            n = hi - lo
            at = slice(h * hidden + lo, h * hidden + hi)
            for k, ref in enumerate((gate, up, down)):
                ref[:, at] = wide(piece[:, k * n : (k + 1) * n])
        o, q = pieces[-2:]
        for ref, piece in ((out, o), (query, q)):
            n = ref.shape[1] // 2
            ref[:, h * n : (h + 1) * n] = wide(piece[:, 0:n])
        start = query.shape[1] // 2
        for ref in (key, value):
            n = ref.shape[0] // 2
            ref[h * n : (h + 1) * n, :] = tn(q[:, start : start + n], eye)
            start += n

    @pl.when(y_ref[0] == 0)
    def _():
        place(0, [ref.at[0:rows] for ref in mine])
        place(1, got)

    @pl.when(y_ref[0] == 1)
    def _():
        place(0, got)
        place(1, [ref.at[rows:] for ref in mine])

    def total(w, g, axis):
        return jnp.sum(w[...].astype(F32) * g[...], axis=axis, keepdims=True)

    sums[:, 0:1] = total(qw, query, 1)
    sums[:, 1:2] = total(gw, gate, 1) + total(uw, up, 1)
    row_sums[...] = total(kw, key, 0) + total(vw, value, 0)
    for copy in copies:
        copy.wait()


def finish(y, pieces, weights, out_columns, chunks, layer, dinput):
    query, key_t, _, gate, _ = weights
    rows, hidden = gate.shape
    f32 = lambda *shape: jax.ShapeDtypeStruct(shape, F32)
    return pl.pallas_call(
        functools.partial(finish_kernel, chunks),
        in_specs=[pl.BlockSpec(memory_space=pltpu.SMEM)]
        + [WHOLE] * (len(pieces) + len(weights) + 2),
        out_specs=[WHOLE] * 9 + [HBM] * 2,
        out_shape=[
            f32(rows, hidden), f32(rows, hidden), f32(rows, hidden), f32(rows, out_columns),
            f32(*query.shape), f32(*key_t.shape), f32(*key_t.shape), f32(rows, 2), f32(1, rows),
            jax.ShapeDtypeStruct(layer.shape, layer.dtype),
            jax.ShapeDtypeStruct(dinput.shape, dinput.dtype),
        ],
        scratch_shapes=[pltpu.SemaphoreType.DMA((2,))],
        compiler_params=params(62),
        name="finish",
        **light(),
    )(y, *pieces, *weights, layer, dinput)


def body(
    inputs,
    grad_output,
    segments,
    attention_gain,
    query_weight,
    key_matrix,
    value_matrix,
    output_weight,
    feedforward_gain,
    gate_weight,
    up_weight,
    down_weight,
):
    grid = Grid()
    bf16 = jnp.bfloat16
    model = inputs.shape[1]
    length = inputs.shape[0] * 8
    hidden = gate_weight.shape[1] // 2
    qdim = query_weight.shape[1] // 2
    kdim = key_matrix.shape[1] // 2
    cuts = []
    at = 0
    for n in FF_CHUNKS:
        cuts.append((at, at + n))
        at += n
    heads = qdim // HEAD_SIZE

    width = -(-(qdim + 2 * kdim + 2) // LANES) * LANES

    (
        own, dout, cosine, sine, first_key, q, k_all, v_all, o, lse, gains, residual, inverse_two,
        a1, dout_all, w_attn, w_out, w_zero, w_one, w_two, w_three, a2,
    ) = attention_forward(
        outside_rotation(grid, inputs), outside_rotation(grid, grad_output),
        jnp.stack([attention_gain, feedforward_gain]),
        query_weight, key_matrix.T, value_matrix.T, output_weight.T,
        segments[None, :], rope_parts(length, grid.z * length, HEAD_SIZE),
        gate_weight, up_weight, down_weight.T, width, cuts,
    )
    flat = lambda v: v.reshape(length, v.shape[-1])

    chunks = []
    at = 0
    for n in FF_PARTS:
        chunks.append((at, at + n))
        at += n
    mixed, dgu, w_feed, grad0, grad1, grad2, grad3, sum_0 = feed_forward(
        flat(a2), flat(dout_all), w_zero, w_one, w_two, w_three, cuts, chunks
    )
    dresidual, da_all, sum_1, sum_3 = feed_back(
        dgu, w_feed, dout, residual, inverse_two, gains, grad1, grad3
    )
    dqkv, layer, grad_o, sum_2, got_0, got_1, got_3 = attention_back(
        da_all, w_out, o, q, k_all, v_all, lse, first_key, cosine, sine, mixed, w_feed, residual,
        grad2, (sum_0, sum_1, sum_3), width,
    )
    dinput, sum_q, sum_o, got_2, got_q, got_o = input_back(
        dqkv, w_attn, own, gains, dresidual, a1, grad_o, sum_2
    )
    pieces = (
        sum_0, got_0, sum_1, got_1, sum_2, got_2, sum_3, got_3, sum_o, got_o, sum_q, got_q
    )
    (
        gate_grad, up_grad, down_grad, output_grad, query_grad, key_grad, value_grad, sums,
        row_sums, layer, dinput,
    ) = finish(
        jnp.reshape(grid.y, (1,)).astype(jnp.int32),
        pieces,
        (query_weight, key_matrix.T, value_matrix.T, gate_weight, up_weight),
        output_weight.shape[0],
        chunks,
        layer,
        dinput,
    )
    sums = jnp.stack([sums[:, 0] + row_sums[0], sums[:, 1]])
    sums = sums + grid.swap(sums, C)
    sums = sums + grid.swap(sums, X)
    return (
        outside_rotation(grid, layer),
        outside_rotation(grid, dinput),
        sums[0] / attention_gain.astype(jnp.float32),
        query_grad,
        key_grad.T,
        value_grad.T,
        output_grad.T,
        sums[1] / feedforward_gain.astype(jnp.float32),
        gate_grad,
        up_grad,
        down_grad.T,
    )


def solution(mesh):
    in_specs = (
        P(("tok", "mp"), None),
        P(("tok", "mp"), None),
        P(),
        P("tok"),
        P("tok", "mp"),
        P("tok", "mp"),
        P("tok", "mp"),
        P("mp", "tok"),
        P("tok"),
        P("tok", "mp"),
        P("tok", "mp"),
        P("mp", "tok"),
    )
    out_specs = (
        P(("tok", "mp"), None),
        P(("tok", "mp"), None),
        P("tok"),
        P("tok", "mp"),
        P("tok", "mp"),
        P("tok", "mp"),
        P("mp", "tok"),
        P("tok"),
        P("tok", "mp"),
        P("tok", "mp"),
        P("mp", "tok"),
    )
    return jax.shard_map(body, mesh=mesh, in_specs=in_specs, out_specs=out_specs, check_vma=False)
```

```python
import functools

import jax
import jax.numpy as jnp
import ml_dtypes
import numpy as np
from jax import lax
from jax.experimental import pallas as pl
from jax.experimental.pallas import tpu as pltpu
from jax.sharding import PartitionSpec as P

HEAD_SIZE = 80
WINDOW_LENGTH = 512
EPS = 1e-05
THETA = 1000000.0
FLOOR = -1e30
AXES = ("tok", "mp")
FF_CHUNKS = (128, 384, 256, 128)
FF_PARTS = (256, 256, 256, 128)


class Grid:
    def __init__(self):
        self.nz = lax.axis_size("tok") // 2
        tok = lax.axis_index("tok")
        mp = lax.axis_index("mp")
        self.z, self.y = tok // 2, tok % 2
        self.x, self.c = mp // 2, mp % 2
        self.me = self.y * 4 + self.x * 2 + self.c

    def pairs(self, move):
        out = []
        for z in range(self.nz):
            for g in range(8):
                target = move(z, g)
                if target is not None:
                    out.append((z * 8 + g, target[0] * 8 + target[1]))
        return out

    def swap(self, value, bit):
        return lax.ppermute(value, AXES, self.pairs(lambda z, g: (z, g ^ bit)))

    def ring(self, value):
        return lax.ppermute(value, AXES, self.pairs(lambda z, g: ((z + 1) % self.nz, g)))

    def step(self, value, d):
        def move(z, g):
            return (z + d, g) if 0 <= z + d < self.nz else None

        return lax.ppermute(value, AXES, self.pairs(move))


Y, X, C = 4, 2, 1


LANES = 128
SCALE = HEAD_SIZE ** (-0.5)
LOG2E = 1.4426950408889634
MIB = 1024 * 1024
BF16 = jnp.bfloat16
F32 = jnp.float32
HBM = pl.BlockSpec(memory_space=pl.ANY)
WHOLE = pl.BlockSpec(memory_space=pltpu.VMEM)
MESH = pl.DeviceIdType.MESH


def light(**kwargs):
    return dict(
        cost_estimate=pl.CostEstimate(flops=1000000, bytes_accessed=100000, transcendentals=0),
        **kwargs,
    )


def params(mib, **kwargs):
    return pltpu.CompilerParams(vmem_limit_bytes=mib * MIB, **kwargs)


ROPE_STEP = 64


def rope_parts(count, first, width):
    half = width // 2
    freqs = THETA ** (-(jnp.arange(half, dtype=jnp.int32).astype(F32) * 2.0 / width))
    high = first + ROPE_STEP * jnp.arange(count // ROPE_STEP, dtype=jnp.int32)
    places = jnp.concatenate([high, jnp.arange(ROPE_STEP, dtype=jnp.int32)]).astype(F32)
    blank = jnp.zeros((LANES // 2 - half,), F32)
    lanes = jnp.concatenate([freqs, blank, freqs, blank])
    angles = places[:, None] * lanes[None, :]
    return jnp.stack([jnp.cos(angles), jnp.sin(angles)])


def spread_matrix(turned, plain, rows=0, columns=0):
    half = HEAD_SIZE // 2
    f = np.arange((turned + plain) * HEAD_SIZE)
    head, place = f // HEAD_SIZE, f % HEAD_SIZE
    target = head * LANES + place
    target = target + np.where((head < turned) & (place >= half), LANES // 2 - half, 0)
    out = np.zeros(
        (max(rows, f.size), max(columns, (turned + plain) * LANES)), ml_dtypes.bfloat16
    )
    out[f, target] = 1
    return out


def nt(left, right):
    return lax.dot_general(left, right, (((1,), (1,)), ((), ())), preferred_element_type=F32)


def nn(left, right):
    return lax.dot_general(left, right, (((1,), (0,)), ((), ())), preferred_element_type=F32)


def tn(left, right):
    return lax.dot_general(left, right, (((0,), (0,)), ((), ())), preferred_element_type=F32)


def mask_bias(first, keys, rows):
    kk = lax.broadcasted_iota(jnp.int32, (keys, rows), 0)
    qq = lax.broadcasted_iota(jnp.int32, (keys, rows), 1)
    return jnp.where((kk >= first) & (kk - qq <= WINDOW_LENGTH), 0.0, FLOOR)


def identity(n):
    i = lax.broadcasted_iota(jnp.int32, (n, n), 0)
    return (i == lax.broadcasted_iota(jnp.int32, (n, n), 1)).astype(BF16)


def rotation(wires, model):
    width = model // wires.nz
    if width % LANES:
        return [(slice(0, model), slice(0, model))]
    out = []
    for s in range(wires.nz):
        block = lax.rem(wires.at_z - s + wires.nz, wires.nz)
        start = pl.multiple_of(block * width, LANES)
        out.append((slice(s * width, (s + 1) * width), pl.ds(start, width)))
    return out


def outside_rotation(grid, value, back=False):
    width = value.shape[-1] // grid.nz
    if width % LANES == 0:
        return value
    parts = []
    for s in range(grid.nz):
        block = lax.rem(grid.z - s + grid.nz, grid.nz)
        parts.append(lax.dynamic_slice_in_dim(value, block * width, width, value.ndim - 1))
    return jnp.concatenate(parts, -1)


def only(condition, act):
    if condition is None:
        act()
    else:
        pl.when(condition)(act)


class Copy:
    def __init__(self, copy, when, got, index):
        self.copy, self.when, self.got, self.index = copy, when, got, index
        self.sent = False

    def wait_recv(self):
        only(self.got, self.copy.wait_recv)

    def wait_send(self):
        if not self.sent:
            only(self.when, self.copy.wait_send)
        self.sent = True


def semaphores():
    nz = lax.axis_size("tok") // 2
    return [
        pltpu.SemaphoreType.DMA((48 + 16 * nz,)),
        pltpu.SemaphoreType.DMA((48 + 16 * nz,)),
        pltpu.SemaphoreType.DMA((24 + 4 * nz,)),
    ]


class Wires:
    def __init__(self, send, recv, local):
        self.send, self.recv, self.here = send, recv, local
        self.count = self.local_count = 0
        self.copies = []
        tokens = lax.axis_size("tok")
        tok, mp = lax.axis_index("tok"), lax.axis_index("mp")
        self.nz = tokens // 2
        self.at_z, self.at_y = tok // 2, tok % 2
        self.at_x, self.at_c = mp // 2, mp % 2
        self.x = (tok, lax.rem(mp + 2, 4))
        self.y = (tok + 1 - 2 * self.at_y, mp)
        self.c = (tok, mp + 1 - 2 * self.at_c)
        self.up = (lax.rem(tok + 2, tokens), mp)
        self.down = (lax.rem(tok + tokens - 2, tokens), mp)

    def hello(self):
        barrier = pltpu.get_barrier_semaphore()
        for peer in (self.x, self.y, self.c, self.up, self.down):
            pl.semaphore_signal(barrier, inc=1, device_id=peer, device_id_type=MESH)

    def ready(self):
        pl.semaphore_wait(pltpu.get_barrier_semaphore(), 5)

    def greet(self):
        self.hello()
        self.ready()

    def start(self, source, target, peer, when=None, got=None, index=None):
        i = index
        if index is None:
            i = self.count
            self.count += 1
        copy = pltpu.make_async_remote_copy(
            src_ref=source,
            dst_ref=target,
            send_sem=self.send.at[i],
            recv_sem=self.recv.at[i],
            device_id=peer,
            device_id_type=MESH,
        )
        only(when, copy.start)
        made = Copy(copy, when, got, i)
        self.copies.append(made)
        return made

    def local(self, source, target):
        copy = pltpu.make_async_copy(source, target, self.here.at[self.local_count])
        self.local_count += 1
        copy.start()
        return copy

    def natural(self, b):
        spots = ((self.at_y, b // 4), (self.at_x, b // 2 % 2), (self.at_c, b % 2))
        place = 0
        for at, bit in spots:
            place = 2 * place + at + bit - 2 * at * bit
        return place

    def finish(self):
        for copy in self.copies:
            copy.wait_send()


def drain(*parts):
    parts = list(parts)
    while parts:
        parts = [part for part in parts if next(part, None) is not None]


def run(part):
    next(part, None)


def exchange_halves(wires, sources, slot, bounce=None):
    n = slot.shape[0] // 2
    rows = pl.ds(pl.multiple_of(wires.at_y * n, n), n)
    arrivals, copies = [], []
    for pick, lo, hi in sources:
        arrivals.append(wires.start(pick(1 - wires.at_y), slot.at[rows, lo:hi], wires.y))
        to = slot.at[rows, lo:hi] if bounce is None else bounce.at[:, lo:hi]
        copies.append(wires.local(pick(wires.at_y), to))
    yield 1
    for copy in copies:
        copy.wait()
    if bounce is not None:
        wires.local(bounce, slot.at[rows]).wait()
    for arrival in arrivals:
        arrival.wait_recv()


def along_z(wires, first, slot):
    nz, z = wires.nz, wires.at_z
    get = lambda s: first if s == 0 else slot(s)
    for s in range(1, nz):
        up = wires.start(get(s - 1), slot(s), wires.up, (z >= s - 1) & (z < nz - 1), z >= s)
        down = wires.start(
            get((nz - s + 1) % nz), slot(nz - s), wires.down, (z + s <= nz) & (z >= 1), z + s < nz
        )
        yield 1
        up.wait_recv()
        down.wait_recv()


EARLY = True


def add_into(target, source):
    step = 32 if target.shape[0] % 32 == 0 else 16

    @pl.loop(0, target.shape[0] // step)
    def _(t):
        part = pl.ds(pl.multiple_of(t * step, step), step)
        target[part, :] = (target[part, :].astype(F32) + source[part, :].astype(F32)).astype(BF16)


def sum_along_z(wires, p, above, below, stage, total, early=EARLY):
    nz, z = wires.nz, wires.at_z
    ups, downs = {}, {}

    def ends(s):
        ups[s] = wires.start(p(s), above.at[s - 1], wires.up, z == 0, (z >= 1) & (z <= s))
        downs[s] = wires.start(
            p(nz - s), below.at[s - 1], wires.down, z == nz - 1, (z + s >= nz - 1) & (z < nz - 1)
        )

    for s in range(1, nz if early else 2):
        ends(s)
    for s in range(2, nz):
        loads = [wires.local(p(s), stage.at[0]), wires.local(p(nz - s), stage.at[1])]
        yield 1
        ups[s - 1].wait_recv()
        downs[s - 1].wait_recv()
        for load in loads:
            load.wait()
        if not early:
            ends(s)
        rising = (z >= 1) & (z < s) & (z < nz - 1)
        falling = (z + s >= nz) & (z < nz - 1) & (z >= 1)
        only(rising, lambda s=s: add_into(above.at[s - 2], stage.at[0]))
        wires.start(above.at[s - 2], above.at[s - 1], wires.up, rising, None, ups[s].index)
        only(falling, lambda s=s: add_into(below.at[s - 2], stage.at[1]))
        wires.start(below.at[s - 2], below.at[s - 1], wires.down, falling, None, downs[s].index)
    load = wires.local(p(0), stage.at[0])
    yield 1
    ups[nz - 1].wait_recv()
    downs[nz - 1].wait_recv()
    load.wait()
    only(z >= 1, lambda: add_into(stage.at[0], above.at[nz - 2]))
    only(z < nz - 1, lambda: add_into(stage.at[0], below.at[nz - 2]))
    if total is not None:
        kept = wires.local(stage.at[0], total)
        yield 1
        kept.wait()


def swap_rows(wires, total, got):
    n = got.shape[0]
    other = pl.ds(pl.multiple_of((1 - wires.at_y) * n, n), n)
    sent = wires.start(total.at[other], got, wires.y)
    yield 1
    sent.wait_recv()


def sum_scratch(nz, rows, cols):
    return [
        pltpu.VMEM((nz - 1, rows, cols), BF16),
        pltpu.VMEM((nz - 1, rows, cols), BF16),
        pltpu.VMEM((2, rows, cols), BF16),
    ]


def swap_outputs(*totals):
    return [jax.ShapeDtypeStruct((t.shape[0] // 2, t.shape[1]), BF16) for t in totals]


def columns(ref, rows, lo, hi):
    return lambda s: ref.at[pl.ds(s * rows, rows), lo:hi]


def gather_weight_rows(wires, sources, out, bounce=None):
    n = out.shape[0] // wires.nz
    slot = lambda s: out.at[pl.ds(s * n, n)]
    yield from exchange_halves(wires, sources, slot(0), bounce)
    yield from along_z(wires, slot(0), slot)


def gather_pack_rows(wires, pack, out):
    n = out.shape[0] // (2 * wires.nz)
    y = wires.at_y

    def slot(s, side):
        return out.at[pl.ds(pl.multiple_of((2 * s + side) * n, n), n)]

    mine = pack.at[y]
    arrival = wires.start(pack.at[1 - y], slot(0, y), wires.y)
    kept = wires.local(mine, slot(0, y))
    own = along_z(wires, mine, lambda s: slot(s, y))
    run(own)
    yield 1
    arrival.wait_recv()
    other = along_z(wires, slot(0, 1 - y), lambda s: slot(s, 1 - y))
    run(other)
    yield 1
    for _ in range(1, wires.nz):
        run(own)
        yield 1
        run(other)
        yield 1
    kept.wait()


def gather_phase(wires, block, out, parts):
    views = [(pl.ds(lo, hi - lo), link) for lo, hi, link in parts]
    on_y = [v for v in views if v[1] == "x"] + [v for v in views if v[1] == "y"]
    on_x = on_y[::-1]
    mine = wires.local(block, out.at[0])
    from_y, from_x, diagonal = {}, {}, []
    c = [wires.start(block, out.at[1], wires.c)]
    for k, (rows, _) in enumerate(on_x):
        from_x[k] = wires.start(block.at[rows], out.at[2, rows], wires.x)
    yield 1
    for k, (rows, _) in enumerate(on_y):
        from_y[k] = wires.start(block.at[rows], out.at[4, rows], wires.y)
    yield 1
    for k in range(len(views)):
        for place, arrived, (rows, link), via, own in (
            (4, from_y[k], on_y[k], wires.x, "x"), (2, from_x[k], on_x[k], wires.y, "y"),
        ):
            arrived.wait_recv()
            if link == own:
                relay = wires.start(out.at[place, rows], out.at[6, rows], via)
                diagonal.append((relay, rows))
            c.append(wires.start(out.at[place, rows], out.at[place + 1, rows], wires.c))
        yield 1
    for relay, rows in diagonal:
        relay.wait_recv()
        c.append(wires.start(out.at[6, rows], out.at[7, rows], wires.c))
        yield 1
    for copy in c:
        copy.wait_recv()
    mine.wait()


def halved(n, cut=None):
    cut = n // 2 if cut is None else cut
    return [(0, cut, "x"), (cut, n, "y")]


def feed_sources(gate, up, down, cut, hidden):
    a, b = cut
    n = b - a
    step = LANES

    def pick(ref):
        return lambda y: ref.at[:, pl.ds(pl.multiple_of(y * hidden + a, step), n)]

    return [(pick(ref), k * n, (k + 1) * n) for k, ref in enumerate((gate, up, down))]


def forward_kernel(
    hidden, cuts,
    x_ref, dout_ref, gain_in, qw_ref, kw_ref, vw_ref, ow_ref, ids_ref, rope_ref, spread_ref,
    squeeze_ref, gate_ref, up_ref, down_ref,
    x_own, dout_own, cos_ref, sin_ref, first_ref, q_ref, k_ref, v_ref, o_ref, lse_ref, gain_ref,
    res_ref, inv_ref, a1_ref, dout_all, w_attn, w_out, w_zero, w_one, w_two, w_three, a2_ref,
    pack, opack, x_all, w_flat, w_pad, w_o, o_slots, o_other, bounce_zero, bounce_one, bounce_two,
    bounce_three, block, cr, xr, yr, tr, br, send, recv, local,
):
    wires = Wires(send, recv, local)
    wires.hello()
    nz, z = wires.nz, wires.at_z
    rows, model = x_ref.shape
    length = 8 * rows
    heads = q_ref.shape[1] // LANES
    keys = rows + WINDOW_LENGTH

    turns = rotation(wires, model)
    at = qw_ref.shape[1] // 2
    for h in range(2):
        pack[h, :, 0:at] = qw_ref[:, h * at : (h + 1) * at]
    for ref in (kw_ref, vw_ref):
        n = ref.shape[0] // 2
        eye = identity(n)
        for h in range(2):
            pack[h, :, at : at + n] = tn(ref[h * n : (h + 1) * n, :], eye).astype(BF16)
        at += n
    rest = pack.shape[2] - at
    row = lax.broadcasted_iota(jnp.int32, (2, rest), 0)
    lane = lax.broadcasted_iota(jnp.int32, (2, rest), 1)
    tail = tn(gain_in[...], (row == lane).astype(BF16)).astype(BF16)
    for h in range(2):
        pack[h, :, at:] = tail
    wires.ready()
    weights = gather_pack_rows(wires, pack, w_flat)
    run(weights)
    for to, of in turns:
        x_own[:, to] = x_ref[:, of]
    tokens = gather_phase(wires, x_own, x_all, halved(rows, START_CUT))
    run(tokens)
    run(weights)
    run(tokens)
    run(weights)
    for to, of in turns:
        dout_own[:, to] = dout_ref[:, of]
    n = ow_ref.shape[1] // 2
    for h in range(2):
        opack[h] = ow_ref[:, h * n : (h + 1) * n]
    run(weights)
    run(tokens)
    run(weights)

    lane = lax.broadcasted_iota(jnp.int32, (1, LANES), 1)
    sign = jnp.where(lane < LANES // 2, -1.0, 1.0)
    steps = length // ROPE_STEP
    cos_low, sin_low = rope_ref[0, steps:, :], rope_ref[1, steps:, :]
    for t in range(steps):
        part = slice(t * ROPE_STEP, (t + 1) * ROPE_STEP)
        cos_high, sin_high = rope_ref[0, t : t + 1, :], rope_ref[1, t : t + 1, :]
        cos_ref[part, :] = cos_high * cos_low - sin_high * sin_low
        sin_ref[part, :] = (sin_high * cos_low + cos_high * sin_low) * sign
    offset = pl.multiple_of(z * length, length)
    ids = ids_ref[:, pl.ds(offset, length)]
    begin = jnp.zeros((1, length), jnp.int32)
    for number in range(1, 5):
        count = jnp.sum((ids_ref[...] < number).astype(jnp.int32), axis=1, keepdims=True)
        begin = jnp.where(ids >= number, count, begin)
    window = lax.broadcasted_iota(jnp.int32, (1, length), 1) - (WINDOW_LENGTH - 1)
    first_ref[...] = jnp.maximum(begin - offset, window) + WINDOW_LENGTH

    run(weights)
    run(tokens)
    run(weights)
    def gather_out():
        y, flat = wires.at_y, opack.shape[2]
        arrival = wires.start(opack.at[1 - y], o_other, wires.y)
        yield 1
        arrival.wait_recv()
        o_slots[0, :, 0:flat] = opack[y]
        o_slots[0, :, flat:] = o_other[...]
        yield from along_z(wires, o_slots.at[0], lambda s: o_slots.at[s])
        n = opack.shape[1]
        for s in range(nz):
            for k, side in enumerate((y, 1 - y)):
                part = pl.ds(pl.multiple_of((2 * s + side) * n, n), n)
                w_o[part, :] = o_slots[s, :, k * flat : (k + 1) * flat]

    out_weights = gather_out()
    zero_weights, one_weights = [
        gather_weight_rows(
            wires, feed_sources(gate_ref, up_ref, down_ref, cut, hidden), out, bounce
        )
        for cut, out, bounce in zip(cuts, (w_zero, w_one), (bounce_zero, bounce_one))
    ]
    exchanges = [
        exchange_halves(
            wires, feed_sources(gate_ref, up_ref, down_ref, cut, hidden), slot, bounce
        )
        for cut, slot, bounce in zip(cuts[2:], (w_two, w_three), (bounce_two, bounce_three))
    ]
    run(out_weights)
    run(zero_weights)
    drain(tokens, weights)
    sent = list(wires.copies)
    quarter = rows // 4
    cotangents = gather_phase(
        wires, dout_own, dout_all, [(t * quarter, (t + 1) * quarter, "x") for t in range(4)]
    )
    run(cotangents)
    run(out_weights)
    run(cotangents)
    for copy in sent:
        copy.wait_send()
    saves = [wires.local(w_flat, w_attn)]

    @pl.loop(0, model // 512)
    def _(t):
        part = pl.ds(pl.multiple_of(t * 512, 512), 512)
        w_pad[part, :] = nn(w_flat[part, :], spread_ref[...]).astype(BF16)

    place = lax.broadcasted_iota(jnp.int32, (8, w_flat.shape[1]), 1)
    row = lax.broadcasted_iota(jnp.int32, (8, w_flat.shape[1]), 0)
    which = (place == (heads + 2) * HEAD_SIZE + row).astype(BF16)
    gain_ref[...] = nt(which, w_flat[...])
    gain = gain_ref[0:1, :]

    @pl.when(z == 0)
    def _():
        k_ref[0:WINDOW_LENGTH, :] = jnp.zeros((WINDOW_LENGTH, LANES), BF16)
        v_ref[0:WINDOW_LENGTH, :] = jnp.zeros((WINDOW_LENGTH, LANES), BF16)

    def project(b, at):
        x = x_all[at].astype(F32)
        inverse = lax.rsqrt(jnp.mean(x * x, axis=1, keepdims=True) + EPS)
        a1 = (x * inverse * gain).astype(BF16)
        x_all[at] = a1
        acc = nn(a1, w_pad[...])
        here = pl.ds(pl.multiple_of(b * rows, rows), rows)
        there = pl.ds(pl.multiple_of(WINDOW_LENGTH + b * rows, rows), rows)
        cosine, sine = cos_ref[here, :], sin_ref[here, :]
        for h in range(heads + 1):
            u = acc[:, h * LANES : (h + 1) * LANES]
            turned = (u * cosine + pltpu.roll(u, LANES // 2, 1) * sine).astype(BF16)
            if h < heads:
                q_ref[here, h * LANES : (h + 1) * LANES] = turned
            else:
                k_ref[there, :] = turned
        v_ref[there, :] = acc[:, (heads + 1) * LANES :].astype(BF16)

    def projected(lo, hi):
        @pl.loop(lo, hi)
        def _(b):
            project(b, wires.natural(b))

        for b in range(lo, hi):
            at = wires.natural(b)
            saves.append(wires.local(x_all.at[at], a1_ref.at[at]))

    projected(6, 8)
    halo = [
        wires.start(
            ref.at[pl.ds(length, WINDOW_LENGTH)], ref.at[pl.ds(0, WINDOW_LENGTH)],
            wires.up, z < nz - 1, z > 0,
        )
        for ref in (k_ref, v_ref)
    ]
    run(zero_weights)
    projected(0, 2)
    run(out_weights)
    projected(2, 6)
    run(zero_weights)
    run(cotangents)
    run(cotangents)
    run(one_weights)
    for copy in halo:
        copy.wait_recv()

    def attend(b, at):
        start = pl.multiple_of(b * rows, rows)
        span = pl.ds(start, keys)
        here = pl.ds(start, rows)
        kb = k_ref[span, :]
        vt = v_ref[span, :].T
        bias = mask_bias(first_ref[:, here] - start, keys, rows)
        outs = []
        for h in range(heads):
            lanes = slice(h * LANES, (h + 1) * LANES)
            s = nt(kb, q_ref[here, lanes]) * (SCALE * LOG2E) + bias
            peak = jnp.max(s, axis=0, keepdims=True)
            p = jnp.exp2(s - peak)
            total = jnp.sum(p, axis=0, keepdims=True)
            ot = nn(vt, p.astype(BF16)) / total
            outs.append(ot.T.astype(BF16))
            lse_ref[b, h : h + 1, :] = peak + jnp.log2(total)
        o_ref[at] = nn(jnp.concatenate(outs, 1), squeeze_ref[...]).astype(BF16)

    def attended(lo, hi):
        @pl.loop(lo, hi)
        def _(b):
            attend(b, wires.natural(b))

    attended(0, 2)
    run(out_weights)
    run(cotangents)
    attended(2, 4)
    run(cotangents)
    run(zero_weights)
    for exchange in exchanges:
        run(exchange)
    attended(4, 6)
    drain(out_weights)
    saves.append(wires.local(w_o, w_out))
    run(one_weights)
    attended(6, 8)
    for save in saves:
        save.wait()

    def emit(part, total):
        residual = x_own[part, :].astype(F32) + total
        inverse = lax.rsqrt(jnp.mean(residual * residual, axis=1, keepdims=True) + EPS)
        res_ref[part, :] = residual
        inv_ref[part, :] = inverse
        block[part, :] = (residual * inverse * gain_ref[1:2, :]).astype(BF16)

    sums = reduce_phase(
        wires, o_ref, w_o, x_all.at[pl.ds(0, 4)], cr, x_all.at[pl.ds(4, 4)], xr, yr, tr, br, emit
    )
    for _ in range(4):
        run(sums)
    drain(zero_weights, cotangents)
    run(sums)
    run(one_weights)
    drain(sums)
    normed = gather_phase(wires, block, a2_ref, halved(rows, NORMED_CUT))
    run(normed)
    run(normed)
    run(one_weights)
    run(normed)
    drain(normed, one_weights, *exchanges)
    wires.finish()


START_CUT = 160
NORMED_CUT = 128


def attention_forward(
    inputs, dout, gains, query, key_t, value_t, out_t, ids, rope, gate, up, down_t, width, cuts
):
    n, model = inputs.shape
    rows = query.shape[0]
    length = 8 * n
    heads = query.shape[1] // 2 // HEAD_SIZE
    hidden = gate.shape[1] // 2
    wide = heads * LANES
    flat = heads * HEAD_SIZE
    half = n // 2
    spread = spread_matrix(heads + 1, 1, rows=width)
    squeeze = spread_matrix(0, heads).T
    sizes = [3 * (b - a) for a, b in cuts]
    b16 = lambda *shape: jax.ShapeDtypeStruct(shape, BF16)
    f32 = lambda *shape: jax.ShapeDtypeStruct(shape, F32)
    v16 = lambda *shape: pltpu.VMEM(shape, BF16)
    return pl.pallas_call(
        functools.partial(forward_kernel, hidden, cuts),
        in_specs=[WHOLE] * 11 + [HBM] * 3,
        out_specs=[WHOLE] * 13 + [HBM] * 9,
        out_shape=[
            b16(n, model), b16(n, model), f32(length, LANES), f32(length, LANES),
            jax.ShapeDtypeStruct((1, length), jnp.int32), b16(length, wide),
            b16(length + WINDOW_LENGTH, LANES), b16(length + WINDOW_LENGTH, LANES),
            b16(8, n, flat), f32(8, heads, n), f32(8, model), f32(n, model), f32(n, 1),
            b16(8, n, model), b16(8, n, model), b16(model, width), b16(model, flat),
            b16(model, sizes[0]), b16(model, sizes[1]), b16(2 * rows, sizes[2]),
            b16(2 * rows, sizes[3]), b16(8, n, model),
        ],
        scratch_shapes=[
            v16(2, rows, width), v16(2, rows, flat), v16(8, n, model), v16(model, width),
            v16(model, spread.shape[1]), v16(model, flat),
            v16(model // (2 * rows), rows, 2 * flat), v16(rows, flat),
        ]
        + [v16(rows, size) for size in sizes]
        + [
            v16(n, model), v16(4, n, model), v16(2, half, model), v16(2, half, model),
            v16(half, model), v16(half, model),
        ]
        + semaphores(),
        compiler_params=params(62, collective_id=0, has_side_effects=True),
        name="attention_forward",
        **light(),
    )(
        inputs, dout, gains, query, key_t, value_t, out_t, ids, rope, spread, squeeze, gate, up,
        down_t,
    )


def feed_kernel(
    hidden, cuts, chunks,
    a_ref, d_ref, w0_ref, w1_ref, w2_ref, w3_ref,
    m_ref, g_ref, w_ref, grad0, grad1, grad2, grad3, total,
    a, d, w, m, g, stage, above, below, extra, send, recv, local,
):
    wires = Wires(send, recv, local)
    nz = wires.nz
    length, model = a.shape
    slot = model // nz
    wires.hello()

    def spots(lo, hi):
        out = []
        for k in range(3):
            for first, last in chunks:
                left, right = max(lo, first), min(hi, last)
                if left < right:
                    base = 2 * hidden if k == 2 else first + k * (last - first)
                    start = base + left
                    out.append((k * (hi - lo) + left - lo, start, right - left, k, left))
        return out

    loads = []
    for ref, (lo, hi) in ((w0_ref, cuts[0]), (w1_ref, cuts[1])):
        for of, to, n, _, _ in spots(lo, hi):
            loads.append(wires.local(ref.at[:, of : of + n], w.at[:, to : to + n]))
    rows = length // 8
    a_loads, d_loads = [], []

    def fetch(half):
        part = pl.ds(half * 4 * rows, 4 * rows)
        a_loads.append(wires.local(a_ref.at[part], a.at[part]))
        d_loads.append(wires.local(d_ref.at[part], d.at[part]))

    fetch(0)

    def carried(ref, cut):
        pieces, copies = [], []
        for of, to, n, _, _ in spots(*cut):
            pieces.append((to, to + n))
            copies.append(wires.local(ref.at[:, of : of + n], w.at[pl.ds(0, slot), to : to + n]))
        yield 1
        for copy in copies:
            copy.wait()
        hops = [
            along_z(
                wires,
                w.at[pl.ds(0, slot), lo:hi],
                lambda s, lo=lo, hi=hi: w.at[pl.ds(s * slot, slot), lo:hi],
            )
            for lo, hi in pieces
        ]
        while hops:
            hops = [hop for hop in hops if next(hop, None) is not None]
            yield 1

    later = [carried(ref, cut) for ref, cut in zip((w2_ref, w3_ref), cuts[2:])]
    for part in later:
        run(part)
    wires.ready()
    run(later[0])
    for copy in loads:
        copy.wait()

    def units(lo, hi, blocks):
        n = hi - lo

        @pl.loop(*blocks)
        def _(b):
            part = pl.ds(pl.multiple_of(b * rows, rows), rows)
            both = nn(a[part, :], w[:, 2 * lo : 2 * hi])
            gate, up = both[:, :n], both[:, n:]
            dmixed = nn(d[part, :], w[:, 2 * hidden + lo : 2 * hidden + hi])
            sigma = jax.nn.sigmoid(gate)
            silu = gate * sigma
            m[part, lo:hi] = (silu * up).astype(BF16)
            g[part, lo + hi : 2 * hi] = (dmixed * silu).astype(BF16)
            g[part, 2 * lo : lo + hi] = (
                dmixed * up * sigma * (1.0 + gate * (1.0 - sigma))
            ).astype(BF16)

    tile = stage.shape[1]
    last = model // tile

    def weight_grads(lo, hi, out, tiles=None):
        n = hi - lo
        tiles = (0, last) if tiles is None else tiles

        def save(t):
            return pltpu.make_async_copy(
                stage.at[t % 2, :, 0 : 3 * n],
                out.at[pl.ds(pl.multiple_of(t * tile, tile), tile)],
                local.at[24 + 4 * nz - 1 - t % 2],
            )

        @pl.loop(*tiles)
        def _(t):
            @pl.when(t >= 2)
            def _():
                save(t - 2).wait()

            cols = pl.ds(pl.multiple_of(t * tile, tile), tile)
            stage[t % 2, :, 0 : 2 * n] = tn(a[:, cols], g[:, 2 * lo : 2 * hi]).astype(BF16)
            stage[t % 2, :, 2 * n : 3 * n] = tn(d[:, cols], m[:, lo:hi]).astype(BF16)
            save(t).start()

        if tiles[1] == last:
            save(last - 2).wait()
            save(last - 1).wait()

    a_loads[0].wait()
    d_loads[0].wait()
    fetch(1)
    units(*chunks[0], (0, 4))
    a_loads[1].wait()
    d_loads[1].wait()
    units(*chunks[0], (4, 8))
    weight_grads(*chunks[0], grad0, (0, 2))
    run(later[0])
    weight_grads(*chunks[0], grad0, (2, last))
    sums = sum_along_z(
        wires, columns(grad0, slot, 0, total.shape[1]), above, below, extra, total, False
    )
    run(sums)
    units(*chunks[1], (0, 8))
    run(later[0])
    weight_grads(*chunks[1], grad1, (0, 4))
    run(later[1])
    weight_grads(*chunks[1], grad1, (4, last))
    drain(later[0])
    run(sums)
    units(*chunks[2], (0, 4))
    run(later[1])
    units(*chunks[2], (4, 8))
    weight_grads(*chunks[2], grad2, (0, 2))
    run(later[1])
    run(sums)
    weight_grads(*chunks[2], grad2, (2, last))
    drain(later[1])
    outs = [wires.local(w, w_ref)]
    units(*chunks[3], (0, 8))
    outs += [wires.local(m, m_ref), wires.local(g, g_ref)]
    weight_grads(*chunks[3], grad3)
    drain(sums)
    for copy in outs:
        copy.wait()
    wires.finish()


def feed_forward(a2, dout, w0, w1, w2, w3, cuts, chunks):
    length, model = a2.shape
    hidden = cuts[-1][1]
    sizes = [b - a for a, b in chunks]
    rows = w3.shape[0]
    nz = model // rows
    return pl.pallas_call(
        functools.partial(feed_kernel, hidden, cuts, chunks),
        in_specs=[HBM] * 6,
        out_specs=[HBM] * 8,
        out_shape=[
            jax.ShapeDtypeStruct((length, hidden), BF16),
            jax.ShapeDtypeStruct((length, 2 * hidden), BF16),
            jax.ShapeDtypeStruct((model, 3 * hidden), BF16),
        ]
        + [jax.ShapeDtypeStruct((model, 3 * n), BF16) for n in sizes]
        + [jax.ShapeDtypeStruct((rows, 3 * sizes[0]), BF16)],
        scratch_shapes=[
            pltpu.VMEM((length, model), BF16),
            pltpu.VMEM((length, model), BF16),
            pltpu.VMEM((model, 3 * hidden), BF16),
            pltpu.VMEM((length, hidden), BF16),
            pltpu.VMEM((length, 2 * hidden), BF16),
            pltpu.VMEM((2, 512, 3 * max(sizes)), BF16),
        ]
        + sum_scratch(nz, rows, 3 * sizes[0])
        + semaphores(),
        compiler_params=params(62, collective_id=1, has_side_effects=True),
        name="feed_forward",
        **light(),
    )(a2, dout, w0, w1, w2, w3)


def reduce_phase(wires, a, w, cs, cr, q, xr, yr, tr, br, emit, ready=None):
    n = q.shape[1]
    half = n // 2
    top, bottom = pl.ds(0, half), pl.ds(half, half)
    model = q.shape[2]
    tile = 512
    deep = a.shape[2]

    def product(place, target):
        if ready is not None:
            ready(place)

        @pl.loop(0, model // tile)
        def _(t):
            cols = pl.ds(pl.multiple_of(t * tile, tile), tile)
            target[:, cols] = nt(a[place], w[cols, 0:deep]).astype(BF16)

    waits = {}
    for j in (3, 1, 2, 0):
        product(2 * j + 1, cs.at[j])
        got = wires.start(cs.at[j], cr.at[j], wires.c)
        product(2 * j, q.at[j])
        got.wait_recv()
        q[j] = (q[j].astype(F32) + cr[j].astype(F32)).astype(BF16)
        if j == 3:
            waits["x1"] = wires.start(q.at[3, top], xr.at[1], wires.x)
            waits["y1"] = wires.start(q.at[3, bottom], yr.at[1], wires.y)
        if j == 1:
            waits["x0"] = wires.start(q.at[1, top], xr.at[0], wires.x)
        if j == 2:
            waits["y0"] = wires.start(q.at[2, bottom], yr.at[0], wires.y)
        yield 1
    waits["x1"].wait_recv()
    q[2, top] = (q[2, top].astype(F32) + xr[1].astype(F32)).astype(BF16)
    waits["t"] = wires.start(q.at[2, top], tr, wires.y)
    waits["y1"].wait_recv()
    q[1, bottom] = (q[1, bottom].astype(F32) + yr[1].astype(F32)).astype(BF16)
    waits["b"] = wires.start(q.at[1, bottom], br, wires.x)
    yield 1
    waits["x0"].wait_recv()
    yield 1
    waits["t"].wait_recv()
    emit(top, q[0, top].astype(F32) + xr[0].astype(F32) + tr[...].astype(F32))
    waits["y0"].wait_recv()
    waits["b"].wait_recv()
    emit(bottom, q[0, bottom].astype(F32) + yr[0].astype(F32) + br[...].astype(F32))


def reduce_scratch(n, model):
    half = n // 2
    return [
        pltpu.VMEM((4, n, model), BF16),
        pltpu.VMEM((4, n, model), BF16),
        pltpu.VMEM((4, n, model), BF16),
        pltpu.VMEM((2, half, model), BF16),
        pltpu.VMEM((2, half, model), BF16),
        pltpu.VMEM((half, model), BF16),
        pltpu.VMEM((half, model), BF16),
    ]


def middle_kernel(
    a_ref, w_ref, dout_ref, res_ref, inv_ref, gain_ref, grad0, grad2,
    dres_ref, out_ref, total0, total2,
    a, w, block, cs, cr, q, xr, yr, tr, br,
    above0, below0, stage0, above2, below2, stage2, send, recv, local,
):
    wires = Wires(send, recv, local)
    wires.hello()
    load_w = wires.local(w_ref.at[:, 0 : w.shape[1]], w)
    loads = {place: wires.local(a_ref.at[place], a.at[place]) for place in (7, 6, 3, 2, 5, 4, 1, 0)}
    wires.ready()
    rows = total0.shape[0]
    first = sum_along_z(
        wires, columns(grad0, rows, 0, total0.shape[1]), above0, below0, stage0, total0
    )
    second = sum_along_z(
        wires, columns(grad2, rows, 0, total2.shape[1]), above2, below2, stage2, total2, False
    )
    run(first)

    def emit(rows, total):
        inverse = inv_ref[rows, :]
        normed = res_ref[rows, :] * inverse
        e = total * gain_ref[1:2, :]
        back = inverse * (e - normed * jnp.mean(e * normed, axis=1, keepdims=True))
        dres = dout_ref[rows, :].astype(F32) + back
        dres_ref[rows, :] = dres
        block[rows, :] = dres.astype(BF16)

    load_w.wait()
    sums = reduce_phase(
        wires, a, w, cs, cr, q, xr, yr, tr, br, emit, lambda place: loads[place].wait()
    )
    for _ in range(4):
        run(sums)
    run(first)
    run(sums)
    run(sums)
    run(first)
    run(second)
    drain(sums)
    tokens = gather_phase(wires, block, out_ref, halved(block.shape[0]))
    run(tokens)
    run(tokens)
    run(first)
    run(second)
    run(tokens)
    run(second)
    run(tokens)
    drain(second, tokens, first)
    wires.finish()


def feed_back(dgu, w, dout, residual, inverse, gain, grad0, grad2):
    n, model = dout.shape
    k = dgu.shape[1]
    rows = 2 * model // lax.axis_size("tok")
    nz = model // rows
    half, small = grad0.shape[1], grad2.shape[1]
    return pl.pallas_call(
        middle_kernel,
        in_specs=[HBM] * 2 + [WHOLE] * 4 + [HBM] * 2,
        out_specs=[WHOLE] + [HBM] * 3,
        out_shape=[
            jax.ShapeDtypeStruct((n, model), F32),
            jax.ShapeDtypeStruct((8, n, model), BF16),
            jax.ShapeDtypeStruct((rows, half), BF16),
            jax.ShapeDtypeStruct((rows, small), BF16),
        ],
        scratch_shapes=[
            pltpu.VMEM((8, n, k), BF16),
            pltpu.VMEM((model, k), BF16),
            pltpu.VMEM((n, model), BF16),
        ]
        + reduce_scratch(n, model)
        + sum_scratch(nz, rows, half)
        + sum_scratch(nz, rows, small)
        + semaphores(),
        compiler_params=params(62, collective_id=3, has_side_effects=True),
        name="feed_back",
        **light(),
    )(dgu.reshape(8, n, k), w, dout, residual, inverse, gain, grad0, grad2)


def back_kernel(
    da_ref, w_ref, o_ref, q_ref, k_ref, v_ref, lse_ref, first_ref, cos_ref, sin_ref,
    spread_ref, squeeze_ref, final_ref, m_ref, down_ref, res_ref, grad1, sum0, sum1, sum2,
    dqkv_ref, out_ref, grad_out, total, got0, got1, got2,
    da, do, dk, dv, halo, fetched, m, w_down, cr, xr, yr, tr, br,
    above, below, stage, stage1, res, send, recv, local,
):
    wires = Wires(send, recv, local)
    nz, z = wires.nz, wires.at_z
    wires.hello()
    n, model = da.shape[1], da.shape[2]
    heads = q_ref.shape[1] // LANES
    wide = heads * HEAD_SIZE
    keys = n + WINDOW_LENGTH
    length = 8 * n
    loads = [wires.local(da_ref.at[b], da.at[b]) for b in range(8)]
    late = [
        wires.local(m_ref, m),
        wires.local(down_ref.at[:, 2 * m.shape[2] :], w_down),
    ]
    rows = total.shape[0]
    wires.ready()
    carried = sum_along_z(
        wires, columns(grad1, rows, 0, total.shape[1]), above, below, stage, total
    )
    run(carried)
    swaps = [
        swap_rows(wires, s, got) for s, got in ((sum0, got0), (sum1, got1), (sum2, got2))
    ]
    for swap in swaps:
        run(swap)
    dk[...] = jnp.zeros_like(dk)
    dv[...] = jnp.zeros_like(dv)
    for b in range(8):
        loads[b].wait()
        flat = nn(da[b], w_ref[...]).astype(BF16)
        do[b] = nn(flat, spread_ref[...]).astype(BF16)

    saves = []
    for t in range(nz):
        cols = slice(t * rows, (t + 1) * rows)
        if t >= 2:
            saves[t - 2].wait()
        total = None
        for b in range(8):
            part = tn(da[b, :, cols], o_ref[b])
            total = part if total is None else total + part
        half = rows // 2
        for h in range(2):
            part = total[h * half : (h + 1) * half].astype(BF16)
            stage1[t % 2, :, h * wide : (h + 1) * wide] = part
        saves.append(wires.local(stage1.at[t % 2], grad_out.at[pl.ds(t * half, half)]))
    for save in saves[-2:]:
        save.wait()
    for load in late:
        load.wait()
    turns = rotation(wires, model)

    def emit(part, total):
        load = wires.local(res_ref.at[part], res)
        load.wait()
        layer = (res[...] + total).astype(BF16)
        for of, to in turns:
            out_ref[part, to] = layer[:, of]

    sums = reduce_phase(
        wires, m, w_down, da.at[pl.ds(0, 4)], cr, da.at[pl.ds(4, 4)], xr, yr, tr, br, emit
    )
    run(sums)
    run(sums)
    run(carried)
    run(sums)
    run(sums)

    def block(b, at):
        start = pl.multiple_of(b * n, n)
        span = pl.ds(start, keys)
        here = pl.ds(start, n)
        kb = k_ref[span, :]
        vb = v_ref[span, :]
        kt = kb.T
        bias = mask_bias(first_ref[:, here] - start, keys, n)
        cosine, sine = cos_ref[here, :], sin_ref[here, :]
        dqs = []
        dk_sum = dv_sum = None
        for h in range(heads):
            lanes = slice(h * LANES, (h + 1) * LANES)
            qh = q_ref[here, lanes]
            doh = do[at, :, lanes]
            p = jnp.exp2(nt(kb, qh) * (SCALE * LOG2E) + (bias - lse_ref[b, h : h + 1, :]))
            t = p * nt(vb, doh)
            inner = jnp.sum(t, axis=0, keepdims=True)
            ds = (t - p * inner).astype(BF16)
            dq = nn(kt, ds).T * SCALE
            dqs.append((dq * cosine - pltpu.roll(dq, LANES // 2, 1) * sine).astype(BF16))
            dk_h = nn(ds, qh)
            dv_h = nn(p.astype(BF16), doh)
            dk_sum = dk_h if dk_sum is None else dk_sum + dk_h
            dv_sum = dv_h if dv_sum is None else dv_sum + dv_h
        dqkv_ref[at, :, 0:wide] = nn(jnp.concatenate(dqs, 1), squeeze_ref[...]).astype(BF16)
        dk[span, :] += dk_sum
        dv[span, :] += dv_sum

    def blocks(lo, hi):
        @pl.loop(lo, hi)
        def _(b):
            block(b, wires.natural(b))

    blocks(0, 2)
    halo[:, 0:LANES] = dk[0:WINDOW_LENGTH, :].astype(BF16)
    halo[:, LANES:] = dv[0:WINDOW_LENGTH, :].astype(BF16)
    borrowed = wires.start(halo, fetched, wires.down, z >= 1, z < nz - 1)
    run(sums)
    blocks(2, 4)
    run(carried)
    blocks(4, 8)
    drain(sums)
    borrowed.wait_recv()

    @pl.when(z < nz - 1)
    def _():
        dk[length:, :] += fetched[:, 0:LANES].astype(F32)
        dv[length:, :] += fetched[:, LANES:].astype(F32)

    for b in range(8):
        here = slice(b * n, (b + 1) * n)
        there = slice(WINDOW_LENGTH + b * n, WINDOW_LENGTH + (b + 1) * n)
        dkb = dk[there, :] * SCALE
        dkb = dkb * cos_ref[here, :] - pltpu.roll(dkb, LANES // 2, 1) * sin_ref[here, :]
        both = jnp.concatenate([dkb.astype(BF16), dv[there, :].astype(BF16)], 1)
        dqkv_ref[wires.natural(b), :, wide:] = nn(both, final_ref[...]).astype(BF16)
    drain(carried, *swaps)
    wires.finish()


def attention_back(
    da_all, w_out, o, q, k_all, v_all, lse, first_key, cosine, sine, mixed, w_feed, residual, grad1,
    sums, width,
):
    _, n, model = da_all.shape
    length = 8 * n
    heads = q.shape[1] // LANES
    wide = heads * HEAD_SIZE
    spread = spread_matrix(0, heads)
    squeeze = spread_matrix(heads, 0).T
    final = spread_matrix(1, 1, rows=width - wide).T
    rows = 2 * model // lax.axis_size("tok")
    nz = model // rows
    hidden = mixed.shape[1]
    half = n // 2
    return pl.pallas_call(
        back_kernel,
        in_specs=[HBM] + [WHOLE] * 12 + [HBM] * 7,
        out_specs=[WHOLE, WHOLE] + [HBM] * 5,
        out_shape=[
            jax.ShapeDtypeStruct((8, n, width), BF16),
            jax.ShapeDtypeStruct((n, model), BF16),
            jax.ShapeDtypeStruct((model // 2, 2 * wide), BF16),
            jax.ShapeDtypeStruct((rows, grad1.shape[1]), BF16),
        ]
        + swap_outputs(*sums),
        scratch_shapes=[
            pltpu.VMEM((8, n, model), BF16),
            pltpu.VMEM((8, n, heads * LANES), BF16),
            pltpu.VMEM(k_all.shape, F32),
            pltpu.VMEM(k_all.shape, F32),
            pltpu.VMEM((WINDOW_LENGTH, 2 * LANES), BF16),
            pltpu.VMEM((WINDOW_LENGTH, 2 * LANES), BF16),
            pltpu.VMEM((8, n, hidden), BF16),
            pltpu.VMEM((model, hidden), BF16),
            pltpu.VMEM((4, n, model), BF16),
            pltpu.VMEM((2, half, model), BF16),
            pltpu.VMEM((2, half, model), BF16),
            pltpu.VMEM((half, model), BF16),
            pltpu.VMEM((half, model), BF16),
        ]
        + sum_scratch(nz, rows, grad1.shape[1])
        + [pltpu.VMEM((2, rows // 2, 2 * wide), BF16), pltpu.VMEM((half, model), F32)]
        + semaphores(),
        compiler_params=params(63, collective_id=6, has_side_effects=True),
        name="attention_back",
        **light(),
    )(
        da_all, w_out, o, q, k_all, v_all, lse, first_key, cosine, sine, spread, squeeze, final,
        mixed.reshape(8, n, hidden), w_feed, residual, grad1, *sums,
    )


def last_kernel(
    a_ref, w_ref, x_ref, gain_ref, dres_ref, a1_ref, grad_out, sum0,
    out_ref, total, total1, got0, got, got1,
    cs, cr, q, xr, yr, tr, br, a1, grad, above, below, stage, above1, below1, stage1, o_rows,
    send, recv, local,
):
    wires = Wires(send, recv, local)
    wires.hello()
    rows = total.shape[0]
    model = a1.shape[2]
    loads = [wires.local(a1_ref.at[b], a1.at[b]) for b in range(8)]
    turns = rotation(wires, model)

    def emit(rows, total):
        x = x_ref[rows, :].astype(F32)
        inverse = lax.rsqrt(jnp.mean(x * x, axis=1, keepdims=True) + EPS)
        normed = x * inverse
        e = total * gain_ref[0:1, :]
        back = inverse * (e - normed * jnp.mean(e * normed, axis=1, keepdims=True))
        done = dres_ref[rows, :] + back
        for of, to in turns:
            out_ref[rows, to] = done[:, of]

    wires.ready()
    first = sum_along_z(
        wires, columns(grad_out, rows // 2, 0, grad_out.shape[1]), above1, below1, stage1, None
    )
    run(first)
    swap = swap_rows(wires, sum0, got0)
    run(swap)
    for load in loads:
        load.wait()
    tile = 640

    def weight_grads(lo, hi):
        @pl.loop(lo, hi)
        def _(t):
            cols = pl.ds(pl.multiple_of(t * tile, tile), tile)
            total = None
            for b in range(8):
                part = tn(a1[b, :, cols], a_ref[b])
                total = part if total is None else total + part
            grad[cols, :] = total.astype(BF16)

    weight_grads(0, 2)
    run(first)
    weight_grads(2, 4)
    carried = sum_along_z(
        wires, columns(grad, rows, 0, total.shape[1]), above, below, stage, total
    )
    run(carried)
    sums = reduce_phase(wires, a_ref, w_ref, cs, cr, q, xr, yr, tr, br, emit)
    run(sums)
    run(sums)
    run(first)
    run(sums)
    run(sums)
    run(sums)
    run(carried)
    run(first)
    run(sums)
    run(carried)
    drain(sums)
    drain(first)
    half, wide = o_rows.shape[1:]
    for h in range(2):
        o_rows[h] = stage1[0, :, h * wide : (h + 1) * wide]
    keep = wires.local(o_rows.at[0], total1.at[0:half]), wires.local(o_rows.at[1], total1.at[half:])
    sent = wires.start(o_rows.at[1 - wires.at_y], got1, wires.y)
    drain(carried)
    drain(swap_rows(wires, total, got), swap)
    sent.wait_recv()
    for copy in keep:
        copy.wait()
    wires.finish()


def input_back(dqkv, w, inputs, gain, dres, a1, grad_out, total):
    n, model = inputs.shape
    rows = 2 * model // lax.axis_size("tok")
    nz = model // rows
    wide = dqkv.shape[2]
    return pl.pallas_call(
        last_kernel,
        in_specs=[WHOLE] * 5 + [HBM] * 3,
        out_specs=[WHOLE] + [HBM] * 5,
        out_shape=[
            jax.ShapeDtypeStruct((n, model), F32),
            jax.ShapeDtypeStruct((rows, wide), BF16),
            jax.ShapeDtypeStruct((rows, grad_out.shape[1] // 2), BF16),
            jax.ShapeDtypeStruct((rows // 2, total.shape[1]), BF16),
            jax.ShapeDtypeStruct((rows // 2, wide), BF16),
            jax.ShapeDtypeStruct((rows // 2, grad_out.shape[1] // 2), BF16),
        ],
        scratch_shapes=reduce_scratch(n, model)
        + [pltpu.VMEM((8, n, model), BF16), pltpu.VMEM((model, wide), BF16)]
        + sum_scratch(nz, rows, wide)
        + sum_scratch(nz, rows // 2, grad_out.shape[1])
        + [pltpu.VMEM((2, rows // 2, grad_out.shape[1] // 2), BF16)]
        + semaphores(),
        compiler_params=params(62, collective_id=4, has_side_effects=True),
        name="input_back",
        **light(),
    )(dqkv, w, inputs, gain, dres, a1, grad_out, total)


def finish_kernel(
    chunks, y_ref, *refs,
):
    count = len(chunks) + 2
    mine, got = refs[0 : 2 * count : 2], refs[1 : 2 * count : 2]
    qw, kw, vw, gw, uw, layer, dinput = refs[2 * count : 2 * count + 7]
    gate, up, down, out, query, key, value, sums, row_sums, layer_out, dinput_out, local = refs[
        2 * count + 7 :
    ]
    copies = [
        pltpu.make_async_copy(layer, layer_out, local.at[0]),
        pltpu.make_async_copy(dinput, dinput_out, local.at[1]),
    ]
    for copy in copies:
        copy.start()
    rows = gate.shape[0]
    hidden = gate.shape[1] // 2
    eye = identity(rows)
    wide = lambda v: v.astype(F32)

    def place(h, pieces):
        for (lo, hi), piece in zip(chunks, pieces):
            n = hi - lo
            at = slice(h * hidden + lo, h * hidden + hi)
            for k, ref in enumerate((gate, up, down)):
                ref[:, at] = wide(piece[:, k * n : (k + 1) * n])
        o, q = pieces[-2:]
        for ref, piece in ((out, o), (query, q)):
            n = ref.shape[1] // 2
            ref[:, h * n : (h + 1) * n] = wide(piece[:, 0:n])
        start = query.shape[1] // 2
        for ref in (key, value):
            n = ref.shape[0] // 2
            ref[h * n : (h + 1) * n, :] = tn(q[:, start : start + n], eye)
            start += n

    @pl.when(y_ref[0] == 0)
    def _():
        place(0, [ref.at[0:rows] for ref in mine])
        place(1, got)

    @pl.when(y_ref[0] == 1)
    def _():
        place(0, got)
        place(1, [ref.at[rows:] for ref in mine])

    def total(w, g, axis):
        return jnp.sum(w[...].astype(F32) * g[...], axis=axis, keepdims=True)

    sums[:, 0:1] = total(qw, query, 1)
    sums[:, 1:2] = total(gw, gate, 1) + total(uw, up, 1)
    row_sums[...] = total(kw, key, 0) + total(vw, value, 0)
    for copy in copies:
        copy.wait()


def finish(y, pieces, weights, out_columns, chunks, layer, dinput):
    query, key_t, _, gate, _ = weights
    rows, hidden = gate.shape
    f32 = lambda *shape: jax.ShapeDtypeStruct(shape, F32)
    return pl.pallas_call(
        functools.partial(finish_kernel, chunks),
        in_specs=[pl.BlockSpec(memory_space=pltpu.SMEM)]
        + [WHOLE] * (len(pieces) + len(weights) + 2),
        out_specs=[WHOLE] * 9 + [HBM] * 2,
        out_shape=[
            f32(rows, hidden), f32(rows, hidden), f32(rows, hidden), f32(rows, out_columns),
            f32(*query.shape), f32(*key_t.shape), f32(*key_t.shape), f32(rows, 2), f32(1, rows),
            jax.ShapeDtypeStruct(layer.shape, layer.dtype),
            jax.ShapeDtypeStruct(dinput.shape, dinput.dtype),
        ],
        scratch_shapes=[pltpu.SemaphoreType.DMA((2,))],
        compiler_params=params(62),
        name="finish",
        **light(),
    )(y, *pieces, *weights, layer, dinput)


def body(
    inputs,
    grad_output,
    segments,
    attention_gain,
    query_weight,
    key_matrix,
    value_matrix,
    output_weight,
    feedforward_gain,
    gate_weight,
    up_weight,
    down_weight,
):
    grid = Grid()
    bf16 = jnp.bfloat16
    model = inputs.shape[1]
    length = inputs.shape[0] * 8
    hidden = gate_weight.shape[1] // 2
    qdim = query_weight.shape[1] // 2
    kdim = key_matrix.shape[1] // 2
    cuts = []
    at = 0
    for n in FF_CHUNKS:
        cuts.append((at, at + n))
        at += n
    heads = qdim // HEAD_SIZE

    width = -(-(qdim + 2 * kdim + 2) // LANES) * LANES

    (
        own, dout, cosine, sine, first_key, q, k_all, v_all, o, lse, gains, residual, inverse_two,
        a1, dout_all, w_attn, w_out, w_zero, w_one, w_two, w_three, a2,
    ) = attention_forward(
        outside_rotation(grid, inputs), outside_rotation(grid, grad_output),
        jnp.stack([attention_gain, feedforward_gain]),
        query_weight, key_matrix.T, value_matrix.T, output_weight.T,
        segments[None, :], rope_parts(length, grid.z * length, HEAD_SIZE),
        gate_weight, up_weight, down_weight.T, width, cuts,
    )
    flat = lambda v: v.reshape(length, v.shape[-1])

    chunks = []
    at = 0
    for n in FF_PARTS:
        chunks.append((at, at + n))
        at += n
    mixed, dgu, w_feed, grad0, grad1, grad2, grad3, sum_0 = feed_forward(
        flat(a2), flat(dout_all), w_zero, w_one, w_two, w_three, cuts, chunks
    )
    dresidual, da_all, sum_1, sum_3 = feed_back(
        dgu, w_feed, dout, residual, inverse_two, gains, grad1, grad3
    )
    dqkv, layer, grad_o, sum_2, got_0, got_1, got_3 = attention_back(
        da_all, w_out, o, q, k_all, v_all, lse, first_key, cosine, sine, mixed, w_feed, residual,
        grad2, (sum_0, sum_1, sum_3), width,
    )
    dinput, sum_q, sum_o, got_2, got_q, got_o = input_back(
        dqkv, w_attn, own, gains, dresidual, a1, grad_o, sum_2
    )
    pieces = (
        sum_0, got_0, sum_1, got_1, sum_2, got_2, sum_3, got_3, sum_o, got_o, sum_q, got_q
    )
    (
        gate_grad, up_grad, down_grad, output_grad, query_grad, key_grad, value_grad, sums,
        row_sums, layer, dinput,
    ) = finish(
        jnp.reshape(grid.y, (1,)).astype(jnp.int32),
        pieces,
        (query_weight, key_matrix.T, value_matrix.T, gate_weight, up_weight),
        output_weight.shape[0],
        chunks,
        layer,
        dinput,
    )
    sums = jnp.stack([sums[:, 0] + row_sums[0], sums[:, 1]])
    sums = (sums + grid.swap(sums, C)) + (grid.swap(sums, X) + grid.swap(sums, X | C))
    return (
        outside_rotation(grid, layer),
        outside_rotation(grid, dinput),
        sums[0] / attention_gain.astype(jnp.float32),
        query_grad,
        key_grad.T,
        value_grad.T,
        output_grad.T,
        sums[1] / feedforward_gain.astype(jnp.float32),
        gate_grad,
        up_grad,
        down_grad.T,
    )


def solution(mesh):
    in_specs = (
        P(("tok", "mp"), None),
        P(("tok", "mp"), None),
        P(),
        P("tok"),
        P("tok", "mp"),
        P("tok", "mp"),
        P("tok", "mp"),
        P("mp", "tok"),
        P("tok"),
        P("tok", "mp"),
        P("tok", "mp"),
        P("mp", "tok"),
    )
    out_specs = (
        P(("tok", "mp"), None),
        P(("tok", "mp"), None),
        P("tok"),
        P("tok", "mp"),
        P("tok", "mp"),
        P("tok", "mp"),
        P("mp", "tok"),
        P("tok"),
        P("tok", "mp"),
        P("tok", "mp"),
        P("mp", "tok"),
    )
    return jax.shard_map(body, mesh=mesh, in_specs=in_specs, out_specs=out_specs, check_vma=False)
```

```python
import functools

import jax
import jax.numpy as jnp
import ml_dtypes
import numpy as np
from jax import lax
from jax.experimental import pallas as pl
from jax.experimental.pallas import tpu as pltpu
from jax.sharding import PartitionSpec as P

HEAD_SIZE = 80
WINDOW_LENGTH = 512
EPS = 1e-05
THETA = 1000000.0
FLOOR = -1e30
AXES = ("tok", "mp")
FF_CHUNKS = (128, 384, 256, 128)
FF_PARTS = (256, 256, 256, 128)


class Grid:
    def __init__(self):
        self.nz = lax.axis_size("tok") // 2
        tok = lax.axis_index("tok")
        mp = lax.axis_index("mp")
        self.z, self.y = tok // 2, tok % 2
        self.x, self.c = mp // 2, mp % 2
        self.me = self.y * 4 + self.x * 2 + self.c

    def pairs(self, move):
        out = []
        for z in range(self.nz):
            for g in range(8):
                target = move(z, g)
                if target is not None:
                    out.append((z * 8 + g, target[0] * 8 + target[1]))
        return out

    def swap(self, value, bit):
        return lax.ppermute(value, AXES, self.pairs(lambda z, g: (z, g ^ bit)))

    def ring(self, value):
        return lax.ppermute(value, AXES, self.pairs(lambda z, g: ((z + 1) % self.nz, g)))

    def step(self, value, d):
        def move(z, g):
            return (z + d, g) if 0 <= z + d < self.nz else None

        return lax.ppermute(value, AXES, self.pairs(move))


Y, X, C = 4, 2, 1


LANES = 128
SCALE = HEAD_SIZE ** (-0.5)
LOG2E = 1.4426950408889634
MIB = 1024 * 1024
BF16 = jnp.bfloat16
F32 = jnp.float32
HBM = pl.BlockSpec(memory_space=pl.ANY)
WHOLE = pl.BlockSpec(memory_space=pltpu.VMEM)
MESH = pl.DeviceIdType.MESH


def light(**kwargs):
    return dict(
        cost_estimate=pl.CostEstimate(flops=1000000, bytes_accessed=100000, transcendentals=0),
        **kwargs,
    )


def params(mib, **kwargs):
    return pltpu.CompilerParams(vmem_limit_bytes=mib * MIB, **kwargs)


ROPE_STEP = 64


def rope_parts(count, first, width):
    half = width // 2
    freqs = THETA ** (-(jnp.arange(half, dtype=jnp.int32).astype(F32) * 2.0 / width))
    high = first + ROPE_STEP * jnp.arange(count // ROPE_STEP, dtype=jnp.int32)
    places = jnp.concatenate([high, jnp.arange(ROPE_STEP, dtype=jnp.int32)]).astype(F32)
    blank = jnp.zeros((LANES // 2 - half,), F32)
    lanes = jnp.concatenate([freqs, blank, freqs, blank])
    angles = places[:, None] * lanes[None, :]
    return jnp.stack([jnp.cos(angles), jnp.sin(angles)])


def spread_matrix(turned, plain, rows=0, columns=0):
    half = HEAD_SIZE // 2
    f = np.arange((turned + plain) * HEAD_SIZE)
    head, place = f // HEAD_SIZE, f % HEAD_SIZE
    target = head * LANES + place
    target = target + np.where((head < turned) & (place >= half), LANES // 2 - half, 0)
    out = np.zeros(
        (max(rows, f.size), max(columns, (turned + plain) * LANES)), ml_dtypes.bfloat16
    )
    out[f, target] = 1
    return out


def nt(left, right):
    return lax.dot_general(left, right, (((1,), (1,)), ((), ())), preferred_element_type=F32)


def nn(left, right):
    return lax.dot_general(left, right, (((1,), (0,)), ((), ())), preferred_element_type=F32)


def tn(left, right):
    return lax.dot_general(left, right, (((0,), (0,)), ((), ())), preferred_element_type=F32)


def mask_bias(first, keys, rows):
    kk = lax.broadcasted_iota(jnp.int32, (keys, rows), 0)
    qq = lax.broadcasted_iota(jnp.int32, (keys, rows), 1)
    return jnp.where((kk >= first) & (kk - qq <= WINDOW_LENGTH), 0.0, FLOOR)


def identity(n):
    i = lax.broadcasted_iota(jnp.int32, (n, n), 0)
    return (i == lax.broadcasted_iota(jnp.int32, (n, n), 1)).astype(BF16)


def rotation(wires, model):
    width = model // wires.nz
    if width % LANES:
        return [(slice(0, model), slice(0, model))]
    out = []
    for s in range(wires.nz):
        block = lax.rem(wires.at_z - s + wires.nz, wires.nz)
        start = pl.multiple_of(block * width, LANES)
        out.append((slice(s * width, (s + 1) * width), pl.ds(start, width)))
    return out


def outside_rotation(grid, value, back=False):
    width = value.shape[-1] // grid.nz
    if width % LANES == 0:
        return value
    parts = []
    for s in range(grid.nz):
        block = lax.rem(grid.z - s + grid.nz, grid.nz)
        parts.append(lax.dynamic_slice_in_dim(value, block * width, width, value.ndim - 1))
    return jnp.concatenate(parts, -1)


def only(condition, act):
    if condition is None:
        act()
    else:
        pl.when(condition)(act)


class Copy:
    def __init__(self, copy, when, got, index):
        self.copy, self.when, self.got, self.index = copy, when, got, index
        self.sent = False

    def wait_recv(self):
        only(self.got, self.copy.wait_recv)

    def wait_send(self):
        if not self.sent:
            only(self.when, self.copy.wait_send)
        self.sent = True


def semaphores():
    nz = lax.axis_size("tok") // 2
    return [
        pltpu.SemaphoreType.DMA((48 + 16 * nz,)),
        pltpu.SemaphoreType.DMA((48 + 16 * nz,)),
        pltpu.SemaphoreType.DMA((24 + 4 * nz,)),
    ]


class Wires:
    def __init__(self, send, recv, local):
        self.send, self.recv, self.here = send, recv, local
        self.count = self.local_count = 0
        self.copies = []
        tokens = lax.axis_size("tok")
        tok, mp = lax.axis_index("tok"), lax.axis_index("mp")
        self.nz = tokens // 2
        self.at_z, self.at_y = tok // 2, tok % 2
        self.at_x, self.at_c = mp // 2, mp % 2
        self.x = (tok, lax.rem(mp + 2, 4))
        self.y = (tok + 1 - 2 * self.at_y, mp)
        self.c = (tok, mp + 1 - 2 * self.at_c)
        self.up = (lax.rem(tok + 2, tokens), mp)
        self.down = (lax.rem(tok + tokens - 2, tokens), mp)

    def hello(self):
        barrier = pltpu.get_barrier_semaphore()
        for peer in (self.x, self.y, self.c, self.up, self.down):
            pl.semaphore_signal(barrier, inc=1, device_id=peer, device_id_type=MESH)

    def ready(self):
        pl.semaphore_wait(pltpu.get_barrier_semaphore(), 5)

    def greet(self):
        self.hello()
        self.ready()

    def start(self, source, target, peer, when=None, got=None, index=None):
        i = index
        if index is None:
            i = self.count
            self.count += 1
        copy = pltpu.make_async_remote_copy(
            src_ref=source,
            dst_ref=target,
            send_sem=self.send.at[i],
            recv_sem=self.recv.at[i],
            device_id=peer,
            device_id_type=MESH,
        )
        only(when, copy.start)
        made = Copy(copy, when, got, i)
        self.copies.append(made)
        return made

    def local(self, source, target):
        copy = pltpu.make_async_copy(source, target, self.here.at[self.local_count])
        self.local_count += 1
        copy.start()
        return copy

    def natural(self, b):
        spots = ((self.at_y, b // 4), (self.at_x, b // 2 % 2), (self.at_c, b % 2))
        place = 0
        for at, bit in spots:
            place = 2 * place + at + bit - 2 * at * bit
        return place

    def finish(self):
        for copy in self.copies:
            copy.wait_send()


def drain(*parts):
    parts = list(parts)
    while parts:
        parts = [part for part in parts if next(part, None) is not None]


def run(part):
    next(part, None)


def exchange_halves(wires, sources, slot, bounce=None):
    n = slot.shape[0] // 2
    rows = pl.ds(pl.multiple_of(wires.at_y * n, n), n)
    arrivals, copies = [], []
    for pick, lo, hi in sources:
        arrivals.append(wires.start(pick(1 - wires.at_y), slot.at[rows, lo:hi], wires.y))
        to = slot.at[rows, lo:hi] if bounce is None else bounce.at[:, lo:hi]
        copies.append(wires.local(pick(wires.at_y), to))
    yield 1
    for copy in copies:
        copy.wait()
    if bounce is not None:
        wires.local(bounce, slot.at[rows]).wait()
    for arrival in arrivals:
        arrival.wait_recv()


def along_z(wires, first, slot):
    nz, z = wires.nz, wires.at_z
    get = lambda s: first if s == 0 else slot(s)
    for s in range(1, nz):
        up = wires.start(get(s - 1), slot(s), wires.up, (z >= s - 1) & (z < nz - 1), z >= s)
        down = wires.start(
            get((nz - s + 1) % nz), slot(nz - s), wires.down, (z + s <= nz) & (z >= 1), z + s < nz
        )
        yield 1
        up.wait_recv()
        down.wait_recv()


EARLY = True


def add_into(target, source):
    step = 32 if target.shape[0] % 32 == 0 else 16

    @pl.loop(0, target.shape[0] // step)
    def _(t):
        part = pl.ds(pl.multiple_of(t * step, step), step)
        target[part, :] = (target[part, :].astype(F32) + source[part, :].astype(F32)).astype(BF16)


def sum_along_z(wires, p, above, below, stage, total, early=EARLY):
    nz, z = wires.nz, wires.at_z
    ups, downs = {}, {}

    def ends(s):
        ups[s] = wires.start(p(s), above.at[s - 1], wires.up, z == 0, (z >= 1) & (z <= s))
        downs[s] = wires.start(
            p(nz - s), below.at[s - 1], wires.down, z == nz - 1, (z + s >= nz - 1) & (z < nz - 1)
        )

    for s in range(1, nz if early else 2):
        ends(s)
    for s in range(2, nz):
        loads = [wires.local(p(s), stage.at[0]), wires.local(p(nz - s), stage.at[1])]
        yield 1
        ups[s - 1].wait_recv()
        downs[s - 1].wait_recv()
        for load in loads:
            load.wait()
        if not early:
            ends(s)
        rising = (z >= 1) & (z < s) & (z < nz - 1)
        falling = (z + s >= nz) & (z < nz - 1) & (z >= 1)
        only(rising, lambda s=s: add_into(above.at[s - 2], stage.at[0]))
        wires.start(above.at[s - 2], above.at[s - 1], wires.up, rising, None, ups[s].index)
        only(falling, lambda s=s: add_into(below.at[s - 2], stage.at[1]))
        wires.start(below.at[s - 2], below.at[s - 1], wires.down, falling, None, downs[s].index)
    load = wires.local(p(0), stage.at[0])
    yield 1
    ups[nz - 1].wait_recv()
    downs[nz - 1].wait_recv()
    load.wait()
    only(z >= 1, lambda: add_into(stage.at[0], above.at[nz - 2]))
    only(z < nz - 1, lambda: add_into(stage.at[0], below.at[nz - 2]))
    if total is not None:
        kept = wires.local(stage.at[0], total)
        yield 1
        kept.wait()


def swap_rows(wires, total, got):
    n = got.shape[0]
    other = pl.ds(pl.multiple_of((1 - wires.at_y) * n, n), n)
    sent = wires.start(total.at[other], got, wires.y)
    yield 1
    sent.wait_recv()


def sum_scratch(nz, rows, cols):
    return [
        pltpu.VMEM((nz - 1, rows, cols), BF16),
        pltpu.VMEM((nz - 1, rows, cols), BF16),
        pltpu.VMEM((2, rows, cols), BF16),
    ]


def swap_outputs(*totals):
    return [jax.ShapeDtypeStruct((t.shape[0] // 2, t.shape[1]), BF16) for t in totals]


def columns(ref, rows, lo, hi):
    return lambda s: ref.at[pl.ds(s * rows, rows), lo:hi]


def gather_weight_rows(wires, sources, out, bounce=None):
    n = out.shape[0] // wires.nz
    slot = lambda s: out.at[pl.ds(s * n, n)]
    yield from exchange_halves(wires, sources, slot(0), bounce)
    yield from along_z(wires, slot(0), slot)


def gather_pack_rows(wires, pack, out):
    n = out.shape[0] // (2 * wires.nz)
    y = wires.at_y

    def slot(s, side):
        return out.at[pl.ds(pl.multiple_of((2 * s + side) * n, n), n)]

    mine = pack.at[y]
    arrival = wires.start(pack.at[1 - y], slot(0, y), wires.y)
    kept = wires.local(mine, slot(0, y))
    own = along_z(wires, mine, lambda s: slot(s, y))
    run(own)
    yield 1
    arrival.wait_recv()
    other = along_z(wires, slot(0, 1 - y), lambda s: slot(s, 1 - y))
    run(other)
    yield 1
    for _ in range(1, wires.nz):
        run(own)
        yield 1
        run(other)
        yield 1
    kept.wait()


def gather_phase(wires, block, out, parts):
    views = [(pl.ds(lo, hi - lo), link) for lo, hi, link in parts]
    on_y = [v for v in views if v[1] == "x"] + [v for v in views if v[1] == "y"]
    on_x = on_y[::-1]
    mine = wires.local(block, out.at[0])
    from_y, from_x, diagonal = {}, {}, []
    c = [wires.start(block, out.at[1], wires.c)]
    for k, (rows, _) in enumerate(on_x):
        from_x[k] = wires.start(block.at[rows], out.at[2, rows], wires.x)
    yield 1
    for k, (rows, _) in enumerate(on_y):
        from_y[k] = wires.start(block.at[rows], out.at[4, rows], wires.y)
    yield 1
    for k in range(len(views)):
        for place, arrived, (rows, link), via, own in (
            (4, from_y[k], on_y[k], wires.x, "x"), (2, from_x[k], on_x[k], wires.y, "y"),
        ):
            arrived.wait_recv()
            if link == own:
                relay = wires.start(out.at[place, rows], out.at[6, rows], via)
                diagonal.append((relay, rows))
            c.append(wires.start(out.at[place, rows], out.at[place + 1, rows], wires.c))
        yield 1
    for relay, rows in diagonal:
        relay.wait_recv()
        c.append(wires.start(out.at[6, rows], out.at[7, rows], wires.c))
        yield 1
    for copy in c:
        copy.wait_recv()
    mine.wait()


def halved(n, cut=None):
    cut = n // 2 if cut is None else cut
    return [(0, cut, "x"), (cut, n, "y")]


def feed_sources(gate, up, down, cut, hidden):
    a, b = cut
    n = b - a
    step = LANES

    def pick(ref):
        return lambda y: ref.at[:, pl.ds(pl.multiple_of(y * hidden + a, step), n)]

    return [(pick(ref), k * n, (k + 1) * n) for k, ref in enumerate((gate, up, down))]


def forward_kernel(
    hidden, cuts,
    x_ref, dout_ref, gain_in, qw_ref, kw_ref, vw_ref, ow_ref, ids_ref, rope_ref, spread_ref,
    squeeze_ref, gate_ref, up_ref, down_ref,
    x_own, dout_own, cos_ref, sin_ref, first_ref, q_ref, k_ref, v_ref, o_ref, lse_ref, gain_ref,
    res_ref, inv_ref, a1_ref, dout_all, w_attn, w_out, w_zero, w_one, w_two, w_three, a2_ref,
    pack, opack, x_all, w_flat, w_pad, w_o, o_slots, o_other, bounce_zero, bounce_one, bounce_two,
    bounce_three, block, cr, xr, yr, tr, br, send, recv, local,
):
    wires = Wires(send, recv, local)
    wires.hello()
    nz, z = wires.nz, wires.at_z
    rows, model = x_ref.shape
    length = 8 * rows
    heads = q_ref.shape[1] // LANES
    keys = rows + WINDOW_LENGTH

    turns = rotation(wires, model)
    at = qw_ref.shape[1] // 2
    for h in range(2):
        pack[h, :, 0:at] = qw_ref[:, h * at : (h + 1) * at]
    for ref in (kw_ref, vw_ref):
        n = ref.shape[0] // 2
        eye = identity(n)
        for h in range(2):
            pack[h, :, at : at + n] = tn(ref[h * n : (h + 1) * n, :], eye).astype(BF16)
        at += n
    rest = pack.shape[2] - at
    row = lax.broadcasted_iota(jnp.int32, (2, rest), 0)
    lane = lax.broadcasted_iota(jnp.int32, (2, rest), 1)
    tail = tn(gain_in[...], (row == lane).astype(BF16)).astype(BF16)
    for h in range(2):
        pack[h, :, at:] = tail
    wires.ready()
    weights = gather_pack_rows(wires, pack, w_flat)
    run(weights)
    for to, of in turns:
        x_own[:, to] = x_ref[:, of]
    tokens = gather_phase(wires, x_own, x_all, halved(rows, START_CUT))
    run(tokens)
    run(weights)
    run(tokens)
    run(weights)
    for to, of in turns:
        dout_own[:, to] = dout_ref[:, of]
    n = ow_ref.shape[1] // 2
    for h in range(2):
        opack[h] = ow_ref[:, h * n : (h + 1) * n]
    run(weights)
    run(tokens)
    run(weights)

    lane = lax.broadcasted_iota(jnp.int32, (1, LANES), 1)
    sign = jnp.where(lane < LANES // 2, -1.0, 1.0)
    steps = length // ROPE_STEP
    cos_low, sin_low = rope_ref[0, steps:, :], rope_ref[1, steps:, :]
    for t in range(steps):
        part = slice(t * ROPE_STEP, (t + 1) * ROPE_STEP)
        cos_high, sin_high = rope_ref[0, t : t + 1, :], rope_ref[1, t : t + 1, :]
        cos_ref[part, :] = cos_high * cos_low - sin_high * sin_low
        sin_ref[part, :] = (sin_high * cos_low + cos_high * sin_low) * sign
    offset = pl.multiple_of(z * length, length)
    ids = ids_ref[:, pl.ds(offset, length)]
    begin = jnp.zeros((1, length), jnp.int32)
    for number in range(1, 5):
        count = jnp.sum((ids_ref[...] < number).astype(jnp.int32), axis=1, keepdims=True)
        begin = jnp.where(ids >= number, count, begin)
    window = lax.broadcasted_iota(jnp.int32, (1, length), 1) - (WINDOW_LENGTH - 1)
    first_ref[...] = jnp.maximum(begin - offset, window) + WINDOW_LENGTH

    run(weights)
    run(tokens)
    run(weights)
    def gather_out():
        y, flat = wires.at_y, opack.shape[2]
        arrival = wires.start(opack.at[1 - y], o_other, wires.y)
        yield 1
        arrival.wait_recv()
        o_slots[0, :, 0:flat] = opack[y]
        o_slots[0, :, flat:] = o_other[...]
        yield from along_z(wires, o_slots.at[0], lambda s: o_slots.at[s])
        n = opack.shape[1]
        for s in range(nz):
            for k, side in enumerate((y, 1 - y)):
                part = pl.ds(pl.multiple_of((2 * s + side) * n, n), n)
                w_o[part, :] = o_slots[s, :, k * flat : (k + 1) * flat]

    out_weights = gather_out()
    zero_weights, one_weights = [
        gather_weight_rows(
            wires, feed_sources(gate_ref, up_ref, down_ref, cut, hidden), out, bounce
        )
        for cut, out, bounce in zip(cuts, (w_zero, w_one), (bounce_zero, bounce_one))
    ]
    exchanges = [
        exchange_halves(
            wires, feed_sources(gate_ref, up_ref, down_ref, cut, hidden), slot, bounce
        )
        for cut, slot, bounce in zip(cuts[2:], (w_two, w_three), (bounce_two, bounce_three))
    ]
    run(out_weights)
    run(zero_weights)
    drain(tokens, weights)
    sent = list(wires.copies)
    quarter = rows // 4
    cotangents = gather_phase(
        wires, dout_own, dout_all, [(t * quarter, (t + 1) * quarter, "x") for t in range(4)]
    )
    run(cotangents)
    run(out_weights)
    run(cotangents)
    for copy in sent:
        copy.wait_send()
    saves = [wires.local(w_flat, w_attn)]

    @pl.loop(0, model // 512)
    def _(t):
        part = pl.ds(pl.multiple_of(t * 512, 512), 512)
        w_pad[part, :] = nn(w_flat[part, :], spread_ref[...]).astype(BF16)

    place = lax.broadcasted_iota(jnp.int32, (8, w_flat.shape[1]), 1)
    row = lax.broadcasted_iota(jnp.int32, (8, w_flat.shape[1]), 0)
    which = (place == (heads + 2) * HEAD_SIZE + row).astype(BF16)
    gain_ref[...] = nt(which, w_flat[...])
    gain = gain_ref[0:1, :]

    @pl.when(z == 0)
    def _():
        k_ref[0:WINDOW_LENGTH, :] = jnp.zeros((WINDOW_LENGTH, LANES), BF16)
        v_ref[0:WINDOW_LENGTH, :] = jnp.zeros((WINDOW_LENGTH, LANES), BF16)

    def project(b, at):
        x = x_all[at].astype(F32)
        inverse = lax.rsqrt(jnp.mean(x * x, axis=1, keepdims=True) + EPS)
        a1 = (x * inverse * gain).astype(BF16)
        x_all[at] = a1
        acc = nn(a1, w_pad[...])
        here = pl.ds(pl.multiple_of(b * rows, rows), rows)
        there = pl.ds(pl.multiple_of(WINDOW_LENGTH + b * rows, rows), rows)
        cosine, sine = cos_ref[here, :], sin_ref[here, :]
        for h in range(heads + 1):
            u = acc[:, h * LANES : (h + 1) * LANES]
            turned = (u * cosine + pltpu.roll(u, LANES // 2, 1) * sine).astype(BF16)
            if h < heads:
                q_ref[here, h * LANES : (h + 1) * LANES] = turned
            else:
                k_ref[there, :] = turned
        v_ref[there, :] = acc[:, (heads + 1) * LANES :].astype(BF16)

    def projected(lo, hi):
        @pl.loop(lo, hi)
        def _(b):
            project(b, wires.natural(b))

        for b in range(lo, hi):
            at = wires.natural(b)
            saves.append(wires.local(x_all.at[at], a1_ref.at[at]))

    projected(6, 8)
    halo = [
        wires.start(
            ref.at[pl.ds(length, WINDOW_LENGTH)], ref.at[pl.ds(0, WINDOW_LENGTH)],
            wires.up, z < nz - 1, z > 0,
        )
        for ref in (k_ref, v_ref)
    ]
    run(zero_weights)
    projected(0, 2)
    run(out_weights)
    projected(2, 6)
    run(zero_weights)
    run(cotangents)
    run(cotangents)
    run(one_weights)
    for copy in halo:
        copy.wait_recv()

    def attend(b, at):
        start = pl.multiple_of(b * rows, rows)
        span = pl.ds(start, keys)
        here = pl.ds(start, rows)
        kb = k_ref[span, :]
        vt = v_ref[span, :].T
        bias = mask_bias(first_ref[:, here] - start, keys, rows)
        outs = []
        for h in range(heads):
            lanes = slice(h * LANES, (h + 1) * LANES)
            s = nt(kb, q_ref[here, lanes]) * (SCALE * LOG2E) + bias
            peak = jnp.max(s, axis=0, keepdims=True)
            p = jnp.exp2(s - peak)
            total = jnp.sum(p, axis=0, keepdims=True)
            ot = nn(vt, p.astype(BF16)) / total
            outs.append(ot.T.astype(BF16))
            lse_ref[b, h : h + 1, :] = peak + jnp.log2(total)
        o_ref[at] = nn(jnp.concatenate(outs, 1), squeeze_ref[...]).astype(BF16)

    def attended(lo, hi):
        @pl.loop(lo, hi)
        def _(b):
            attend(b, wires.natural(b))

    attended(0, 2)
    run(out_weights)
    run(cotangents)
    attended(2, 4)
    run(cotangents)
    run(zero_weights)
    for exchange in exchanges:
        run(exchange)
    attended(4, 6)
    drain(out_weights)
    saves.append(wires.local(w_o, w_out))
    run(one_weights)
    attended(6, 8)
    for save in saves:
        save.wait()

    def emit(part, total):
        residual = x_own[part, :].astype(F32) + total
        inverse = lax.rsqrt(jnp.mean(residual * residual, axis=1, keepdims=True) + EPS)
        res_ref[part, :] = residual
        inv_ref[part, :] = inverse
        block[part, :] = (residual * inverse * gain_ref[1:2, :]).astype(BF16)

    sums = reduce_phase(
        wires, o_ref, w_o, x_all.at[pl.ds(0, 4)], cr, x_all.at[pl.ds(4, 4)], xr, yr, tr, br, emit
    )
    for _ in range(4):
        run(sums)
    drain(zero_weights, cotangents)
    run(sums)
    run(one_weights)
    drain(sums)
    normed = gather_phase(wires, block, a2_ref, halved(rows, NORMED_CUT))
    run(normed)
    run(normed)
    run(one_weights)
    run(normed)
    drain(normed, one_weights, *exchanges)
    wires.finish()


START_CUT = 160
NORMED_CUT = 128


def attention_forward(
    inputs, dout, gains, query, key_t, value_t, out_t, ids, rope, gate, up, down_t, width, cuts
):
    n, model = inputs.shape
    rows = query.shape[0]
    length = 8 * n
    heads = query.shape[1] // 2 // HEAD_SIZE
    hidden = gate.shape[1] // 2
    wide = heads * LANES
    flat = heads * HEAD_SIZE
    half = n // 2
    spread = spread_matrix(heads + 1, 1, rows=width)
    squeeze = spread_matrix(0, heads).T
    sizes = [3 * (b - a) for a, b in cuts]
    b16 = lambda *shape: jax.ShapeDtypeStruct(shape, BF16)
    f32 = lambda *shape: jax.ShapeDtypeStruct(shape, F32)
    v16 = lambda *shape: pltpu.VMEM(shape, BF16)
    return pl.pallas_call(
        functools.partial(forward_kernel, hidden, cuts),
        in_specs=[WHOLE] * 11 + [HBM] * 3,
        out_specs=[WHOLE] * 13 + [HBM] * 9,
        out_shape=[
            b16(n, model), b16(n, model), f32(length, LANES), f32(length, LANES),
            jax.ShapeDtypeStruct((1, length), jnp.int32), b16(length, wide),
            b16(length + WINDOW_LENGTH, LANES), b16(length + WINDOW_LENGTH, LANES),
            b16(8, n, flat), f32(8, heads, n), f32(8, model), f32(n, model), f32(n, 1),
            b16(8, n, model), b16(8, n, model), b16(model, width), b16(model, flat),
            b16(model, sizes[0]), b16(model, sizes[1]), b16(2 * rows, sizes[2]),
            b16(2 * rows, sizes[3]), b16(8, n, model),
        ],
        scratch_shapes=[
            v16(2, rows, width), v16(2, rows, flat), v16(8, n, model), v16(model, width),
            v16(model, spread.shape[1]), v16(model, flat),
            v16(model // (2 * rows), rows, 2 * flat), v16(rows, flat),
        ]
        + [v16(rows, size) for size in sizes]
        + [
            v16(n, model), v16(4, n, model), v16(2, half, model), v16(2, half, model),
            v16(half, model), v16(half, model),
        ]
        + semaphores(),
        compiler_params=params(62, collective_id=0, has_side_effects=True),
        name="attention_forward",
        **light(),
    )(
        inputs, dout, gains, query, key_t, value_t, out_t, ids, rope, spread, squeeze, gate, up,
        down_t,
    )


def feed_kernel(
    hidden, cuts, chunks,
    a_ref, d_ref, w0_ref, w1_ref, w2_ref, w3_ref,
    m_ref, g_ref, w_ref, grad0, grad1, grad2, grad3, total,
    a, d, w, m, g, stage, above, below, extra, send, recv, local,
):
    wires = Wires(send, recv, local)
    nz = wires.nz
    length, model = a.shape
    slot = model // nz
    wires.hello()

    def spots(lo, hi):
        out = []
        for k in range(3):
            for first, last in chunks:
                left, right = max(lo, first), min(hi, last)
                if left < right:
                    base = 2 * hidden if k == 2 else first + k * (last - first)
                    start = base + left
                    out.append((k * (hi - lo) + left - lo, start, right - left, k, left))
        return out

    loads = []
    for ref, (lo, hi) in ((w0_ref, cuts[0]), (w1_ref, cuts[1])):
        for of, to, n, _, _ in spots(lo, hi):
            loads.append(wires.local(ref.at[:, of : of + n], w.at[:, to : to + n]))
    rows = length // 8
    a_loads, d_loads = [], []

    def fetch(half):
        part = pl.ds(half * 4 * rows, 4 * rows)
        a_loads.append(wires.local(a_ref.at[part], a.at[part]))
        d_loads.append(wires.local(d_ref.at[part], d.at[part]))

    fetch(0)

    def carried(ref, cut):
        pieces, copies = [], []
        for of, to, n, _, _ in spots(*cut):
            pieces.append((to, to + n))
            copies.append(wires.local(ref.at[:, of : of + n], w.at[pl.ds(0, slot), to : to + n]))
        yield 1
        for copy in copies:
            copy.wait()
        hops = [
            along_z(
                wires,
                w.at[pl.ds(0, slot), lo:hi],
                lambda s, lo=lo, hi=hi: w.at[pl.ds(s * slot, slot), lo:hi],
            )
            for lo, hi in pieces
        ]
        while hops:
            hops = [hop for hop in hops if next(hop, None) is not None]
            yield 1

    later = [carried(ref, cut) for ref, cut in zip((w2_ref, w3_ref), cuts[2:])]
    for part in later:
        run(part)
    wires.ready()
    run(later[0])
    for copy in loads:
        copy.wait()

    def units(lo, hi, blocks):
        n = hi - lo

        @pl.loop(*blocks)
        def _(b):
            part = pl.ds(pl.multiple_of(b * rows, rows), rows)
            both = nn(a[part, :], w[:, 2 * lo : 2 * hi])
            gate, up = both[:, :n], both[:, n:]
            dmixed = nn(d[part, :], w[:, 2 * hidden + lo : 2 * hidden + hi])
            sigma = jax.nn.sigmoid(gate)
            silu = gate * sigma
            m[part, lo:hi] = (silu * up).astype(BF16)
            g[part, lo + hi : 2 * hi] = (dmixed * silu).astype(BF16)
            g[part, 2 * lo : lo + hi] = (
                dmixed * up * sigma * (1.0 + gate * (1.0 - sigma))
            ).astype(BF16)

    tile = stage.shape[1]
    last = model // tile

    def weight_grads(lo, hi, out, tiles=None):
        n = hi - lo
        tiles = (0, last) if tiles is None else tiles

        def save(t):
            return pltpu.make_async_copy(
                stage.at[t % 2, :, 0 : 3 * n],
                out.at[pl.ds(pl.multiple_of(t * tile, tile), tile)],
                local.at[24 + 4 * nz - 1 - t % 2],
            )

        @pl.loop(*tiles)
        def _(t):
            @pl.when(t >= 2)
            def _():
                save(t - 2).wait()

            cols = pl.ds(pl.multiple_of(t * tile, tile), tile)
            stage[t % 2, :, 0 : 2 * n] = tn(a[:, cols], g[:, 2 * lo : 2 * hi]).astype(BF16)
            stage[t % 2, :, 2 * n : 3 * n] = tn(d[:, cols], m[:, lo:hi]).astype(BF16)
            save(t).start()

        if tiles[1] == last:
            save(last - 2).wait()
            save(last - 1).wait()

    a_loads[0].wait()
    d_loads[0].wait()
    fetch(1)
    units(*chunks[0], (0, 4))
    a_loads[1].wait()
    d_loads[1].wait()
    units(*chunks[0], (4, 8))
    weight_grads(*chunks[0], grad0, (0, 2))
    run(later[0])
    weight_grads(*chunks[0], grad0, (2, last))
    sums = sum_along_z(
        wires, columns(grad0, slot, 0, total.shape[1]), above, below, extra, total, False
    )
    run(sums)
    units(*chunks[1], (0, 8))
    run(later[0])
    weight_grads(*chunks[1], grad1, (0, 4))
    run(later[1])
    weight_grads(*chunks[1], grad1, (4, last))
    drain(later[0])
    run(sums)
    units(*chunks[2], (0, 4))
    run(later[1])
    units(*chunks[2], (4, 8))
    weight_grads(*chunks[2], grad2, (0, 2))
    run(later[1])
    run(sums)
    weight_grads(*chunks[2], grad2, (2, last))
    drain(later[1])
    outs = [wires.local(w, w_ref)]
    units(*chunks[3], (0, 8))
    outs += [wires.local(m, m_ref), wires.local(g, g_ref)]
    weight_grads(*chunks[3], grad3)
    drain(sums)
    for copy in outs:
        copy.wait()
    wires.finish()


def feed_forward(a2, dout, w0, w1, w2, w3, cuts, chunks):
    length, model = a2.shape
    hidden = cuts[-1][1]
    sizes = [b - a for a, b in chunks]
    rows = w3.shape[0]
    nz = model // rows
    return pl.pallas_call(
        functools.partial(feed_kernel, hidden, cuts, chunks),
        in_specs=[HBM] * 6,
        out_specs=[HBM] * 8,
        out_shape=[
            jax.ShapeDtypeStruct((length, hidden), BF16),
            jax.ShapeDtypeStruct((length, 2 * hidden), BF16),
            jax.ShapeDtypeStruct((model, 3 * hidden), BF16),
        ]
        + [jax.ShapeDtypeStruct((model, 3 * n), BF16) for n in sizes]
        + [jax.ShapeDtypeStruct((rows, 3 * sizes[0]), BF16)],
        scratch_shapes=[
            pltpu.VMEM((length, model), BF16),
            pltpu.VMEM((length, model), BF16),
            pltpu.VMEM((model, 3 * hidden), BF16),
            pltpu.VMEM((length, hidden), BF16),
            pltpu.VMEM((length, 2 * hidden), BF16),
            pltpu.VMEM((2, 512, 3 * max(sizes)), BF16),
        ]
        + sum_scratch(nz, rows, 3 * sizes[0])
        + semaphores(),
        compiler_params=params(62, collective_id=1, has_side_effects=True),
        name="feed_forward",
        **light(),
    )(a2, dout, w0, w1, w2, w3)


def reduce_phase(wires, a, w, cs, cr, q, xr, yr, tr, br, emit, ready=None):
    n = q.shape[1]
    half = n // 2
    top, bottom = pl.ds(0, half), pl.ds(half, half)
    model = q.shape[2]
    tile = 512
    deep = a.shape[2]

    def product(place, target):
        if ready is not None:
            ready(place)

        @pl.loop(0, model // tile)
        def _(t):
            cols = pl.ds(pl.multiple_of(t * tile, tile), tile)
            target[:, cols] = nt(a[place], w[cols, 0:deep]).astype(BF16)

    waits = {}
    for j in (3, 1, 2, 0):
        product(2 * j + 1, cs.at[j])
        got = wires.start(cs.at[j], cr.at[j], wires.c)
        product(2 * j, q.at[j])
        got.wait_recv()
        q[j] = (q[j].astype(F32) + cr[j].astype(F32)).astype(BF16)
        if j == 3:
            waits["x1"] = wires.start(q.at[3, top], xr.at[1], wires.x)
            waits["y1"] = wires.start(q.at[3, bottom], yr.at[1], wires.y)
        if j == 1:
            waits["x0"] = wires.start(q.at[1, top], xr.at[0], wires.x)
        if j == 2:
            waits["y0"] = wires.start(q.at[2, bottom], yr.at[0], wires.y)
        yield 1
    waits["x1"].wait_recv()
    q[2, top] = (q[2, top].astype(F32) + xr[1].astype(F32)).astype(BF16)
    waits["t"] = wires.start(q.at[2, top], tr, wires.y)
    waits["y1"].wait_recv()
    q[1, bottom] = (q[1, bottom].astype(F32) + yr[1].astype(F32)).astype(BF16)
    waits["b"] = wires.start(q.at[1, bottom], br, wires.x)
    yield 1
    waits["x0"].wait_recv()
    yield 1
    waits["t"].wait_recv()
    emit(top, q[0, top].astype(F32) + xr[0].astype(F32) + tr[...].astype(F32))
    waits["y0"].wait_recv()
    waits["b"].wait_recv()
    emit(bottom, q[0, bottom].astype(F32) + yr[0].astype(F32) + br[...].astype(F32))


def reduce_scratch(n, model):
    half = n // 2
    return [
        pltpu.VMEM((4, n, model), BF16),
        pltpu.VMEM((4, n, model), BF16),
        pltpu.VMEM((4, n, model), BF16),
        pltpu.VMEM((2, half, model), BF16),
        pltpu.VMEM((2, half, model), BF16),
        pltpu.VMEM((half, model), BF16),
        pltpu.VMEM((half, model), BF16),
    ]


def middle_kernel(
    a_ref, w_ref, dout_ref, res_ref, inv_ref, gain_ref, grad0, grad2,
    dres_ref, out_ref, total0, total2,
    a, w, block, cs, cr, q, xr, yr, tr, br,
    above0, below0, stage0, above2, below2, stage2, send, recv, local,
):
    wires = Wires(send, recv, local)
    wires.hello()
    load_w = wires.local(w_ref.at[:, 0 : w.shape[1]], w)
    loads = {place: wires.local(a_ref.at[place], a.at[place]) for place in (7, 6)}
    wires.ready()
    rows = total0.shape[0]
    first = sum_along_z(
        wires, columns(grad0, rows, 0, total0.shape[1]), above0, below0, stage0, total0
    )
    second = sum_along_z(
        wires, columns(grad2, rows, 0, total2.shape[1]), above2, below2, stage2, total2, False
    )
    run(first)

    def emit(rows, total):
        inverse = inv_ref[rows, :]
        normed = res_ref[rows, :] * inverse
        e = total * gain_ref[1:2, :]
        back = inverse * (e - normed * jnp.mean(e * normed, axis=1, keepdims=True))
        dres = dout_ref[rows, :].astype(F32) + back
        dres_ref[rows, :] = dres
        block[rows, :] = dres.astype(BF16)

    load_w.wait()
    for place in (3, 2, 5, 4, 1, 0):
        loads[place] = wires.local(a_ref.at[place], a.at[place])
    sums = reduce_phase(
        wires, a, w, cs, cr, q, xr, yr, tr, br, emit, lambda place: loads[place].wait()
    )
    for _ in range(4):
        run(sums)
    run(first)
    run(sums)
    run(sums)
    run(first)
    run(second)
    drain(sums)
    tokens = gather_phase(wires, block, out_ref, halved(block.shape[0]))
    run(tokens)
    run(tokens)
    run(first)
    run(second)
    run(tokens)
    run(second)
    run(tokens)
    drain(second, tokens, first)
    wires.finish()


def feed_back(dgu, w, dout, residual, inverse, gain, grad0, grad2):
    n, model = dout.shape
    k = dgu.shape[1]
    rows = 2 * model // lax.axis_size("tok")
    nz = model // rows
    half, small = grad0.shape[1], grad2.shape[1]
    return pl.pallas_call(
        middle_kernel,
        in_specs=[HBM] * 2 + [WHOLE] * 4 + [HBM] * 2,
        out_specs=[WHOLE] + [HBM] * 3,
        out_shape=[
            jax.ShapeDtypeStruct((n, model), F32),
            jax.ShapeDtypeStruct((8, n, model), BF16),
            jax.ShapeDtypeStruct((rows, half), BF16),
            jax.ShapeDtypeStruct((rows, small), BF16),
        ],
        scratch_shapes=[
            pltpu.VMEM((8, n, k), BF16),
            pltpu.VMEM((model, k), BF16),
            pltpu.VMEM((n, model), BF16),
        ]
        + reduce_scratch(n, model)
        + sum_scratch(nz, rows, half)
        + sum_scratch(nz, rows, small)
        + semaphores(),
        compiler_params=params(62, collective_id=3, has_side_effects=True),
        name="feed_back",
        **light(),
    )(dgu.reshape(8, n, k), w, dout, residual, inverse, gain, grad0, grad2)


def back_kernel(
    da_ref, w_ref, o_ref, q_ref, k_ref, v_ref, lse_ref, first_ref, cos_ref, sin_ref,
    spread_ref, squeeze_ref, final_ref, m_ref, down_ref, res_ref, grad1, sum0, sum1, sum2,
    dqkv_ref, out_ref, grad_out, total, got0, got1, got2,
    da, do, dk, dv, halo, fetched, m, w_down, cr, xr, yr, tr, br,
    above, below, stage, stage1, res, send, recv, local,
):
    wires = Wires(send, recv, local)
    nz, z = wires.nz, wires.at_z
    wires.hello()
    n, model = da.shape[1], da.shape[2]
    heads = q_ref.shape[1] // LANES
    wide = heads * HEAD_SIZE
    keys = n + WINDOW_LENGTH
    length = 8 * n
    loads = [wires.local(da_ref.at[b], da.at[b]) for b in range(8)]
    late = [
        wires.local(m_ref, m),
        wires.local(down_ref.at[:, 2 * m.shape[2] :], w_down),
    ]
    rows = total.shape[0]
    wires.ready()
    carried = sum_along_z(
        wires, columns(grad1, rows, 0, total.shape[1]), above, below, stage, total
    )
    run(carried)
    swaps = [
        swap_rows(wires, s, got) for s, got in ((sum0, got0), (sum1, got1), (sum2, got2))
    ]
    for swap in swaps:
        run(swap)
    dk[...] = jnp.zeros_like(dk)
    dv[...] = jnp.zeros_like(dv)
    for b in range(8):
        loads[b].wait()
        flat = nn(da[b], w_ref[...]).astype(BF16)
        do[b] = nn(flat, spread_ref[...]).astype(BF16)

    saves = []
    for t in range(nz):
        cols = slice(t * rows, (t + 1) * rows)
        if t >= 2:
            saves[t - 2].wait()
        total = None
        for b in range(8):
            part = tn(da[b, :, cols], o_ref[b])
            total = part if total is None else total + part
        half = rows // 2
        for h in range(2):
            part = total[h * half : (h + 1) * half].astype(BF16)
            stage1[t % 2, :, h * wide : (h + 1) * wide] = part
        saves.append(wires.local(stage1.at[t % 2], grad_out.at[pl.ds(t * half, half)]))
    for save in saves[-2:]:
        save.wait()
    for load in late:
        load.wait()
    turns = rotation(wires, model)

    def emit(part, total):
        load = wires.local(res_ref.at[part], res)
        load.wait()
        layer = (res[...] + total).astype(BF16)
        for of, to in turns:
            out_ref[part, to] = layer[:, of]

    sums = reduce_phase(
        wires, m, w_down, da.at[pl.ds(0, 4)], cr, da.at[pl.ds(4, 4)], xr, yr, tr, br, emit
    )
    run(sums)
    run(sums)
    run(carried)
    run(sums)
    run(sums)

    def block(b, at):
        start = pl.multiple_of(b * n, n)
        span = pl.ds(start, keys)
        here = pl.ds(start, n)
        kb = k_ref[span, :]
        vb = v_ref[span, :]
        kt = kb.T
        bias = mask_bias(first_ref[:, here] - start, keys, n)
        cosine, sine = cos_ref[here, :], sin_ref[here, :]
        dqs = []
        dk_sum = dv_sum = None
        for h in range(heads):
            lanes = slice(h * LANES, (h + 1) * LANES)
            qh = q_ref[here, lanes]
            doh = do[at, :, lanes]
            p = jnp.exp2(nt(kb, qh) * (SCALE * LOG2E) + (bias - lse_ref[b, h : h + 1, :]))
            t = p * nt(vb, doh)
            inner = jnp.sum(t, axis=0, keepdims=True)
            ds = (t - p * inner).astype(BF16)
            dq = nn(kt, ds).T * SCALE
            dqs.append((dq * cosine - pltpu.roll(dq, LANES // 2, 1) * sine).astype(BF16))
            dk_h = nn(ds, qh)
            dv_h = nn(p.astype(BF16), doh)
            dk_sum = dk_h if dk_sum is None else dk_sum + dk_h
            dv_sum = dv_h if dv_sum is None else dv_sum + dv_h
        dqkv_ref[at, :, 0:wide] = nn(jnp.concatenate(dqs, 1), squeeze_ref[...]).astype(BF16)
        dk[span, :] += dk_sum
        dv[span, :] += dv_sum

    def blocks(lo, hi):
        @pl.loop(lo, hi)
        def _(b):
            block(b, wires.natural(b))

    blocks(0, 2)
    halo[:, 0:LANES] = dk[0:WINDOW_LENGTH, :].astype(BF16)
    halo[:, LANES:] = dv[0:WINDOW_LENGTH, :].astype(BF16)
    borrowed = wires.start(halo, fetched, wires.down, z >= 1, z < nz - 1)
    run(sums)
    blocks(2, 4)
    run(carried)
    blocks(4, 8)
    drain(sums)
    borrowed.wait_recv()

    @pl.when(z < nz - 1)
    def _():
        dk[length:, :] += fetched[:, 0:LANES].astype(F32)
        dv[length:, :] += fetched[:, LANES:].astype(F32)

    for b in range(8):
        here = slice(b * n, (b + 1) * n)
        there = slice(WINDOW_LENGTH + b * n, WINDOW_LENGTH + (b + 1) * n)
        dkb = dk[there, :] * SCALE
        dkb = dkb * cos_ref[here, :] - pltpu.roll(dkb, LANES // 2, 1) * sin_ref[here, :]
        both = jnp.concatenate([dkb.astype(BF16), dv[there, :].astype(BF16)], 1)
        dqkv_ref[wires.natural(b), :, wide:] = nn(both, final_ref[...]).astype(BF16)
    drain(carried, *swaps)
    wires.finish()


def attention_back(
    da_all, w_out, o, q, k_all, v_all, lse, first_key, cosine, sine, mixed, w_feed, residual, grad1,
    sums, width,
):
    _, n, model = da_all.shape
    length = 8 * n
    heads = q.shape[1] // LANES
    wide = heads * HEAD_SIZE
    spread = spread_matrix(0, heads)
    squeeze = spread_matrix(heads, 0).T
    final = spread_matrix(1, 1, rows=width - wide).T
    rows = 2 * model // lax.axis_size("tok")
    nz = model // rows
    hidden = mixed.shape[1]
    half = n // 2
    return pl.pallas_call(
        back_kernel,
        in_specs=[HBM] + [WHOLE] * 12 + [HBM] * 7,
        out_specs=[WHOLE, WHOLE] + [HBM] * 5,
        out_shape=[
            jax.ShapeDtypeStruct((8, n, width), BF16),
            jax.ShapeDtypeStruct((n, model), BF16),
            jax.ShapeDtypeStruct((model // 2, 2 * wide), BF16),
            jax.ShapeDtypeStruct((rows, grad1.shape[1]), BF16),
        ]
        + swap_outputs(*sums),
        scratch_shapes=[
            pltpu.VMEM((8, n, model), BF16),
            pltpu.VMEM((8, n, heads * LANES), BF16),
            pltpu.VMEM(k_all.shape, F32),
            pltpu.VMEM(k_all.shape, F32),
            pltpu.VMEM((WINDOW_LENGTH, 2 * LANES), BF16),
            pltpu.VMEM((WINDOW_LENGTH, 2 * LANES), BF16),
            pltpu.VMEM((8, n, hidden), BF16),
            pltpu.VMEM((model, hidden), BF16),
            pltpu.VMEM((4, n, model), BF16),
            pltpu.VMEM((2, half, model), BF16),
            pltpu.VMEM((2, half, model), BF16),
            pltpu.VMEM((half, model), BF16),
            pltpu.VMEM((half, model), BF16),
        ]
        + sum_scratch(nz, rows, grad1.shape[1])
        + [pltpu.VMEM((2, rows // 2, 2 * wide), BF16), pltpu.VMEM((half, model), F32)]
        + semaphores(),
        compiler_params=params(63, collective_id=6, has_side_effects=True),
        name="attention_back",
        **light(),
    )(
        da_all, w_out, o, q, k_all, v_all, lse, first_key, cosine, sine, spread, squeeze, final,
        mixed.reshape(8, n, hidden), w_feed, residual, grad1, *sums,
    )


def last_kernel(
    a_ref, w_ref, x_ref, gain_ref, dres_ref, a1_ref, grad_out, sum0,
    out_ref, total, total1, got0, got, got1,
    cs, cr, q, xr, yr, tr, br, a1, grad, above, below, stage, above1, below1, stage1, o_rows,
    send, recv, local,
):
    wires = Wires(send, recv, local)
    wires.hello()
    rows = total.shape[0]
    model = a1.shape[2]
    loads = [wires.local(a1_ref.at[b], a1.at[b]) for b in range(8)]
    turns = rotation(wires, model)

    def emit(rows, total):
        x = x_ref[rows, :].astype(F32)
        inverse = lax.rsqrt(jnp.mean(x * x, axis=1, keepdims=True) + EPS)
        normed = x * inverse
        e = total * gain_ref[0:1, :]
        back = inverse * (e - normed * jnp.mean(e * normed, axis=1, keepdims=True))
        done = dres_ref[rows, :] + back
        for of, to in turns:
            out_ref[rows, to] = done[:, of]

    wires.ready()
    first = sum_along_z(
        wires, columns(grad_out, rows // 2, 0, grad_out.shape[1]), above1, below1, stage1, None
    )
    run(first)
    swap = swap_rows(wires, sum0, got0)
    run(swap)
    for load in loads:
        load.wait()
    tile = 640

    def weight_grads(lo, hi):
        @pl.loop(lo, hi)
        def _(t):
            cols = pl.ds(pl.multiple_of(t * tile, tile), tile)
            total = None
            for b in range(8):
                part = tn(a1[b, :, cols], a_ref[b])
                total = part if total is None else total + part
            grad[cols, :] = total.astype(BF16)

    weight_grads(0, 2)
    run(first)
    weight_grads(2, 4)
    carried = sum_along_z(
        wires, columns(grad, rows, 0, total.shape[1]), above, below, stage, total
    )
    run(carried)
    sums = reduce_phase(wires, a_ref, w_ref, cs, cr, q, xr, yr, tr, br, emit)
    run(sums)
    run(sums)
    run(first)
    run(sums)
    run(sums)
    run(sums)
    run(carried)
    run(first)
    run(sums)
    run(carried)
    drain(sums)
    drain(first)
    half, wide = o_rows.shape[1:]
    for h in range(2):
        o_rows[h] = stage1[0, :, h * wide : (h + 1) * wide]
    keep = wires.local(o_rows.at[0], total1.at[0:half]), wires.local(o_rows.at[1], total1.at[half:])
    sent = wires.start(o_rows.at[1 - wires.at_y], got1, wires.y)
    drain(carried)
    drain(swap_rows(wires, total, got), swap)
    sent.wait_recv()
    for copy in keep:
        copy.wait()
    wires.finish()


def input_back(dqkv, w, inputs, gain, dres, a1, grad_out, total):
    n, model = inputs.shape
    rows = 2 * model // lax.axis_size("tok")
    nz = model // rows
    wide = dqkv.shape[2]
    return pl.pallas_call(
        last_kernel,
        in_specs=[WHOLE] * 5 + [HBM] * 3,
        out_specs=[WHOLE] + [HBM] * 5,
        out_shape=[
            jax.ShapeDtypeStruct((n, model), F32),
            jax.ShapeDtypeStruct((rows, wide), BF16),
            jax.ShapeDtypeStruct((rows, grad_out.shape[1] // 2), BF16),
            jax.ShapeDtypeStruct((rows // 2, total.shape[1]), BF16),
            jax.ShapeDtypeStruct((rows // 2, wide), BF16),
            jax.ShapeDtypeStruct((rows // 2, grad_out.shape[1] // 2), BF16),
        ],
        scratch_shapes=reduce_scratch(n, model)
        + [pltpu.VMEM((8, n, model), BF16), pltpu.VMEM((model, wide), BF16)]
        + sum_scratch(nz, rows, wide)
        + sum_scratch(nz, rows // 2, grad_out.shape[1])
        + [pltpu.VMEM((2, rows // 2, grad_out.shape[1] // 2), BF16)]
        + semaphores(),
        compiler_params=params(62, collective_id=4, has_side_effects=True),
        name="input_back",
        **light(),
    )(dqkv, w, inputs, gain, dres, a1, grad_out, total)


def finish_kernel(
    chunks, y_ref, *refs,
):
    count = len(chunks) + 2
    mine, got = refs[0 : 2 * count : 2], refs[1 : 2 * count : 2]
    qw, kw, vw, gw, uw, layer, dinput = refs[2 * count : 2 * count + 7]
    gate, up, down, out, query, key, value, sums, row_sums, layer_out, dinput_out, local = refs[
        2 * count + 7 :
    ]
    copies = [
        pltpu.make_async_copy(layer, layer_out, local.at[0]),
        pltpu.make_async_copy(dinput, dinput_out, local.at[1]),
    ]
    for copy in copies:
        copy.start()
    rows = gate.shape[0]
    hidden = gate.shape[1] // 2
    eye = identity(rows)
    wide = lambda v: v.astype(F32)

    def place(h, pieces):
        for (lo, hi), piece in zip(chunks, pieces):
            n = hi - lo
            at = slice(h * hidden + lo, h * hidden + hi)
            for k, ref in enumerate((gate, up, down)):
                ref[:, at] = wide(piece[:, k * n : (k + 1) * n])
        o, q = pieces[-2:]
        for ref, piece in ((out, o), (query, q)):
            n = ref.shape[1] // 2
            ref[:, h * n : (h + 1) * n] = wide(piece[:, 0:n])
        start = query.shape[1] // 2
        for ref in (key, value):
            n = ref.shape[0] // 2
            ref[h * n : (h + 1) * n, :] = tn(q[:, start : start + n], eye)
            start += n

    @pl.when(y_ref[0] == 0)
    def _():
        place(0, [ref.at[0:rows] for ref in mine])
        place(1, got)

    @pl.when(y_ref[0] == 1)
    def _():
        place(0, got)
        place(1, [ref.at[rows:] for ref in mine])

    def total(w, g, axis):
        return jnp.sum(w[...].astype(F32) * g[...], axis=axis, keepdims=True)

    sums[:, 0:1] = total(qw, query, 1)
    sums[:, 1:2] = total(gw, gate, 1) + total(uw, up, 1)
    row_sums[...] = total(kw, key, 0) + total(vw, value, 0)
    for copy in copies:
        copy.wait()


def finish(y, pieces, weights, out_columns, chunks, layer, dinput):
    query, key_t, _, gate, _ = weights
    rows, hidden = gate.shape
    f32 = lambda *shape: jax.ShapeDtypeStruct(shape, F32)
    return pl.pallas_call(
        functools.partial(finish_kernel, chunks),
        in_specs=[pl.BlockSpec(memory_space=pltpu.SMEM)]
        + [WHOLE] * (len(pieces) + len(weights) + 2),
        out_specs=[WHOLE] * 9 + [HBM] * 2,
        out_shape=[
            f32(rows, hidden), f32(rows, hidden), f32(rows, hidden), f32(rows, out_columns),
            f32(*query.shape), f32(*key_t.shape), f32(*key_t.shape), f32(rows, 2), f32(1, rows),
            jax.ShapeDtypeStruct(layer.shape, layer.dtype),
            jax.ShapeDtypeStruct(dinput.shape, dinput.dtype),
        ],
        scratch_shapes=[pltpu.SemaphoreType.DMA((2,))],
        compiler_params=params(62),
        name="finish",
        **light(),
    )(y, *pieces, *weights, layer, dinput)


def body(
    inputs,
    grad_output,
    segments,
    attention_gain,
    query_weight,
    key_matrix,
    value_matrix,
    output_weight,
    feedforward_gain,
    gate_weight,
    up_weight,
    down_weight,
):
    grid = Grid()
    bf16 = jnp.bfloat16
    model = inputs.shape[1]
    length = inputs.shape[0] * 8
    hidden = gate_weight.shape[1] // 2
    qdim = query_weight.shape[1] // 2
    kdim = key_matrix.shape[1] // 2
    cuts = []
    at = 0
    for n in FF_CHUNKS:
        cuts.append((at, at + n))
        at += n
    heads = qdim // HEAD_SIZE

    width = -(-(qdim + 2 * kdim + 2) // LANES) * LANES

    (
        own, dout, cosine, sine, first_key, q, k_all, v_all, o, lse, gains, residual, inverse_two,
        a1, dout_all, w_attn, w_out, w_zero, w_one, w_two, w_three, a2,
    ) = attention_forward(
        outside_rotation(grid, inputs), outside_rotation(grid, grad_output),
        jnp.stack([attention_gain, feedforward_gain]),
        query_weight, key_matrix.T, value_matrix.T, output_weight.T,
        segments[None, :], rope_parts(length, grid.z * length, HEAD_SIZE),
        gate_weight, up_weight, down_weight.T, width, cuts,
    )
    flat = lambda v: v.reshape(length, v.shape[-1])

    chunks = []
    at = 0
    for n in FF_PARTS:
        chunks.append((at, at + n))
        at += n
    mixed, dgu, w_feed, grad0, grad1, grad2, grad3, sum_0 = feed_forward(
        flat(a2), flat(dout_all), w_zero, w_one, w_two, w_three, cuts, chunks
    )
    dresidual, da_all, sum_1, sum_3 = feed_back(
        dgu, w_feed, dout, residual, inverse_two, gains, grad1, grad3
    )
    dqkv, layer, grad_o, sum_2, got_0, got_1, got_3 = attention_back(
        da_all, w_out, o, q, k_all, v_all, lse, first_key, cosine, sine, mixed, w_feed, residual,
        grad2, (sum_0, sum_1, sum_3), width,
    )
    dinput, sum_q, sum_o, got_2, got_q, got_o = input_back(
        dqkv, w_attn, own, gains, dresidual, a1, grad_o, sum_2
    )
    pieces = (
        sum_0, got_0, sum_1, got_1, sum_2, got_2, sum_3, got_3, sum_o, got_o, sum_q, got_q
    )
    (
        gate_grad, up_grad, down_grad, output_grad, query_grad, key_grad, value_grad, sums,
        row_sums, layer, dinput,
    ) = finish(
        jnp.reshape(grid.y, (1,)).astype(jnp.int32),
        pieces,
        (query_weight, key_matrix.T, value_matrix.T, gate_weight, up_weight),
        output_weight.shape[0],
        chunks,
        layer,
        dinput,
    )
    sums = jnp.stack([sums[:, 0] + row_sums[0], sums[:, 1]])
    sums = (sums + grid.swap(sums, C)) + (grid.swap(sums, X) + grid.swap(sums, X | C))
    return (
        outside_rotation(grid, layer),
        outside_rotation(grid, dinput),
        sums[0] / attention_gain.astype(jnp.float32),
        query_grad,
        key_grad.T,
        value_grad.T,
        output_grad.T,
        sums[1] / feedforward_gain.astype(jnp.float32),
        gate_grad,
        up_grad,
        down_grad.T,
    )


def solution(mesh):
    in_specs = (
        P(("tok", "mp"), None),
        P(("tok", "mp"), None),
        P(),
        P("tok"),
        P("tok", "mp"),
        P("tok", "mp"),
        P("tok", "mp"),
        P("mp", "tok"),
        P("tok"),
        P("tok", "mp"),
        P("tok", "mp"),
        P("mp", "tok"),
    )
    out_specs = (
        P(("tok", "mp"), None),
        P(("tok", "mp"), None),
        P("tok"),
        P("tok", "mp"),
        P("tok", "mp"),
        P("tok", "mp"),
        P("mp", "tok"),
        P("tok"),
        P("tok", "mp"),
        P("tok", "mp"),
        P("mp", "tok"),
    )
    return jax.shard_map(body, mesh=mesh, in_specs=in_specs, out_specs=out_specs, check_vma=False)
```
